512 devices in a mesh: slab: 8 (over z), curve: 64 (over y, x, core).
Axes of the slice: x: 4, y: 8, z: 8, core: 2. Of those that a mesh axis runs over, the one named last changes fastest.
Arguments:
- state: float32 [8192, 8, 512], P(('slab', 'curve')), may hold values from -6 to 6
- velocity: bfloat16 [3, 64, 8192], P(None, None, ('slab', 'curve')), may hold values from -4 to 4
- pre_exp: float32 [8192], P(('slab', 'curve')), may hold values from 0.5 to 5
- stoich: float32 [8], replicated, may hold values from -3 to 3
- neighbours: int32 [8192, 6], P(('slab', 'curve')), may hold values from 0 to 8191, as said below
- switch: int32 [8192], P(('slab', 'curve')), may hold values from 0 to 1
- new_owner: int32 [8192], P(('slab', 'curve')), may hold values from 0 to 63, as said below
Outputs:
- state7_out: float32 [6144, 8, 512], P(('slab', 'curve'))
- state3_out: float32 [8192, 512], P(('slab', 'curve'))
The draws below stay inside these ranges and needn't reach their ends.
Inputs may be any that keep to these rules, and one draw needn't show every extreme that they name: Element g lives on device g // 16 of the mesh flattened slab first. The neighbour across face 0 (1) is on the same device or on the previous (next) curve index with wrap, same slab; across faces 2 and 3 on the same device; across face 4 (5) on the same device or the previous (next) slab with wrap, same curve index. The relation is symmetric: the neighbour of neighbours[g, s] across face s xor 1 is g, and face nodes match in the stated order. Each device has exactly 8 faces 0, 8 faces 1, 16 faces 4 and 16 faces 5 whose neighbour lies on another device. `new_owner`: the new owner is in the same slab: the element's own curve index or one next to it with wrap; elements with switch 1 keep their own. From one device at most 2 elements go to each of its two neighbours, and afterwards a device holds at most 12 elements with switch 0; both bounds are reached in every draw.
All inputs are finite; a program needn't handle non-finite values.
Results may differ from the reference program's by a relative error of at most 0.0005.
Values may be sent and summed in bfloat16 or wider, within the bound.
A program may use at most 64 MiB of HBM per device.

```python
import math
import jax
import jax.numpy as jnp
import numpy as np
from jax import lax

P7 = 8
P3 = 4
FIELDS = 8
BX = 2
BY = 8
BZ = 1
NODES7 = 512
NODES3 = 64
E_DEV = 16
MOVE_CAP = 2
HOLD7 = 12
SLABS = 8
PIECES = 64
ELEMENTS = 8192


def mesh_plan(key):
    plan_key = jax.random.fold_in(key, 417)
    local_count = BX * BY * BZ
    devices = SLABS * PIECES
    key_list = jax.random.split(plan_key, 8)
    labels = jax.vmap(lambda sub_key: jax.random.permutation(sub_key, local_count))(jax.random.split(key_list[0], devices)).astype(jnp.int32)
    places = jnp.argsort(labels, axis=1).astype(jnp.int32)
    device_grid = jnp.arange(devices, dtype=jnp.int32)[:, None]
    slab_of = device_grid // PIECES
    curve_of = device_grid % PIECES
    along_x = places // (BY * BZ)
    along_y = places // BZ % BY
    along_z = places % BZ
    flat_labels = labels.reshape(-1)

    def global_id(slab_new, curve_new, x_new, y_new, z_new):
        device_new = slab_new * PIECES + curve_new
        return device_new * local_count + flat_labels[device_new * local_count + x_new * BY * BZ + y_new * BZ + z_new]
    lower_x = along_x > 0
    upper_x = along_x < BX - 1
    lower_z = along_z > 0
    upper_z = along_z < BZ - 1
    sides = [global_id(slab_of, jnp.where(lower_x, curve_of, (curve_of + PIECES - 1) % PIECES), jnp.where(lower_x, along_x - 1, BX - 1), along_y, along_z), global_id(slab_of, jnp.where(upper_x, curve_of, (curve_of + 1) % PIECES), jnp.where(upper_x, along_x + 1, 0), along_y, along_z), global_id(slab_of, curve_of, along_x, (along_y + BY - 1) % BY, along_z), global_id(slab_of, curve_of, along_x, (along_y + 1) % BY, along_z), global_id(jnp.where(lower_z, slab_of, (slab_of + SLABS - 1) % SLABS), curve_of, along_x, along_y, jnp.where(lower_z, along_z - 1, BZ - 1)), global_id(jnp.where(upper_z, slab_of, (slab_of + 1) % SLABS), curve_of, along_x, along_y, jnp.where(upper_z, along_z + 1, 0))]
    neighbours = jnp.stack(sides, axis=-1).reshape(devices * local_count, 6).astype(jnp.int32)
    parity = jax.random.randint(key_list[1], (SLABS, 1), 0, 2)
    donor_mask = (curve_of + parity[slab_of[:, 0]]) % 2 == 0
    forced_pair = jax.random.randint(key_list[2], (SLABS, 1), 0, PIECES // 2)
    forced_curve = 2 * forced_pair + parity
    is_forced = curve_of == forced_curve[slab_of[:, 0]]
    donor_switch = jax.random.randint(key_list[3], (devices, 1), 0, 2 * MOVE_CAP + 1)
    taker_switch = jax.random.randint(key_list[4], (devices, 1), 4 * MOVE_CAP, 6 * MOVE_CAP + 1)
    switched_count = jnp.where(donor_mask, jnp.where(is_forced, 0, donor_switch), taker_switch)
    switch_order = jax.vmap(lambda sub_key: jax.random.permutation(sub_key, local_count))(jax.random.split(key_list[5], devices)).astype(jnp.int32)
    switched = switch_order < switched_count
    shed_count = jnp.where(donor_mask, 2 * MOVE_CAP - switched_count, 0)
    lower_bound = jnp.maximum(shed_count - MOVE_CAP, 0)
    upper_bound = jnp.minimum(shed_count, MOVE_CAP)
    left_count = jax.random.randint(key_list[6], (devices, 1), lower_bound, upper_bound + 1)
    right_count = shed_count - left_count
    mover_order = jax.vmap(lambda sub_key: jax.random.permutation(sub_key, local_count))(jax.random.split(key_list[7], devices)).astype(jnp.int32)
    mover_key = jnp.where(switched, local_count + mover_order, mover_order)
    mover_rank = jnp.argsort(jnp.argsort(mover_key, axis=1), axis=1).astype(jnp.int32)
    to_left = mover_rank < left_count
    to_right = (mover_rank >= left_count) & (mover_rank < left_count + right_count)
    owner_curve = jnp.where(to_left, (curve_of + PIECES - 1) % PIECES, jnp.where(to_right, (curve_of + 1) % PIECES, curve_of))
    return (neighbours, switched.astype(jnp.int32).reshape(-1), owner_curve.astype(jnp.int32).reshape(-1))


def draw_neighbours(key, part):
    return mesh_plan(key)[0]


def draw_switch(key, part):
    return mesh_plan(key)[1]


def draw_new_owner(key, part):
    return mesh_plan(key)[2]


def shard_levels(rng, shape, cuts, low, largest):
    def one(dim, parts):
        heights = jax.random.uniform(jax.random.fold_in(jax.random.fold_in(rng, 6), dim), (parts,), jnp.float32, low / len(cuts), largest / len(cuts))
        return jnp.repeat(jnp.exp(heights), shape[dim] // parts).reshape((-1,) + (1,) * (len(shape) - dim - 1))

    loudness = one(*cuts[0])
    for cut in cuts[1:]:
        loudness = loudness * one(*cut)
    return loudness


def normal_values(stream_key, shape, deviation, limit, cuts=(), held_as=jnp.bfloat16):
    values = deviation * jax.random.normal(stream_key, shape, jnp.float32)
    if cuts:
        values = values * shard_levels(stream_key, shape, cuts, -0.22, 0.18)
    return jnp.clip(values, -limit, limit).astype(held_as)


def setup_inputs(seed: int = 0) -> dict:
    streams_of = jax.random.split(jax.random.key(seed), 8)
    state = normal_values(streams_of[0], (ELEMENTS, FIELDS, NODES7), 1.0, 6.0, ((0, 512),), jnp.float32)
    velocity = normal_values(streams_of[1], (3, NODES3, ELEMENTS), 1.0, 4.0, ((2, 512),))
    pre_exp = jnp.clip(jnp.exp(math.log(5.0) - 2.3025851 * jax.random.uniform(streams_of[2], (ELEMENTS,), jnp.float32) ** shard_levels(streams_of[2], (ELEMENTS,), ((0, 512),), -0.2, 0.2)), 0.5, 5.0)
    stoich = normal_values(streams_of[3], (FIELDS,), 1.0, 3.0, (), jnp.float32)
    neighbours = draw_neighbours(jax.random.fold_in(streams_of[7], 71), 0)
    switch = draw_switch(jax.random.fold_in(streams_of[7], 71), 0)
    new_owner = draw_new_owner(jax.random.fold_in(streams_of[7], 71), 0)
    return {"state": state, "velocity": velocity, "pre_exp": pre_exp, "stoich": stoich, "neighbours": neighbours, "switch": switch, "new_owner": new_owner}


TIME_STEP = 0.002
ACTIVATION = 1.5
SIDE_SIGNS = (-1.0, 1.0, -1.0, 1.0, -1.0, 1.0)
OPPOSITE = (1, 0, 3, 2, 5, 4)


def lobatto_points(number):
    return -np.cos(np.pi * np.arange(number) / (number - 1))


def lagrange_weights(points):
    weights = np.ones(points.shape[0])
    for row_id in range(points.shape[0]):
        for col_id in range(points.shape[0]):
            if col_id != row_id:
                weights[row_id] = weights[row_id] / (points[row_id] - points[col_id])
    return weights


def derivative_matrix(points):
    weights = lagrange_weights(points)
    number = points.shape[0]
    matrix = np.zeros((number, number))
    for row_id in range(number):
        for col_id in range(number):
            if col_id != row_id:
                matrix[row_id, col_id] = weights[col_id] / weights[row_id] / (points[row_id] - points[col_id])
        matrix[row_id, row_id] = -np.sum(matrix[row_id])
    return matrix


def interpolation_matrix(source, target):
    matrix = np.ones((target.shape[0], source.shape[0]))
    for col_id in range(source.shape[0]):
        for other_id in range(source.shape[0]):
            if other_id != col_id:
                matrix[:, col_id] = matrix[:, col_id] * (target - source[other_id]) / (source[col_id] - source[other_id])
    return matrix


def spread_three(matrix, identity):
    return (np.kron(matrix, np.kron(identity, identity)), np.kron(identity, np.kron(matrix, identity)), np.kron(identity, np.kron(identity, matrix)))


def make_tables():
    fine_points = lobatto_points(P7)
    coarse_points = lobatto_points(P3)
    fine_derivs = spread_three(derivative_matrix(fine_points), np.eye(P7))
    coarse_derivs = spread_three(derivative_matrix(coarse_points), np.eye(P3))
    downward = interpolation_matrix(fine_points, coarse_points)
    upward = interpolation_matrix(coarse_points, fine_points)
    fine_stack = jnp.asarray(np.concatenate([matrix.T for matrix in fine_derivs], axis=0), jnp.float32).astype(jnp.bfloat16)
    coarse_stack = jnp.asarray(np.stack(coarse_derivs, axis=0), jnp.float32).astype(jnp.bfloat16)
    lift_table = jnp.asarray(np.kron(upward, np.kron(upward, upward)), jnp.float32).astype(jnp.bfloat16)
    projection = jnp.asarray(np.kron(downward, np.kron(downward, downward)), jnp.float32)
    mortar_up = jnp.asarray(np.kron(upward, upward), jnp.float32)
    mortar_down = jnp.asarray(np.kron(downward, downward), jnp.float32)
    return fine_stack, coarse_stack, lift_table, projection, mortar_up, mortar_down


def take_faces(volume):
    extent = volume.shape[-1]
    final_index = extent - 1
    pieces = (volume[:, :, 0], volume[:, :, final_index], volume[:, :, :, 0], volume[:, :, :, final_index], volume[:, :, :, :, 0], volume[:, :, :, :, final_index])
    return jnp.stack([face_part.reshape(volume.shape[0], volume.shape[1], extent * extent) for face_part in pieces], axis=1)


def add_faces(volume, face_terms):
    extent = volume.shape[-1]
    face_grids = face_terms.reshape(face_terms.shape[0], 6, face_terms.shape[2], extent, extent)
    total = volume
    for side_id in range(6):
        axis_id = 2 + side_id // 2
        piece = jnp.expand_dims(face_grids[:, side_id], axis_id)
        widths = [(0, 0)] * 5
        widths[axis_id] = (0, extent - 1) if side_id % 2 == 0 else (extent - 1, 0)
        total = total + jnp.pad(piece, widths)
    return total


def normal_speed(vel_faces):
    return jnp.stack([SIDE_SIGNS[side_id] * vel_faces[:, side_id, side_id // 2] for side_id in range(6)], axis=1)


def source_term(values, pre_exp, stoich):
    rate = pre_exp[:, None] * jnp.exp(-ACTIVATION * jnp.exp(-values[:, 0])) * values[:, 1] * values[:, 2]
    return stoich[None, :, None] * rate[:, None, :]


def fine_traces(values):
    elem_count, field_count, node_count = values.shape
    faces = take_faces(values.reshape(elem_count, field_count, P7, P7, P7)).astype(jnp.bfloat16)
    return faces.reshape(elem_count, 6, field_count * P7 * P7)


def coarse_traces(values, mortar_up):
    elem_count, field_count, node_count = values.shape
    faces = take_faces(values.reshape(elem_count, field_count, P3, P3, P3))
    mortar = jnp.einsum("mk,esfk->esfm", mortar_up, faces, precision=lax.Precision.HIGHEST)
    return mortar.astype(jnp.bfloat16).reshape(elem_count, 6, field_count * P7 * P7)


def fine_rate(values, fine_vel, pre_exp, stoich, own_tr, near_tr, fine_stack):
    elem_count, field_count, node_count = values.shape
    fluxes = (fine_vel.astype(jnp.float32)[:, None] * values[:, :, None]).astype(jnp.bfloat16)
    divergence = jnp.dot(fluxes.reshape(elem_count * field_count, 3 * node_count), fine_stack, preferred_element_type=jnp.float32).reshape(elem_count, field_count, node_count)
    result = source_term(values, pre_exp, stoich) - divergence
    normal_vel = normal_speed(take_faces(fine_vel.astype(jnp.float32).reshape(elem_count, 3, P7, P7, P7)))
    difference = (own_tr.astype(jnp.float32) - near_tr.astype(jnp.float32)).reshape(elem_count, 6, field_count, P7 * P7)
    jump_term = jnp.minimum(normal_vel, 0.0)[:, :, None] * difference
    lift_coef = P7 * (P7 - 1) / 2.0
    return add_faces(result.reshape(elem_count, field_count, P7, P7, P7), lift_coef * jump_term).reshape(elem_count, field_count, node_count)


def coarse_rate(values, coarse_vel, pre_exp, stoich, own_tr, near_tr, coarse_stack, mortar_up, mortar_down):
    elem_count, field_count, node_count = values.shape
    fluxes = (coarse_vel.astype(jnp.float32)[:, None] * values[:, :, None]).astype(jnp.bfloat16)
    divergence = jnp.einsum("dnm,efdm->efn", coarse_stack.astype(jnp.float32), fluxes.astype(jnp.float32))
    result = source_term(values, pre_exp, stoich) - divergence
    normal_vel = normal_speed(take_faces(coarse_vel.astype(jnp.float32).reshape(elem_count, 3, P3, P3, P3)))
    mortar_vel = jnp.einsum("mk,esk->esm", mortar_up, normal_vel, precision=lax.Precision.HIGHEST)
    difference = (own_tr.astype(jnp.float32) - near_tr.astype(jnp.float32)).reshape(elem_count, 6, field_count, P7 * P7)
    jump_term = jnp.minimum(mortar_vel, 0.0)[:, :, None] * difference
    coarse_jump = jnp.einsum("km,esfm->esfk", mortar_down, jump_term, precision=lax.Precision.HIGHEST)
    lift_coef = P3 * (P3 - 1) / 2.0
    return add_faces(result.reshape(elem_count, field_count, P3, P3, P3), lift_coef * coarse_jump).reshape(elem_count, field_count, node_count)


def blocked_fine(values, fine_vel, pre_exp, stoich, own_tr, near_tr, fine_stack):
    blocks = values.shape[0] // E_DEV

    def one_block(pieces):
        return fine_rate(pieces[0], pieces[1], pieces[2], stoich, pieces[3], pieces[4], fine_stack)

    packed = tuple(member.reshape((blocks, E_DEV) + member.shape[1:]) for member in (values, fine_vel, pre_exp, own_tr, near_tr))
    return lax.map(one_block, packed).reshape(values.shape)


def reference(state, velocity, pre_exp, stoich, neighbours, switch, new_owner):
    fine_stack, coarse_stack, lift_table, projection, mortar_up, mortar_down = make_tables()
    total_count = state.shape[0]
    trace_width = FIELDS * P7 * P7
    coarse_vel = jnp.transpose(velocity, (2, 0, 1))
    fine_vel = jnp.einsum("nm,edm->edn", lift_table.astype(jnp.float32), coarse_vel.astype(jnp.float32)).astype(jnp.bfloat16)
    gather_index = (neighbours * 6 + jnp.asarray(OPPOSITE, jnp.int32)[None, :]).astype(jnp.int32)

    def near_of(own_tr):
        return own_tr.reshape(total_count * 6, trace_width)[gather_index]

    def fine_only(current):
        own_tr = fine_traces(current)
        return blocked_fine(current, fine_vel, pre_exp, stoich, own_tr, near_of(own_tr), fine_stack)

    first_section = state + TIME_STEP * fine_only(state)
    after_one = 0.5 * (state + first_section + TIME_STEP * fine_only(first_section))
    coarse = jnp.einsum("mn,efn->efm", projection, after_one, precision=lax.Precision.HIGHEST)
    switched = (switch == 1)[:, None, None]

    def mixed(fine_now, coarse_now):
        own_fine = fine_traces(fine_now)
        own_coarse = coarse_traces(coarse_now, mortar_up)
        near_tr = near_of(jnp.where(switched, own_coarse, own_fine))
        fine_part = blocked_fine(fine_now, fine_vel, pre_exp, stoich, own_fine, near_tr, fine_stack)
        coarse_part = coarse_rate(coarse_now, coarse_vel, pre_exp, stoich, own_coarse, near_tr, coarse_stack, mortar_up, mortar_down)
        return fine_part, coarse_part

    fine_step, coarse_step = mixed(after_one, coarse)
    first_fine = after_one + TIME_STEP * fine_step
    first_coarse = coarse + TIME_STEP * coarse_step
    fine_again, coarse_again = mixed(first_fine, first_coarse)
    final_fine = 0.5 * (after_one + first_fine + TIME_STEP * fine_again)
    final_coarse = 0.5 * (coarse + first_coarse + TIME_STEP * coarse_again)

    element_ids = jnp.arange(total_count, dtype=jnp.int32)
    home_device = element_ids // E_DEV
    owner_dev = ((home_device // PIECES) * PIECES + new_owner).astype(jnp.int32)
    held_mask = switch == 0
    device_total = SLABS * PIECES
    sort_key = jnp.where(held_mask, owner_dev * total_count + element_ids, device_total * total_count + element_ids).astype(jnp.int32)
    ordering = jnp.argsort(sort_key).astype(jnp.int32)
    counts = jax.ops.segment_sum(held_mask.astype(jnp.int32), owner_dev, num_segments=device_total).astype(jnp.int32)
    starts = (jnp.cumsum(counts) - counts).astype(jnp.int32)
    sorted_owner = owner_dev[ordering]
    sorted_held = held_mask[ordering]
    slot_index = (element_ids - starts[sorted_owner]).astype(jnp.int32)
    target_rows = jnp.where(sorted_held, sorted_owner * HOLD7 + slot_index, device_total * HOLD7).astype(jnp.int32)
    state7_out = jnp.zeros((device_total * HOLD7, FIELDS, NODES7), jnp.float32).at[target_rows].set(final_fine[ordering], mode="drop")
    state3_out = jnp.where(switched, final_coarse, 0.0).reshape(total_count, FIELDS * NODES3)
    return state7_out, state3_out
```

```python
import functools

import jax
import jax.numpy as jnp
import ml_dtypes
import numpy as np
from jax import lax
from jax.experimental import pallas as pl
from jax.experimental.pallas import tpu as pltpu
from jax.sharding import PartitionSpec as P

P7 = 8
P3 = 4
ELEMS = 16
FIELDS = 8
LANES = ELEMS * FIELDS
HOLD7 = 12
STEP = 0.002
ACTIVATION = 1.5
MESH = pl.DeviceIdType.MESH
F32 = jnp.float32
BF16 = jnp.bfloat16


def lobatto_points(number):
    return -np.cos(np.pi * np.arange(number) / (number - 1))


def derivative_matrix(points):
    number = points.shape[0]
    weights = np.ones(number)
    for row in range(number):
        for col in range(number):
            if col != row:
                weights[row] = weights[row] / (points[row] - points[col])
    matrix = np.zeros((number, number))
    for row in range(number):
        for col in range(number):
            if col != row:
                matrix[row, col] = weights[col] / weights[row] / (points[row] - points[col])
        matrix[row, row] = -np.sum(matrix[row])
    return matrix


def interpolation_matrix(source, target):
    matrix = np.ones((target.shape[0], source.shape[0]))
    for col in range(source.shape[0]):
        for other in range(source.shape[0]):
            if other != col:
                matrix[:, col] = (
                    matrix[:, col] * (target - source[other]) / (source[col] - source[other])
                )
    return matrix


def kron3(a, b, c):
    return np.kron(a, np.kron(b, c))


def to_bf16(matrix):
    return np.asarray(matrix, np.float32).astype(ml_dtypes.bfloat16)


def split_columns(matrix):
    full = np.asarray(matrix, np.float32)
    high = full.astype(ml_dtypes.bfloat16)
    low = (full - high.astype(np.float32)).astype(ml_dtypes.bfloat16)
    return np.concatenate([high, low, high], axis=1)


def face_selectors(extent):
    ident = np.eye(extent)
    first, last = ident[:1], ident[-1:]
    picks = []
    for end in (first, last):
        picks.append(kron3(end, ident, ident))
    for end in (first, last):
        picks.append(kron3(ident, end, ident))
    for end in (first, last):
        picks.append(kron3(ident, ident, end))
    return np.stack(picks)


def make_tables():
    r7, r3 = lobatto_points(P7), lobatto_points(P3)
    d7, d3 = derivative_matrix(r7), derivative_matrix(r3)
    down = interpolation_matrix(r7, r3)
    up = interpolation_matrix(r3, r7)
    i7, i3 = np.eye(P7), np.eye(P3)
    div_i = np.kron(d7, np.eye(32))
    two = np.eye(2)
    div_jk = np.concatenate([np.kron(two, np.kron(d7, i7)), np.kron(two, np.kron(i7, d7))], axis=1)
    fine = to_bf16(np.concatenate([div_i, div_jk], axis=0))
    lift = to_bf16(kron3(up, up, up))
    project = split_columns(kron3(down, down, down))
    mortar_up = np.asarray(np.kron(up, up), np.float32).astype(np.float64)
    mortar_down = np.asarray(np.kron(down, down), np.float32).astype(np.float64)
    selectors = face_selectors(P3)
    raise_faces = split_columns(
        np.concatenate([mortar_up @ selectors[side] for side in range(6)], axis=0)
    )
    lower_faces = split_columns(
        np.concatenate([selectors[side].T @ mortar_down for side in range(6)], axis=1)
    )
    coarse = to_bf16(
        np.concatenate([kron3(d3, i3, i3), kron3(i3, d3, i3), kron3(i3, i3, d3)], axis=1)
    )
    return fine, lift, project, raise_faces, lower_faces, coarse


def dot(a, b):
    return jnp.dot(a, b, preferred_element_type=F32)


def split_rows(value):
    high = value.astype(BF16)
    low = (value - high.astype(F32)).astype(BF16)
    return jnp.concatenate([high, high, low], axis=0)


def face_slices(side):
    dim, end = side // 2, side % 2
    if dim == 0:
        return [pl.ds(448 * end, 64)]
    if dim == 1:
        return [pl.ds(i * 64 + 56 * end, 8) for i in range(P7)]
    return [pl.ds(7 * end, 64, stride=8)]


def face_get(ref, side):
    parts = [ref[where, :] for where in face_slices(side)]
    return parts[0] if len(parts) == 1 else jnp.concatenate(parts, axis=0)


def face_add(ref, side, value):
    start = 0
    for where in face_slices(side):
        ref[where, :] += value[start : start + where.size]
        start += where.size


def kernel(
    slabs,
    pieces,
    state_h,
    vel_h,
    nbr_h,
    pre_h,
    stoich_h,
    switch_h,
    owner_h,
    fine_h,
    lift_h,
    project_h,
    raise_h,
    lower_h,
    coarse_h,
    out7_h,
    out3_h,
    state_v,
    vel_v,
    nbr_v,
    pre_s,
    stoich_s,
    switch_s,
    owner_s,
    fine_v,
    lift_v,
    project_v,
    raise_v,
    lower_v,
    coarse_v,
    u0,
    u1,
    u2,
    u3,
    speed,
    coef,
    vel_rep,
    vmin,
    perm_x,
    perm_o,
    local_nb,
    send,
    recv,
    count_send,
    count_recv,
    home,
    move_send,
    move_recv,
    out7_v,
    out3_v,
    turned,
    home_list,
    load_sem,
    send_sem,
    recv_sem,
    count_ssem,
    count_rsem,
    move_ssem,
    move_rsem,
    store_sem,
):
    slab, pos = lax.axis_index("slab"), lax.axis_index("curve")
    left, right = lax.rem(pos + pieces - 1, pieces), lax.rem(pos + 1, pieces)
    below, above = lax.rem(slab + slabs - 1, slabs), lax.rem(slab + 1, slabs)
    partner = {0: (slab, left), 1: (slab, right), 4: (below, pos), 5: (above, pos)}

    barrier = pltpu.get_barrier_semaphore()
    for side in (0, 1, 4, 5):
        pl.semaphore_signal(barrier, inc=1, device_id=partner[side], device_id_type=MESH)

    pairs = [
        (state_h, state_v),
        (vel_h, vel_v),
        (nbr_h, nbr_v),
        (lift_h, lift_v),
        (pre_h, pre_s),
        (stoich_h, stoich_s),
        (switch_h, switch_s),
        (owner_h, owner_s),
        (fine_h, fine_v),
        (raise_h, raise_v),
        (project_h, project_v),
        (lower_h, lower_v),
        (coarse_h, coarse_v),
    ]
    loads = [
        pltpu.make_async_copy(source, target, load_sem.at[number])
        for number, (source, target) in enumerate(pairs)
    ]
    for load in loads:
        load.start()

    lane_row = lax.broadcasted_iota(jnp.int32, (1, LANES), 1)
    lane_elem = lane_row // FIELDS
    lane_field = lane_row % FIELDS
    lanes = lax.broadcasted_iota(jnp.int32, (LANES, LANES), 1)
    rows = lax.broadcasted_iota(jnp.int32, (LANES, LANES), 0)
    spread = (
        lax.broadcasted_iota(jnp.int32, (ELEMS, LANES), 0)
        == lax.broadcasted_iota(jnp.int32, (ELEMS, LANES), 1) // FIELDS
    ).astype(F32)
    rep = ((rows % FIELDS == 0) & (rows // FIELDS == lanes // FIELDS)).astype(F32).astype(BF16)
    rep2 = jnp.concatenate([rep, rep], axis=0)

    loads[0].wait()
    u0[...] = jnp.transpose(state_v[...].reshape(LANES, 512))

    loads[2].wait()
    ids = nbr_v[...]
    me = slab * pieces + pos
    here = lax.shift_right_logical(ids, 4) == me
    code = jnp.where(here, ids & 15, (ids & 15) + 16).astype(F32)
    spread_t = (
        lax.broadcasted_iota(jnp.int32, (LANES, ELEMS), 1)
        == lax.broadcasted_iota(jnp.int32, (LANES, ELEMS), 0) // FIELDS
    ).astype(F32)
    target = dot(spread_t.astype(BF16), code.astype(BF16)).astype(jnp.int32) * FIELDS
    target = target + lax.broadcasted_iota(jnp.int32, (LANES, 6), 0) % FIELDS
    for side in range(6):
        column = target[:, side : side + 1]
        near = (column == lanes).astype(F32).astype(BF16)
        far = (column == lanes + LANES).astype(F32).astype(BF16)
        if side < 2:
            perm_x[side, :, :LANES] = far
            perm_x[side, :, LANES:] = near
        else:
            perm_o[side - 2] = near if side < 4 else far

    def post(number, traces):
        copies = []
        for side in (0, 1, 4, 5):
            if side < 2:
                both = dot(traces[side], perm_x[side])
                send[number, side] = both[:, :LANES].astype(BF16)
                local_nb[side ^ 1] = both[:, LANES:]
                slot = side
            else:
                slot = side - 2
                send[number, slot] = dot(traces[side], perm_o[side - 2]).astype(BF16)
            copy = pltpu.make_async_remote_copy(
                src_ref=send.at[number, slot],
                dst_ref=recv.at[number, slot ^ 1],
                send_sem=send_sem.at[number, slot],
                recv_sem=recv_sem.at[number, slot ^ 1],
                device_id=partner[side],
                device_id_type=MESH,
            )
            copy.start()
            copies.append(copy)
        for side in (2, 3):
            local_nb[side ^ 1] = dot(traces[side], perm_o[side - 2])
        return copies

    def fine_traces(ref):
        return [face_get(ref, side).astype(BF16) for side in range(6)]

    traces = fine_traces(u0)
    pl.semaphore_wait(barrier, 4)
    copies = post(0, traces)

    loads[6].wait()
    loads[7].wait()
    left_count = right_count = home_count = jnp.int32(0)
    left_pick = [jnp.int32(0)] * 2
    right_pick = [jnp.int32(0)] * 2
    home_pick = [jnp.int32(0)] * HOLD7
    switch_row = jnp.zeros((1, LANES), F32)
    for elem in range(ELEMS):
        switched = switch_s[elem]
        owner = owner_s[elem]
        switch_row = jnp.where(lane_elem == elem, switched.astype(F32), switch_row)
        fine_one = switched != 1
        goes_left = fine_one & (owner == left)
        goes_right = fine_one & (owner == right)
        stays = fine_one & jnp.logical_not(owner == left) & jnp.logical_not(owner == right)
        for slot in range(2):
            left_pick[slot] = jnp.where(goes_left & (left_count == slot), elem, left_pick[slot])
            right_pick[slot] = jnp.where(goes_right & (right_count == slot), elem, right_pick[slot])
        for slot in range(min(elem + 1, HOLD7)):
            home_pick[slot] = jnp.where(stays & (home_count == slot), elem, home_pick[slot])
        left_count = left_count + goes_left.astype(jnp.int32)
        right_count = right_count + goes_right.astype(jnp.int32)
        home_count = home_count + stays.astype(jnp.int32)
    for slot in range(HOLD7):
        home_list[slot] = home_pick[slot]
    count_send[0] = jnp.full((8, LANES), left_count, jnp.int32)
    count_send[1] = jnp.full((8, LANES), right_count, jnp.int32)
    for side in (0, 1):
        copy = pltpu.make_async_remote_copy(
            src_ref=count_send.at[side],
            dst_ref=count_recv.at[side ^ 1],
            send_sem=count_ssem.at[side],
            recv_sem=count_rsem.at[side ^ 1],
            device_id=partner[side],
            device_id_type=MESH,
        )
        copy.start()
        copies.append(copy)
    is_switched = switch_row > 0.5

    loads[1].wait()
    loads[3].wait()
    loads[9].wait()
    for dim in range(3):
        spread_vel = dot(vel_v[dim], spread.astype(BF16)).astype(BF16)
        vel_rep[dim * 64 : dim * 64 + 64] = spread_vel.astype(F32)
        speed[dim] = dot(lift_v[...], spread_vel).astype(BF16).astype(F32)
        mortar = dot(raise_v[dim * 128 : dim * 128 + 128, :128], jnp.concatenate([spread_vel, spread_vel], axis=0))
        vmin[dim * 128 : dim * 128 + 64] = jnp.minimum(-mortar[:64], 0.0)
        vmin[dim * 128 + 64 : dim * 128 + 128] = jnp.minimum(mortar[64:], 0.0)
        for end in range(2):
            side = 2 * dim + end
            normal = face_get(speed.at[dim], side)
            lift_coef = STEP * (P7 * (P7 - 1) / 2.0)
            coef[side] = lift_coef * jnp.minimum(normal if end else -normal, 0.0)

    loads[4].wait()
    loads[5].wait()
    pre_row = jnp.zeros((1, LANES), F32)
    stoich_row = jnp.zeros((1, LANES), F32)
    for elem in range(ELEMS):
        pre_row = jnp.where(lane_elem == elem, pre_s[elem], pre_row)
    for field in range(FIELDS):
        stoich_row = jnp.where(lane_field == field, stoich_s[field], stoich_row)

    def source(u):
        rate = (
            pre_row
            * jnp.exp(-ACTIVATION * jnp.exp(-u))
            * pltpu.roll(u, LANES - 1, 1)
            * pltpu.roll(u, LANES - 2, 1)
        )
        high = rate.astype(BF16)
        low = (rate - high.astype(F32)).astype(BF16)
        return stoich_row * dot(jnp.concatenate([high, low], axis=1), rep2)

    for number in range(8, 13):
        if number != 9:
            loads[number].wait()

    def fine_start(ref, start, out, traces):
        scale = 1.0 if start is None else 0.5
        along_i = []
        for half in range(2):
            parts = []
            for i in range(P7):
                at = pl.ds(i * 64 + half * 32, 32)
                parts.append((speed[0, at, :] * ref[at, :]).astype(BF16))
            along_i.append(dot(fine_v[:256, :], jnp.concatenate(parts, axis=0)))
        for block in range(4):
            at = pl.ds(block * 128, 128)
            u = ref[at, :]
            flux = jnp.concatenate(
                [(speed[1, at, :] * u).astype(BF16), (speed[2, at, :] * u).astype(BF16)], axis=0
            )
            div = dot(fine_v[256:, :], flux) + jnp.concatenate(
                [
                    along_i[half][i * 32 : i * 32 + 32]
                    for i in (2 * block, 2 * block + 1)
                    for half in range(2)
                ],
                axis=0,
            )
            rate = STEP * (source(u) - div)
            out[at, :] = u + rate if start is None else 0.5 * (start[at, :] + u + rate)
        for side in range(6):
            jump = traces[side].astype(F32)
            if side < 4:
                jump = jump - local_nb[side]
            face_add(out, side, scale * (coef[side] * jump))

    def fine_end(number, copies, start, out):
        scale = 1.0 if start is None else 0.5
        for copy in copies:
            copy.wait()
        for side in (0, 1, 4, 5):
            slot = side if side < 2 else side - 2
            face_add(out, side, -scale * (coef[side] * recv[number, slot].astype(F32)))

    def coarse_traces(c):
        return dot(raise_v[...], split_rows(c))

    def coarse_start(c, start):
        flux = jnp.concatenate(
            [(vel_rep[dim * 64 : dim * 64 + 64] * c).astype(BF16) for dim in range(3)], axis=0
        )
        rate = STEP * (source(c) - dot(coarse_v[...], flux))
        return c + rate if start is None else 0.5 * (start + c + rate)

    def coarse_end(number, own, start, partial):
        scale = 1.0 if start is None else 0.5
        jumps = []
        for side in range(6):
            near = None
            if side < 4:
                near = local_nb[side]
            if side not in (2, 3):
                far = recv[number, side if side < 2 else side - 2].astype(F32)
                near = far if near is None else near + far
            mine = own[side * 64 : side * 64 + 64].astype(F32)
            jumps.append(vmin[side * 64 : side * 64 + 64] * (mine - near))
        lift_coef = scale * STEP * (P3 * (P3 - 1) / 2.0)
        return partial + lift_coef * dot(lower_v[...], split_rows(jnp.concatenate(jumps, axis=0)))

    def mixed(fine, raised):
        return [
            jnp.where(is_switched, raised[side * 64 : side * 64 + 64], fine[side].astype(F32)).astype(BF16)
            for side in range(6)
        ]

    fine_start(u0, None, u1, traces)
    fine_end(0, copies, None, u1)
    traces = fine_traces(u1)
    copies = post(1, traces)
    fine_start(u1, u0, u2, traces)
    fine_end(1, copies, u0, u2)

    c0 = dot(project_v[...], split_rows(u2[...]))
    traces = fine_traces(u2)
    raised = coarse_traces(c0)
    copies = post(2, mixed(traces, raised))
    own = raised.astype(BF16)
    fine_start(u2, None, u3, traces)
    partial = coarse_start(c0, None)
    fine_end(2, copies, None, u3)
    c1 = coarse_end(2, own, None, partial)
    traces = fine_traces(u3)
    raised = coarse_traces(c1)
    copies = post(3, mixed(traces, raised))
    own = raised.astype(BF16)
    fine_start(u3, u2, u1, traces)
    partial = coarse_start(c1, c0)
    fine_end(3, copies, u2, u1)

    for number in range(4):
        home[:, :, number * 128 : number * 128 + 128] = jnp.transpose(
            u1[number * 128 : number * 128 + 128, :]
        ).reshape(ELEMS, FIELDS, 128)
    copies = []
    for side in range(2):
        for slot in range(2):
            pick = (left_pick, right_pick)[side][slot]
            move_send[side, slot] = home[pick]
        copy = pltpu.make_async_remote_copy(
            src_ref=move_send.at[side],
            dst_ref=move_recv.at[side ^ 1],
            send_sem=move_ssem.at[side],
            recv_sem=move_rsem.at[side ^ 1],
            device_id=partner[side],
            device_id_type=MESH,
        )
        copy.start()
        copies.append(copy)

    c2 = coarse_end(3, own, c0, partial)
    c2 = jnp.where(is_switched, c2, 0.0)
    turned[...] = jnp.transpose(jnp.concatenate([c2, pltpu.roll(c2, LANES - 1, 1)], axis=0))
    for pair in range(4):
        out3_v[:, pair * 128 : pair * 128 + 128] = turned[pl.ds(2 * pair, ELEMS, stride=FIELDS), :]
    store3 = pltpu.make_async_copy(out3_v, out3_h, store_sem.at[0])
    store3.start()

    from_left = count_recv[0][0, 0]
    from_right = count_recv[1][0, 0]
    is_first, is_last = pos == 0, pos == pieces - 1
    at_left = jnp.where(is_first, home_count + from_right, jnp.where(is_last, from_right, 0))
    at_home = jnp.where(is_first, 0, jnp.where(is_last, from_right + from_left, from_left))
    at_right = jnp.where(is_first, home_count, jnp.where(is_last, 0, from_left + home_count))
    picks = []
    for slot in range(HOLD7):
        rank = slot - at_home
        stay = (rank >= 0) & (rank < home_count)
        value = home[home_list[jnp.clip(rank, 0, HOLD7 - 1)]]
        out7_v[slot] = jnp.where(stay, value, 0.0)
        rank_left, rank_right = slot - at_left, slot - at_right
        is_left = (rank_left >= 0) & (rank_left < from_left)
        is_right = (rank_right >= 0) & (rank_right < from_right)
        pick = jnp.where(is_left, rank_left, jnp.where(is_right, 2 + rank_right, 0))
        picks.append((is_left | is_right, pick))
    for copy in copies:
        copy.wait()
    for slot in range(HOLD7):
        arrived, pick = picks[slot]
        value = move_recv[pick // 2, pick % 2]
        out7_v[slot] = jnp.where(arrived, value, out7_v[slot])
    store7 = pltpu.make_async_copy(out7_v, out7_h, store_sem.at[1])
    store7.start()
    store3.wait()
    store7.wait()


def solution(mesh):
    slabs, pieces = mesh.shape["slab"], mesh.shape["curve"]
    tables = make_tables()

    def per_device(state, velocity, pre_exp, stoich, neighbours, switch, new_owner):
        operands = (state, velocity, neighbours, pre_exp, stoich, switch, new_owner) + tuple(
            jnp.asarray(table) for table in tables
        )
        vm, sm, dma = pltpu.VMEM, pltpu.SMEM, pltpu.SemaphoreType.DMA
        nodes = (512, LANES)
        return pl.pallas_call(
            functools.partial(kernel, slabs, pieces),
            out_shape=(
                jax.ShapeDtypeStruct((HOLD7, FIELDS, 512), F32),
                jax.ShapeDtypeStruct((ELEMS, 512), F32),
            ),
            in_specs=[pl.BlockSpec(memory_space=pl.ANY)] * len(operands),
            out_specs=[pl.BlockSpec(memory_space=pl.ANY)] * 2,
            scratch_shapes=[
                vm((ELEMS, FIELDS, 512), F32),
                vm((3, 64, ELEMS), BF16),
                vm((ELEMS, 6), jnp.int32),
                sm((ELEMS,), F32),
                sm((FIELDS,), F32),
                sm((ELEMS,), jnp.int32),
                sm((ELEMS,), jnp.int32),
            ]
            + [vm(table.shape, BF16) for table in tables]
            + [
                vm(nodes, F32),
                vm(nodes, F32),
                vm(nodes, F32),
                vm(nodes, F32),
                vm((3, 512, LANES), F32),
                vm((6, 64, LANES), F32),
                vm((192, LANES), F32),
                vm((384, LANES), F32),
                vm((2, LANES, 2 * LANES), BF16),
                vm((4, LANES, LANES), BF16),
                vm((4, 64, LANES), F32),
                vm((4, 4, 64, LANES), BF16),
                vm((4, 4, 64, LANES), BF16),
                vm((2, 8, LANES), jnp.int32),
                vm((2, 8, LANES), jnp.int32),
                vm((ELEMS, FIELDS, 512), F32),
                vm((2, 2, FIELDS, 512), F32),
                vm((2, 2, FIELDS, 512), F32),
                vm((HOLD7, FIELDS, 512), F32),
                vm((ELEMS, 512), F32),
                vm((LANES, LANES), F32),
                sm((HOLD7,), jnp.int32),
                dma((13,)),
                dma((4, 4)),
                dma((4, 4)),
                dma((2,)),
                dma((2,)),
                dma((2,)),
                dma((2,)),
                dma((2,)),
            ],
            compiler_params=pltpu.CompilerParams(
                collective_id=0, has_side_effects=True, vmem_limit_bytes=40 * 2**20
            ),
        )(*operands)

    return jax.shard_map(
        per_device,
        mesh=mesh,
        in_specs=(
            P(("slab", "curve"), None, None),
            P(None, None, ("slab", "curve")),
            P(("slab", "curve")),
            P(),
            P(("slab", "curve"), None),
            P(("slab", "curve")),
            P(("slab", "curve")),
        ),
        out_specs=(P(("slab", "curve"), None, None), P(("slab", "curve"), None)),
        check_vma=False,
    )
```

```python
import functools

import jax
import jax.numpy as jnp
import ml_dtypes
import numpy as np
from jax import lax
from jax.experimental import pallas as pl
from jax.experimental.pallas import tpu as pltpu
from jax.sharding import PartitionSpec as P

P7 = 8
P3 = 4
ELEMS = 16
FIELDS = 8
LANES = ELEMS * FIELDS
HOLD7 = 12
STEP = 0.002
ACTIVATION = 1.5
MESH = pl.DeviceIdType.MESH
F32 = jnp.float32
BF16 = jnp.bfloat16


def lobatto_points(number):
    return -np.cos(np.pi * np.arange(number) / (number - 1))


def derivative_matrix(points):
    number = points.shape[0]
    weights = np.ones(number)
    for row in range(number):
        for col in range(number):
            if col != row:
                weights[row] = weights[row] / (points[row] - points[col])
    matrix = np.zeros((number, number))
    for row in range(number):
        for col in range(number):
            if col != row:
                matrix[row, col] = weights[col] / weights[row] / (points[row] - points[col])
        matrix[row, row] = -np.sum(matrix[row])
    return matrix


def interpolation_matrix(source, target):
    matrix = np.ones((target.shape[0], source.shape[0]))
    for col in range(source.shape[0]):
        for other in range(source.shape[0]):
            if other != col:
                matrix[:, col] = (
                    matrix[:, col] * (target - source[other]) / (source[col] - source[other])
                )
    return matrix


def kron3(a, b, c):
    return np.kron(a, np.kron(b, c))


def to_bf16(matrix):
    return np.asarray(matrix, np.float32).astype(ml_dtypes.bfloat16)


def split_columns(matrix):
    full = np.asarray(matrix, np.float32)
    high = full.astype(ml_dtypes.bfloat16)
    low = (full - high.astype(np.float32)).astype(ml_dtypes.bfloat16)
    return np.concatenate([high, low, high], axis=1)


def face_selectors(extent):
    ident = np.eye(extent)
    first, last = ident[:1], ident[-1:]
    picks = []
    for end in (first, last):
        picks.append(kron3(end, ident, ident))
    for end in (first, last):
        picks.append(kron3(ident, end, ident))
    for end in (first, last):
        picks.append(kron3(ident, ident, end))
    return np.stack(picks)


def make_tables():
    r7, r3 = lobatto_points(P7), lobatto_points(P3)
    d7, d3 = derivative_matrix(r7), derivative_matrix(r3)
    down = interpolation_matrix(r7, r3)
    up = interpolation_matrix(r3, r7)
    i7, i3 = np.eye(P7), np.eye(P3)
    div_i = np.kron(d7, np.eye(32))
    two = np.eye(2)
    div_jk = np.concatenate([np.kron(two, np.kron(d7, i7)), np.kron(two, np.kron(i7, d7))], axis=1)
    fine = to_bf16(np.concatenate([div_i, div_jk], axis=0))
    lift = to_bf16(kron3(up, up, up))
    project = split_columns(kron3(down, down, down))
    mortar_up = np.asarray(np.kron(up, up), np.float32).astype(np.float64)
    mortar_down = np.asarray(np.kron(down, down), np.float32).astype(np.float64)
    selectors = face_selectors(P3)
    raise_faces = split_columns(
        np.concatenate([mortar_up @ selectors[side] for side in range(6)], axis=0)
    )
    lower_faces = split_columns(
        np.concatenate([selectors[side].T @ mortar_down for side in range(6)], axis=1)
    )
    coarse = to_bf16(
        np.concatenate([kron3(d3, i3, i3), kron3(i3, d3, i3), kron3(i3, i3, d3)], axis=1)
    )
    return fine, lift, project, raise_faces, lower_faces, coarse


def dot(a, b):
    return jnp.dot(a, b, preferred_element_type=F32)


def split_rows(value):
    high = value.astype(BF16)
    low = (value - high.astype(F32)).astype(BF16)
    return jnp.concatenate([high, high, low], axis=0)


def face_slices(side):
    dim, end = side // 2, side % 2
    if dim == 0:
        return [pl.ds(448 * end, 64)]
    if dim == 1:
        return [pl.ds(i * 64 + 56 * end, 8) for i in range(P7)]
    return [pl.ds(7 * end, 64, stride=8)]


def face_get(ref, side):
    parts = [ref[where, :] for where in face_slices(side)]
    return parts[0] if len(parts) == 1 else jnp.concatenate(parts, axis=0)


def face_add(ref, side, value):
    start = 0
    for where in face_slices(side):
        ref[where, :] += value[start : start + where.size]
        start += where.size


def kernel(
    slabs,
    pieces,
    state_h,
    vel_h,
    nbr_h,
    pre_h,
    stoich_h,
    switch_h,
    owner_h,
    fine_h,
    lift_h,
    project_h,
    raise_h,
    lower_h,
    coarse_h,
    out7_h,
    out3_h,
    state_v,
    vel_v,
    nbr_v,
    pre_s,
    stoich_s,
    switch_s,
    owner_s,
    fine_v,
    lift_v,
    project_v,
    raise_v,
    lower_v,
    coarse_v,
    u0,
    u1,
    u2,
    u3,
    speed,
    coef,
    vel_rep,
    vmin,
    perm_x,
    perm_o,
    local_nb,
    send,
    recv,
    count_send,
    count_recv,
    home,
    move_send,
    move_recv,
    out7_v,
    out3_v,
    turned,
    home_list,
    load_sem,
    send_sem,
    recv_sem,
    count_ssem,
    count_rsem,
    move_ssem,
    move_rsem,
    store_sem,
):
    slab, pos = lax.axis_index("slab"), lax.axis_index("curve")
    left, right = lax.rem(pos + pieces - 1, pieces), lax.rem(pos + 1, pieces)
    below, above = lax.rem(slab + slabs - 1, slabs), lax.rem(slab + 1, slabs)
    partner = {0: (slab, left), 1: (slab, right), 4: (below, pos), 5: (above, pos)}

    barrier = pltpu.get_barrier_semaphore()
    for side in (0, 1, 4, 5):
        pl.semaphore_signal(barrier, inc=1, device_id=partner[side], device_id_type=MESH)

    pairs = [
        (state_h, state_v),
        (vel_h, vel_v),
        (nbr_h, nbr_v),
        (lift_h, lift_v),
        (pre_h, pre_s),
        (stoich_h, stoich_s),
        (switch_h, switch_s),
        (owner_h, owner_s),
        (fine_h, fine_v),
        (raise_h, raise_v),
        (project_h, project_v),
        (lower_h, lower_v),
        (coarse_h, coarse_v),
    ]
    loads = [
        pltpu.make_async_copy(source, target, load_sem.at[number])
        for number, (source, target) in enumerate(pairs)
    ]
    for load in loads:
        load.start()

    lane_row = lax.broadcasted_iota(jnp.int32, (1, LANES), 1)
    lane_elem = lane_row // FIELDS
    lane_field = lane_row % FIELDS
    lanes = lax.broadcasted_iota(jnp.int32, (LANES, LANES), 1)
    rows = lax.broadcasted_iota(jnp.int32, (LANES, LANES), 0)
    spread = (
        lax.broadcasted_iota(jnp.int32, (ELEMS, LANES), 0)
        == lax.broadcasted_iota(jnp.int32, (ELEMS, LANES), 1) // FIELDS
    ).astype(F32)
    rep = ((rows % FIELDS == 0) & (rows // FIELDS == lanes // FIELDS)).astype(F32).astype(BF16)
    rep2 = jnp.concatenate([rep, rep], axis=0)

    loads[0].wait()
    u0[...] = jnp.transpose(state_v[...].reshape(LANES, 512))

    loads[2].wait()
    ids = nbr_v[...]
    me = slab * pieces + pos
    here = lax.shift_right_logical(ids, 4) == me
    code = jnp.where(here, ids & 15, (ids & 15) + 16).astype(F32)
    spread_t = (
        lax.broadcasted_iota(jnp.int32, (LANES, ELEMS), 1)
        == lax.broadcasted_iota(jnp.int32, (LANES, ELEMS), 0) // FIELDS
    ).astype(F32)
    target = lax.dot_general(
        spread_t.astype(BF16),
        code.astype(BF16),
        (((1,), (1,)), ((), ())),
        preferred_element_type=F32,
    )
    target = target.astype(jnp.int32) * FIELDS
    target = target + lax.broadcasted_iota(jnp.int32, (LANES, 6), 0) % FIELDS
    for side in range(6):
        column = target[:, side : side + 1]
        near = (column == lanes).astype(F32).astype(BF16)
        far = (column == lanes + LANES).astype(F32).astype(BF16)
        if side < 2:
            perm_x[side, :, :LANES] = far
            perm_x[side, :, LANES:] = near
        else:
            perm_o[side - 2] = near if side < 4 else far

    def post(number, traces):
        copies = []
        for side in (0, 1, 4, 5):
            if side < 2:
                both = dot(traces[side], perm_x[side])
                send[number, side] = both[:, :LANES].astype(BF16)
                local_nb[side ^ 1] = both[:, LANES:]
                slot = side
            else:
                slot = side - 2
                send[number, slot] = dot(traces[side], perm_o[side - 2]).astype(BF16)
            copy = pltpu.make_async_remote_copy(
                src_ref=send.at[number, slot],
                dst_ref=recv.at[number, slot ^ 1],
                send_sem=send_sem.at[number, slot],
                recv_sem=recv_sem.at[number, slot ^ 1],
                device_id=partner[side],
                device_id_type=MESH,
            )
            copy.start()
            copies.append(copy)
        for side in (2, 3):
            local_nb[side ^ 1] = dot(traces[side], perm_o[side - 2])
        return copies

    def fine_traces(ref):
        return [face_get(ref, side).astype(BF16) for side in range(6)]

    traces = fine_traces(u0)
    pl.semaphore_wait(barrier, 4)
    copies = post(0, traces)

    loads[6].wait()
    loads[7].wait()
    left_count = right_count = home_count = jnp.int32(0)
    left_pick = [jnp.int32(0)] * 2
    right_pick = [jnp.int32(0)] * 2
    home_pick = [jnp.int32(0)] * HOLD7
    switch_row = jnp.zeros((1, LANES), F32)
    for elem in range(ELEMS):
        switched = switch_s[elem]
        owner = owner_s[elem]
        switch_row = jnp.where(lane_elem == elem, switched.astype(F32), switch_row)
        fine_one = switched != 1
        goes_left = fine_one & (owner == left)
        goes_right = fine_one & (owner == right)
        stays = fine_one & jnp.logical_not(owner == left) & jnp.logical_not(owner == right)
        for slot in range(2):
            left_pick[slot] = jnp.where(goes_left & (left_count == slot), elem, left_pick[slot])
            right_pick[slot] = jnp.where(goes_right & (right_count == slot), elem, right_pick[slot])
        for slot in range(min(elem + 1, HOLD7)):
            home_pick[slot] = jnp.where(stays & (home_count == slot), elem, home_pick[slot])
        left_count = left_count + goes_left.astype(jnp.int32)
        right_count = right_count + goes_right.astype(jnp.int32)
        home_count = home_count + stays.astype(jnp.int32)
    for slot in range(HOLD7):
        home_list[slot] = home_pick[slot]
    count_send[0] = jnp.full((8, LANES), left_count, jnp.int32)
    count_send[1] = jnp.full((8, LANES), right_count, jnp.int32)
    for side in (0, 1):
        copy = pltpu.make_async_remote_copy(
            src_ref=count_send.at[side],
            dst_ref=count_recv.at[side ^ 1],
            send_sem=count_ssem.at[side],
            recv_sem=count_rsem.at[side ^ 1],
            device_id=partner[side],
            device_id_type=MESH,
        )
        copy.start()
        copies.append(copy)
    is_switched = switch_row > 0.5

    loads[1].wait()
    loads[3].wait()
    loads[9].wait()
    for dim in range(3):
        spread_vel = lax.dot_general(
            vel_v[dim],
            spread.astype(BF16),
            (((0,), (0,)), ((), ())),
            preferred_element_type=F32,
        ).astype(BF16)
        vel_rep[dim * 64 : dim * 64 + 64] = spread_vel.astype(F32)
        speed[dim] = dot(lift_v[...], spread_vel).astype(BF16).astype(F32)
        mortar = dot(raise_v[dim * 128 : dim * 128 + 128, :128], jnp.concatenate([spread_vel, spread_vel], axis=0))
        vmin[dim * 128 : dim * 128 + 64] = jnp.minimum(-mortar[:64], 0.0)
        vmin[dim * 128 + 64 : dim * 128 + 128] = jnp.minimum(mortar[64:], 0.0)
        for end in range(2):
            side = 2 * dim + end
            normal = face_get(speed.at[dim], side)
            lift_coef = STEP * (P7 * (P7 - 1) / 2.0)
            coef[side] = lift_coef * jnp.minimum(normal if end else -normal, 0.0)

    loads[4].wait()
    loads[5].wait()
    pre_row = jnp.zeros((1, LANES), F32)
    stoich_row = jnp.zeros((1, LANES), F32)
    for elem in range(ELEMS):
        pre_row = jnp.where(lane_elem == elem, pre_s[elem], pre_row)
    for field in range(FIELDS):
        stoich_row = jnp.where(lane_field == field, stoich_s[field], stoich_row)

    def source(u):
        rate = (
            pre_row
            * jnp.exp(-ACTIVATION * jnp.exp(-u))
            * pltpu.roll(u, LANES - 1, 1)
            * pltpu.roll(u, LANES - 2, 1)
        )
        high = rate.astype(BF16)
        low = (rate - high.astype(F32)).astype(BF16)
        return stoich_row * dot(jnp.concatenate([high, low], axis=1), rep2)

    for number in range(8, 13):
        if number != 9:
            loads[number].wait()

    def fine_start(ref, start, out, traces):
        scale = 1.0 if start is None else 0.5
        along_i = []
        for half in range(2):
            parts = []
            for i in range(P7):
                at = pl.ds(i * 64 + half * 32, 32)
                parts.append((speed[0, at, :] * ref[at, :]).astype(BF16))
            along_i.append(dot(fine_v[:256, :], jnp.concatenate(parts, axis=0)))
        for block in range(4):
            at = pl.ds(block * 128, 128)
            u = ref[at, :]
            flux = jnp.concatenate(
                [(speed[1, at, :] * u).astype(BF16), (speed[2, at, :] * u).astype(BF16)], axis=0
            )
            div = dot(fine_v[256:, :], flux) + jnp.concatenate(
                [
                    along_i[half][i * 32 : i * 32 + 32]
                    for i in (2 * block, 2 * block + 1)
                    for half in range(2)
                ],
                axis=0,
            )
            rate = STEP * (source(u) - div)
            out[at, :] = u + rate if start is None else 0.5 * (start[at, :] + u + rate)
        for side in range(6):
            jump = traces[side].astype(F32)
            if side < 4:
                jump = jump - local_nb[side]
            face_add(out, side, scale * (coef[side] * jump))

    def fine_end(number, copies, start, out):
        scale = 1.0 if start is None else 0.5
        for copy in copies:
            copy.wait()
        for side in (0, 1, 4, 5):
            slot = side if side < 2 else side - 2
            face_add(out, side, -scale * (coef[side] * recv[number, slot].astype(F32)))

    def coarse_traces(c):
        return dot(raise_v[...], split_rows(c))

    def coarse_start(c, start):
        flux = jnp.concatenate(
            [(vel_rep[dim * 64 : dim * 64 + 64] * c).astype(BF16) for dim in range(3)], axis=0
        )
        rate = STEP * (source(c) - dot(coarse_v[...], flux))
        return c + rate if start is None else 0.5 * (start + c + rate)

    def coarse_end(number, own, start, partial):
        scale = 1.0 if start is None else 0.5
        jumps = []
        for side in range(6):
            near = None
            if side < 4:
                near = local_nb[side]
            if side not in (2, 3):
                far = recv[number, side if side < 2 else side - 2].astype(F32)
                near = far if near is None else near + far
            mine = own[side * 64 : side * 64 + 64].astype(F32)
            jumps.append(vmin[side * 64 : side * 64 + 64] * (mine - near))
        lift_coef = scale * STEP * (P3 * (P3 - 1) / 2.0)
        return partial + lift_coef * dot(lower_v[...], split_rows(jnp.concatenate(jumps, axis=0)))

    def mixed(fine, raised):
        return [
            jnp.where(is_switched, raised[side * 64 : side * 64 + 64], fine[side].astype(F32)).astype(BF16)
            for side in range(6)
        ]

    fine_start(u0, None, u1, traces)
    fine_end(0, copies, None, u1)
    traces = fine_traces(u1)
    copies = post(1, traces)
    fine_start(u1, u0, u2, traces)
    fine_end(1, copies, u0, u2)

    c0 = dot(project_v[...], split_rows(u2[...]))
    traces = fine_traces(u2)
    raised = coarse_traces(c0)
    copies = post(2, mixed(traces, raised))
    own = raised.astype(BF16)
    fine_start(u2, None, u3, traces)
    partial = coarse_start(c0, None)
    fine_end(2, copies, None, u3)
    c1 = coarse_end(2, own, None, partial)
    traces = fine_traces(u3)
    raised = coarse_traces(c1)
    copies = post(3, mixed(traces, raised))
    own = raised.astype(BF16)
    fine_start(u3, u2, u1, traces)
    partial = coarse_start(c1, c0)
    fine_end(3, copies, u2, u1)

    for number in range(4):
        home[:, :, number * 128 : number * 128 + 128] = jnp.transpose(
            u1[number * 128 : number * 128 + 128, :]
        ).reshape(ELEMS, FIELDS, 128)
    copies = []
    for side in range(2):
        for slot in range(2):
            pick = (left_pick, right_pick)[side][slot]
            move_send[side, slot] = home[pick]
        copy = pltpu.make_async_remote_copy(
            src_ref=move_send.at[side],
            dst_ref=move_recv.at[side ^ 1],
            send_sem=move_ssem.at[side],
            recv_sem=move_rsem.at[side ^ 1],
            device_id=partner[side],
            device_id_type=MESH,
        )
        copy.start()
        copies.append(copy)

    c2 = coarse_end(3, own, c0, partial)
    c2 = jnp.where(is_switched, c2, 0.0)
    turned[...] = jnp.transpose(jnp.concatenate([c2, pltpu.roll(c2, LANES - 1, 1)], axis=0))
    for pair in range(4):
        out3_v[:, pair * 128 : pair * 128 + 128] = turned[pl.ds(2 * pair, ELEMS, stride=FIELDS), :]
    store3 = pltpu.make_async_copy(out3_v, out3_h, store_sem.at[0])
    store3.start()

    from_left = jnp.minimum(count_recv[0][0, 0], 2)
    from_right = jnp.minimum(count_recv[1][0, 0], 2)
    is_first, is_last = pos == 0, pos == pieces - 1
    at_left = jnp.where(is_first, home_count + from_right, jnp.where(is_last, from_right, 0))
    at_home = jnp.where(is_first, 0, jnp.where(is_last, from_right + from_left, from_left))
    at_right = jnp.where(is_first, home_count, jnp.where(is_last, 0, from_left + home_count))
    picks = []
    for slot in range(HOLD7):
        rank = slot - at_home
        stay = (rank >= 0) & (rank < home_count)
        value = home[home_list[jnp.clip(rank, 0, HOLD7 - 1)]]
        out7_v[slot] = jnp.where(stay, value, 0.0)
        rank_left, rank_right = slot - at_left, slot - at_right
        is_left = (rank_left >= 0) & (rank_left < from_left)
        is_right = (rank_right >= 0) & (rank_right < from_right)
        pick = jnp.where(is_left, rank_left, jnp.where(is_right, 2 + rank_right, 0))
        picks.append((is_left | is_right, pick))
    for copy in copies:
        copy.wait()
    for slot in range(HOLD7):
        arrived, pick = picks[slot]
        value = move_recv[pick // 2, pick % 2]
        out7_v[slot] = jnp.where(arrived, value, out7_v[slot])
    store7 = pltpu.make_async_copy(out7_v, out7_h, store_sem.at[1])
    store7.start()
    store3.wait()
    store7.wait()


def solution(mesh):
    slabs, pieces = mesh.shape["slab"], mesh.shape["curve"]
    tables = make_tables()

    def per_device(state, velocity, pre_exp, stoich, neighbours, switch, new_owner):
        velocity = jnp.transpose(velocity, (0, 2, 1))
        neighbours = jnp.transpose(neighbours)
        operands = (state, velocity, neighbours, pre_exp, stoich, switch, new_owner) + tuple(
            jnp.asarray(table) for table in tables
        )
        vm, sm, dma = pltpu.VMEM, pltpu.SMEM, pltpu.SemaphoreType.DMA
        nodes = (512, LANES)
        return pl.pallas_call(
            functools.partial(kernel, slabs, pieces),
            out_shape=(
                jax.ShapeDtypeStruct((HOLD7, FIELDS, 512), F32),
                jax.ShapeDtypeStruct((ELEMS, 512), F32),
            ),
            in_specs=[pl.BlockSpec(memory_space=pltpu.HBM)] * len(operands),
            out_specs=[pl.BlockSpec(memory_space=pltpu.HBM)] * 2,
            scratch_shapes=[
                vm((ELEMS, FIELDS, 512), F32),
                vm((3, ELEMS, 64), BF16),
                vm((6, ELEMS), jnp.int32),
                sm((ELEMS,), F32),
                sm((FIELDS,), F32),
                sm((ELEMS,), jnp.int32),
                sm((ELEMS,), jnp.int32),
            ]
            + [vm(table.shape, BF16) for table in tables]
            + [
                vm(nodes, F32),
                vm(nodes, F32),
                vm(nodes, F32),
                vm(nodes, F32),
                vm((3, 512, LANES), F32),
                vm((6, 64, LANES), F32),
                vm((192, LANES), F32),
                vm((384, LANES), F32),
                vm((2, LANES, 2 * LANES), BF16),
                vm((4, LANES, LANES), BF16),
                vm((4, 64, LANES), F32),
                vm((4, 4, 64, LANES), BF16),
                vm((4, 4, 64, LANES), BF16),
                vm((2, 8, LANES), jnp.int32),
                vm((2, 8, LANES), jnp.int32),
                vm((ELEMS, FIELDS, 512), F32),
                vm((2, 2, FIELDS, 512), F32),
                vm((2, 2, FIELDS, 512), F32),
                vm((HOLD7, FIELDS, 512), F32),
                vm((ELEMS, 512), F32),
                vm((LANES, LANES), F32),
                sm((HOLD7,), jnp.int32),
                dma((13,)),
                dma((4, 4)),
                dma((4, 4)),
                dma((2,)),
                dma((2,)),
                dma((2,)),
                dma((2,)),
                dma((2,)),
            ],
            compiler_params=pltpu.CompilerParams(
                collective_id=0, has_side_effects=True, vmem_limit_bytes=63 * 2**20
            ),
        )(*operands)

    return jax.shard_map(
        per_device,
        mesh=mesh,
        in_specs=(
            P(("slab", "curve"), None, None),
            P(None, None, ("slab", "curve")),
            P(("slab", "curve")),
            P(),
            P(("slab", "curve"), None),
            P(("slab", "curve")),
            P(("slab", "curve")),
        ),
        out_specs=(P(("slab", "curve"), None, None), P(("slab", "curve"), None)),
        check_vma=False,
    )
```

```python
import functools

import jax
import jax.numpy as jnp
import ml_dtypes
import numpy as np
from jax import lax
from jax.experimental import pallas as pl
from jax.experimental.pallas import tpu as pltpu
from jax.sharding import PartitionSpec as P

P7 = 8
P3 = 4
ELEMS = 16
FIELDS = 8
LANES = ELEMS * FIELDS
HOLD7 = 12
STEP = 0.002
ACTIVATION = 1.5
MESH = pl.DeviceIdType.MESH
F32 = jnp.float32
BF16 = jnp.bfloat16


def lobatto_points(number):
    return -np.cos(np.pi * np.arange(number) / (number - 1))


def derivative_matrix(points):
    number = points.shape[0]
    weights = np.ones(number)
    for row in range(number):
        for col in range(number):
            if col != row:
                weights[row] = weights[row] / (points[row] - points[col])
    matrix = np.zeros((number, number))
    for row in range(number):
        for col in range(number):
            if col != row:
                matrix[row, col] = weights[col] / weights[row] / (points[row] - points[col])
        matrix[row, row] = -np.sum(matrix[row])
    return matrix


def interpolation_matrix(source, target):
    matrix = np.ones((target.shape[0], source.shape[0]))
    for col in range(source.shape[0]):
        for other in range(source.shape[0]):
            if other != col:
                matrix[:, col] = (
                    matrix[:, col] * (target - source[other]) / (source[col] - source[other])
                )
    return matrix


def kron3(a, b, c):
    return np.kron(a, np.kron(b, c))


def to_bf16(matrix):
    return np.asarray(matrix, np.float32).astype(ml_dtypes.bfloat16)


def split_columns(matrix):
    full = np.asarray(matrix, np.float32)
    high = full.astype(ml_dtypes.bfloat16)
    low = (full - high.astype(np.float32)).astype(ml_dtypes.bfloat16)
    return np.concatenate([high, low, high], axis=1)


def face_selectors(extent):
    ident = np.eye(extent)
    first, last = ident[:1], ident[-1:]
    picks = []
    for end in (first, last):
        picks.append(kron3(end, ident, ident))
    for end in (first, last):
        picks.append(kron3(ident, end, ident))
    for end in (first, last):
        picks.append(kron3(ident, ident, end))
    return np.stack(picks)


def make_tables():
    r7, r3 = lobatto_points(P7), lobatto_points(P3)
    d7, d3 = derivative_matrix(r7), derivative_matrix(r3)
    down = interpolation_matrix(r7, r3)
    up = interpolation_matrix(r3, r7)
    i7, i3 = np.eye(P7), np.eye(P3)
    div_i = np.kron(d7, np.eye(32))
    two = np.eye(2)
    div_jk = np.concatenate([np.kron(two, np.kron(d7, i7)), np.kron(two, np.kron(i7, d7))], axis=1)
    fine = to_bf16(np.concatenate([div_i, div_jk], axis=0))
    lift = to_bf16(kron3(up, up, up))
    project = split_columns(kron3(down, down, down))
    mortar_up = np.asarray(np.kron(up, up), np.float32).astype(np.float64)
    mortar_down = np.asarray(np.kron(down, down), np.float32).astype(np.float64)
    selectors = face_selectors(P3)
    raise_all = np.concatenate([mortar_up @ selectors[side] for side in range(6)], axis=0)
    lower_all = np.concatenate([selectors[side].T @ mortar_down for side in range(6)], axis=1)
    lower_all = STEP * (P3 * (P3 - 1) / 2.0) * lower_all
    raise_faces = split_columns(raise_all)
    lower_faces = split_columns(lower_all)
    project_all = np.asarray(kron3(down, down, down), np.float32).astype(np.float64)
    project_x = np.concatenate([project_all[:, :64], project_all[:, 448:]], axis=1)
    late_fine = split_columns(np.concatenate([raise_all @ project_x, project_x], axis=0))
    lower_x = lower_all[:, :128]
    late_coarse = split_columns(np.concatenate([raise_all @ lower_x, lower_x], axis=0))
    coarse = to_bf16(
        np.concatenate([kron3(d3, i3, i3), kron3(i3, d3, i3), kron3(i3, i3, d3)], axis=1)
    )
    return fine, lift, project, raise_faces, lower_faces, coarse, late_fine, late_coarse


def dot(a, b):
    return jnp.dot(a, b, preferred_element_type=F32)


def split_rows(value):
    high = value.astype(BF16)
    low = (value - high.astype(F32)).astype(BF16)
    return jnp.concatenate([high, high, low], axis=0)


def face_slices(side):
    dim, end = side // 2, side % 2
    if dim == 0:
        return [pl.ds(448 * end, 64)]
    if dim == 1:
        return [pl.ds(i * 64 + 56 * end, 8) for i in range(P7)]
    return [pl.ds(7 * end, 64, stride=8)]


def face_get(ref, side):
    parts = [ref[where, :] for where in face_slices(side)]
    return parts[0] if len(parts) == 1 else jnp.concatenate(parts, axis=0)


def face_add(ref, side, value):
    start = 0
    for where in face_slices(side):
        ref[where, :] += value[start : start + where.size]
        start += where.size


def kernel(
    slabs,
    pieces,
    state_h,
    vel_h,
    nbr_h,
    pre_h,
    stoich_h,
    switch_h,
    owner_h,
    fine_h,
    lift_h,
    project_h,
    raise_h,
    lower_h,
    coarse_h,
    late_fine_h,
    late_coarse_h,
    out7_v,
    out3_v,
    state_v,
    vel_v,
    nbr_v,
    pre_s,
    stoich_s,
    switch_s,
    owner_s,
    fine_v,
    lift_v,
    project_v,
    raise_v,
    lower_v,
    coarse_v,
    late_fine_v,
    late_coarse_v,
    u0,
    u1,
    u2,
    u3,
    speed,
    coef,
    vel_rep,
    vmin,
    perm_far,
    perm_near,
    local_nb,
    send,
    recv,
    count_send,
    count_recv,
    home,
    move_send,
    move_recv,
    early_send,
    early_recv,
    extra_recv,
    move_coef,
    turned,
    home_list,
    load_sem,
    send_sem,
    recv_sem,
    count_ssem,
    count_rsem,
    move_ssem,
    move_rsem,
    early_ssem,
    early_rsem,
    extra_ssem,
    extra_rsem,
):
    slab, pos = lax.axis_index("slab"), lax.axis_index("curve")
    left, right = lax.rem(pos + pieces - 1, pieces), lax.rem(pos + 1, pieces)
    below, above = lax.rem(slab + slabs - 1, slabs), lax.rem(slab + 1, slabs)
    partner = {0: (slab, left), 1: (slab, right), 4: (below, pos), 5: (above, pos)}

    barrier = pltpu.get_barrier_semaphore()
    for side in (0, 1, 4, 5):
        pl.semaphore_signal(barrier, inc=1, device_id=partner[side], device_id_type=MESH)

    pairs = [
        (state_h, state_v),
        (vel_h, vel_v),
        (nbr_h, nbr_v),
        (lift_h, lift_v),
        (pre_h, pre_s),
        (stoich_h, stoich_s),
        (switch_h, switch_s),
        (owner_h, owner_s),
        (fine_h, fine_v),
        (raise_h, raise_v),
        (project_h, project_v),
        (lower_h, lower_v),
        (coarse_h, coarse_v),
        (late_fine_h, late_fine_v),
        (late_coarse_h, late_coarse_v),
    ]
    loads = [
        pltpu.make_async_copy(source, target, load_sem.at[number])
        for number, (source, target) in enumerate(pairs)
    ]
    for load in loads:
        load.start()

    lane_row = lax.broadcasted_iota(jnp.int32, (1, LANES), 1)
    lane_elem = lane_row // FIELDS
    lane_field = lane_row % FIELDS
    lanes = lax.broadcasted_iota(jnp.int32, (LANES, LANES), 1)
    rows = lax.broadcasted_iota(jnp.int32, (LANES, LANES), 0)
    spread = (
        lax.broadcasted_iota(jnp.int32, (ELEMS, LANES), 0)
        == lax.broadcasted_iota(jnp.int32, (ELEMS, LANES), 1) // FIELDS
    ).astype(F32)
    rep = ((rows % FIELDS == 0) & (rows // FIELDS == lanes // FIELDS)).astype(F32).astype(BF16)
    rep2 = jnp.concatenate([rep, rep], axis=0)

    loads[0].wait()
    u0[...] = jnp.transpose(state_v[...].reshape(LANES, 512))

    loads[2].wait()
    ids = nbr_v[...]
    me = slab * pieces + pos
    here = lax.shift_right_logical(ids, 4) == me
    code = jnp.where(here, ids & 15, (ids & 15) + 16).astype(F32)
    spread_t = (
        lax.broadcasted_iota(jnp.int32, (LANES, ELEMS), 1)
        == lax.broadcasted_iota(jnp.int32, (LANES, ELEMS), 0) // FIELDS
    ).astype(F32)
    target = lax.dot_general(
        spread_t.astype(BF16),
        code.astype(BF16),
        (((1,), (1,)), ((), ())),
        preferred_element_type=F32,
    )
    target = target.astype(jnp.int32) * FIELDS
    target = target + lax.broadcasted_iota(jnp.int32, (LANES, 6), 0) % FIELDS
    for side in range(6):
        column = target[:, side : side + 1]
        near = (column == lanes).astype(F32).astype(BF16)
        far = (column == lanes + LANES).astype(F32).astype(BF16)
        if side < 2:
            perm_far[side] = far
            perm_near[side] = near
        elif side < 4:
            perm_near[side] = near
        else:
            perm_far[side - 2] = far

    def launch(number, side, trace):
        slot = side if side < 2 else side - 2
        send[number, slot] = dot(trace, perm_far[slot]).astype(BF16)
        copy = pltpu.make_async_remote_copy(
            src_ref=send.at[number, slot],
            dst_ref=recv.at[number, slot ^ 1],
            send_sem=send_sem.at[number, slot],
            recv_sem=recv_sem.at[number, slot ^ 1],
            device_id=partner[side],
            device_id_type=MESH,
        )
        copy.start()
        started.append(copy)
        arrivals[number, side ^ 1] = copy

    def gather_local(traces):
        for side in range(4):
            local_nb[side ^ 1] = dot(traces[side], perm_near[side])

    started, arrivals = [], {}

    def fine_trace(ref, side):
        return face_get(ref, side).astype(BF16)

    traces = [fine_trace(u0, side) for side in range(6)]
    pl.semaphore_wait(barrier, 4)
    for side in (0, 1, 4, 5):
        launch(0, side, traces[side])
    gather_local(traces)

    loads[6].wait()
    loads[7].wait()
    left_count = right_count = home_count = jnp.int32(0)
    left_pick = [jnp.int32(0)] * 2
    right_pick = [jnp.int32(0)] * 2
    home_pick = [jnp.int32(0)] * HOLD7
    switch_row = jnp.zeros((1, LANES), F32)
    for elem in range(ELEMS):
        switched = switch_s[elem]
        owner = owner_s[elem]
        switch_row = jnp.where(lane_elem == elem, switched.astype(F32), switch_row)
        fine_one = switched != 1
        goes_left = fine_one & (owner == left)
        goes_right = fine_one & (owner == right)
        stays = fine_one & jnp.logical_not(owner == left) & jnp.logical_not(owner == right)
        for slot in range(2):
            left_pick[slot] = jnp.where(goes_left & (left_count == slot), elem, left_pick[slot])
            right_pick[slot] = jnp.where(goes_right & (right_count == slot), elem, right_pick[slot])
        for slot in range(min(elem + 1, HOLD7)):
            home_pick[slot] = jnp.where(stays & (home_count == slot), elem, home_pick[slot])
        left_count = left_count + goes_left.astype(jnp.int32)
        right_count = right_count + goes_right.astype(jnp.int32)
        home_count = home_count + stays.astype(jnp.int32)
    for slot in range(HOLD7):
        home_list[slot] = home_pick[slot]
    count_arrivals = []
    count_send[0] = jnp.full((8, LANES), left_count, jnp.int32)
    count_send[1] = jnp.full((8, LANES), right_count, jnp.int32)
    for side in (0, 1):
        copy = pltpu.make_async_remote_copy(
            src_ref=count_send.at[side],
            dst_ref=count_recv.at[side ^ 1],
            send_sem=count_ssem.at[side],
            recv_sem=count_rsem.at[side ^ 1],
            device_id=partner[side],
            device_id_type=MESH,
        )
        copy.start()
        started.append(copy)
        count_arrivals.append(copy)
    is_switched = switch_row > 0.5

    loads[1].wait()
    loads[3].wait()
    loads[9].wait()
    for dim in range(3):
        spread_vel = lax.dot_general(
            vel_v[dim],
            spread.astype(BF16),
            (((0,), (0,)), ((), ())),
            preferred_element_type=F32,
        ).astype(BF16)
        vel_rep[dim * 64 : dim * 64 + 64] = spread_vel.astype(F32)
        speed[dim] = dot(lift_v[...], spread_vel).astype(BF16).astype(F32)
        mortar = dot(raise_v[dim * 128 : dim * 128 + 128, :128], jnp.concatenate([spread_vel, spread_vel], axis=0))
        vmin[dim * 128 : dim * 128 + 64] = jnp.minimum(-mortar[:64], 0.0)
        vmin[dim * 128 + 64 : dim * 128 + 128] = jnp.minimum(mortar[64:], 0.0)
        for end in range(2):
            side = 2 * dim + end
            normal = face_get(speed.at[dim], side)
            lift_coef = STEP * (P7 * (P7 - 1) / 2.0)
            coef[side] = lift_coef * jnp.minimum(normal if end else -normal, 0.0)

    for side, picks, count in ((0, left_pick, left_count), (1, right_pick, right_count)):
        chosen = jnp.zeros((LANES, LANES), F32)
        for slot in range(2):
            place = lanes // FIELDS == 2 * (1 - side) + slot
            source_row = rows - (lanes % FIELDS) == picks[slot] * FIELDS
            chosen = jnp.where(place & source_row & (count > slot), 1.0, chosen)
        chosen = chosen.astype(BF16)
        early_send[side, :LANES] = chosen
        normals = jnp.concatenate(
            [face_get(speed.at[other // 2], other).astype(BF16) for other in (0, 1, 4, 5)], axis=0
        )
        early_send[side, LANES:] = dot(normals, chosen).astype(BF16)
        copy = pltpu.make_async_remote_copy(
            src_ref=early_send.at[side],
            dst_ref=early_recv.at[side ^ 1],
            send_sem=early_ssem.at[side],
            recv_sem=early_rsem.at[side ^ 1],
            device_id=partner[side],
            device_id_type=MESH,
        )
        copy.start()
        started.append(copy)
        count_arrivals.append(copy)

    loads[4].wait()
    loads[5].wait()
    pre_row = jnp.zeros((1, LANES), F32)
    stoich_row = jnp.zeros((1, LANES), F32)
    for elem in range(ELEMS):
        pre_row = jnp.where(lane_elem == elem, pre_s[elem], pre_row)
    for field in range(FIELDS):
        stoich_row = jnp.where(lane_field == field, stoich_s[field], stoich_row)

    def source(u):
        rate = (
            pre_row
            * jnp.exp(-ACTIVATION * jnp.exp(-u))
            * pltpu.roll(u, LANES - 1, 1)
            * pltpu.roll(u, LANES - 2, 1)
        )
        high = rate.astype(BF16)
        low = (rate - high.astype(F32)).astype(BF16)
        return stoich_row * dot(jnp.concatenate([high, low], axis=1), rep2)

    for number in range(8, 15):
        if number != 9:
            loads[number].wait()

    def fine_start(ref, start, out, traces):
        scale = 1.0 if start is None else 0.5
        along_i = []
        for half in range(2):
            parts = []
            for i in range(P7):
                at = pl.ds(i * 64 + half * 32, 32)
                parts.append((speed[0, at, :] * ref[at, :]).astype(BF16))
            along_i.append(dot(fine_v[:256, :], jnp.concatenate(parts, axis=0)))
        for block in range(4):
            at = pl.ds(block * 128, 128)
            u = ref[at, :]
            flux = jnp.concatenate(
                [(speed[1, at, :] * u).astype(BF16), (speed[2, at, :] * u).astype(BF16)], axis=0
            )
            div = dot(fine_v[256:, :], flux) + jnp.concatenate(
                [
                    along_i[half][i * 32 : i * 32 + 32]
                    for i in (2 * block, 2 * block + 1)
                    for half in range(2)
                ],
                axis=0,
            )
            rate = STEP * (source(u) - div)
            out[at, :] = u + rate if start is None else 0.5 * (start[at, :] + u + rate)
        for side in range(6):
            jump = traces[side].astype(F32)
            if side < 4:
                jump = jump - local_nb[side]
            face_add(out, side, scale * (coef[side] * jump))

    def late_term(number, side, scale):
        slot = side if side < 2 else side - 2
        arrivals[number, side].wait_recv()
        return scale * (coef[side] * recv[number, slot].astype(F32))

    def fine_end_z(number, scale, out):
        for side in (4, 5):
            face_add(out, side, -late_term(number, side, scale))

    def fine_end_x(number, scale, out):
        terms = [late_term(number, side, scale) for side in (0, 1)]
        for side in (0, 1):
            face_add(out, side, -terms[side])
        return jnp.concatenate(terms, axis=0)

    def coarse_start(c, start):
        flux = jnp.concatenate(
            [(vel_rep[dim * 64 : dim * 64 + 64] * c).astype(BF16) for dim in range(3)], axis=0
        )
        rate = STEP * (source(c) - dot(coarse_v[...], flux))
        return c + rate if start is None else 0.5 * (start + c + rate)

    def coarse_end_z(number, own, scale, partial):
        jumps = []
        for side in range(6):
            near = local_nb[side] if side < 4 else recv[number, side - 2].astype(F32)
            mine = own[side * 64 : side * 64 + 64].astype(F32)
            jumps.append(vmin[side * 64 : side * 64 + 64] * (mine - near))
        return partial + scale * dot(lower_v[...], split_rows(jnp.concatenate(jumps, axis=0)))

    def coarse_jump_x(number):
        return split_rows(
            jnp.concatenate(
                [vmin[side * 64 : side * 64 + 64] * recv[number, side].astype(F32) for side in (0, 1)],
                axis=0,
            )
        )

    def launch_mixed(number, fine, raised_base, table, late):
        own, traces = [None] * 6, [None] * 6
        for sides in ((0, 1), (4, 5), (2, 3)):
            at = slice(sides[0] * 64, sides[0] * 64 + 128)
            raised = raised_base[at] - dot(table[at, :], late)
            for place, side in enumerate(sides):
                own[side] = raised[place * 64 : place * 64 + 64]
                traces[side] = fine_trace(fine, side)
                mixed = jnp.where(is_switched, own[side], traces[side].astype(F32)).astype(BF16)
                if side in (2, 3):
                    mixes[side] = mixed
                else:
                    launch(number, side, mixed)
                    mixes[side] = mixed
        return traces, jnp.concatenate(own, axis=0).astype(BF16)

    mixes = [None] * 6

    fine_start(u0, None, u1, traces)
    fine_end_z(0, 1.0, u1)
    fine_end_x(0, 1.0, u1)
    traces = [None] * 6
    for side in (0, 1, 4, 5):
        traces[side] = fine_trace(u1, side)
        launch(1, side, traces[side])
    for side in (2, 3):
        traces[side] = fine_trace(u1, side)
    gather_local(traces)
    fine_start(u1, u0, u2, traces)
    fine_end_z(1, 0.5, u2)
    c0 = dot(project_v[...], split_rows(u2[...]))
    raised = dot(raise_v[...], split_rows(c0))
    late = split_rows(fine_end_x(1, 0.5, u2))

    traces, own = launch_mixed(2, u2, raised, late_fine_v, late)
    gather_local(mixes)
    c0 = c0 - dot(late_fine_v[384:, :], late)
    fine_start(u2, None, u3, traces)
    partial = coarse_start(c0, None)
    for copy in count_arrivals:
        copy.wait_recv()
    for place, side in enumerate((0, 1, 4, 5)):
        at = pl.ds(LANES + 64 * place, 64)
        normal = early_recv[0, at, :].astype(F32) + early_recv[1, at, :].astype(F32)
        lift_coef = 0.5 * STEP * (P7 * (P7 - 1) / 2.0)
        move_coef[place] = lift_coef * jnp.minimum(normal if side % 2 else -normal, 0.0)
    fine_end_z(2, 1.0, u3)
    c1 = coarse_end_z(2, own, 1.0, partial)
    raised = dot(raise_v[...], split_rows(c1))
    fine_end_x(2, 1.0, u3)
    late = coarse_jump_x(2)
    traces, own = launch_mixed(3, u3, raised, late_coarse_v, late)

    left2, right2 = lax.rem(pos + pieces - 2, pieces), lax.rem(pos + 2, pieces)
    extras = {
        (1, 1): (2, (below, right)),
        (1, 2): (3, (above, right)),
        (0, 1): (2, (below, left)),
        (0, 2): (3, (above, left)),
        (0, 0): (0, (slab, left2)),
        (1, 0): (1, (slab, right2)),
    }
    extra_copies = []
    for (toward, kind), (slot, device) in extras.items():
        place = 3 - kind if kind else 0
        copy = pltpu.make_async_remote_copy(
            src_ref=send.at[3, slot],
            dst_ref=extra_recv.at[1 - toward, place],
            send_sem=extra_ssem.at[toward, kind],
            recv_sem=extra_rsem.at[1 - toward, place],
            device_id=device,
            device_id_type=MESH,
        )
        copy.start()
        started.append(copy)
        extra_copies.append(copy)
    gather_local(mixes)
    c1 = c1 - dot(late_coarse_v[384:, :], late)
    fine_start(u3, u2, u1, traces)

    def turn_home():
        for number in range(4):
            home[:, :, number * 128 : number * 128 + 128] = jnp.transpose(
                u1[number * 128 : number * 128 + 128, :]
            ).reshape(ELEMS, FIELDS, 128)

    turn_home()
    for side in range(2):
        for slot in range(2):
            pick = (left_pick, right_pick)[side][slot]
            move_send[side, slot] = home[pick]
        copy = pltpu.make_async_remote_copy(
            src_ref=move_send.at[side],
            dst_ref=move_recv.at[side ^ 1],
            send_sem=move_ssem.at[side],
            recv_sem=move_rsem.at[side ^ 1],
            device_id=partner[side],
            device_id_type=MESH,
        )
        copy.start()
        started.append(copy)
        extra_copies.append(copy)
    partial = coarse_start(c1, c0)
    u3[...] = jnp.zeros_like(u3)
    fine_end_z(3, 0.5, u1)
    c2 = coarse_end_z(3, own, 0.5, partial)
    fine_end_x(3, 0.5, u1)
    c2 = c2 - 0.5 * dot(late_coarse_v[384:, :], coarse_jump_x(3))

    c2 = jnp.where(is_switched, c2, 0.0)
    turned[...] = jnp.transpose(jnp.concatenate([c2, pltpu.roll(c2, LANES - 1, 1)], axis=0))
    for pair in range(4):
        out3_v[:, pair * 128 : pair * 128 + 128] = turned[pl.ds(2 * pair, ELEMS, stride=FIELDS), :]
    turn_home()

    from_left = jnp.minimum(count_recv[0][0, 0], 2)
    from_right = jnp.minimum(count_recv[1][0, 0], 2)
    is_first, is_last = pos == 0, pos == pieces - 1
    at_left = jnp.where(is_first, home_count + from_right, jnp.where(is_last, from_right, 0))
    at_home = jnp.where(is_first, 0, jnp.where(is_last, from_right + from_left, from_left))
    at_right = jnp.where(is_first, home_count, jnp.where(is_last, 0, from_left + home_count))
    picks = []
    for slot in range(HOLD7):
        rank = slot - at_home
        stay = (rank >= 0) & (rank < home_count)
        value = home[home_list[jnp.clip(rank, 0, HOLD7 - 1)]]
        out7_v[slot] = jnp.where(stay, value, 0.0)
        rank_left, rank_right = slot - at_left, slot - at_right
        is_left = (rank_left >= 0) & (rank_left < from_left)
        is_right = (rank_right >= 0) & (rank_right < from_right)
        pick = jnp.where(is_left, rank_left, jnp.where(is_right, 2 + rank_right, 0))
        picks.append((is_left | is_right, pick))
    for copy in extra_copies:
        copy.wait_recv()
    chosen = jnp.concatenate([early_recv[0, :LANES, :], early_recv[1, :LANES, :]], axis=0)
    nears = {
        0: (extra_recv[0, 0], send[3, 1]),
        1: (send[3, 0], extra_recv[1, 0]),
        4: (extra_recv[0, 1], extra_recv[1, 1]),
        5: (extra_recv[0, 2], extra_recv[1, 2]),
    }
    for place, side in enumerate((0, 1, 4, 5)):
        near = dot(jnp.concatenate(nears[side], axis=1), chosen)
        face_add(u3, side, -(move_coef[place] * near))
    for number in range(4):
        moved = jnp.transpose(u3[number * 128 : number * 128 + 128, :])
        at = pl.ds(number * 128, 128)
        for pick in range(4):
            move_recv[pick // 2, pick % 2, :, at] += moved[pick * FIELDS : pick * FIELDS + FIELDS]
    for slot in range(HOLD7):
        arrived, pick = picks[slot]
        value = move_recv[pick // 2, pick % 2]
        out7_v[slot] = jnp.where(arrived, value, out7_v[slot])
    for copy in started:
        copy.wait_send()


def solution(mesh):
    slabs, pieces = mesh.shape["slab"], mesh.shape["curve"]
    tables = make_tables()

    def per_device(state, velocity, pre_exp, stoich, neighbours, switch, new_owner):
        velocity = jnp.transpose(velocity, (0, 2, 1))
        neighbours = jnp.transpose(neighbours)
        operands = (state, velocity, neighbours, pre_exp, stoich, switch, new_owner) + tuple(
            jnp.asarray(table) for table in tables
        )
        vm, sm, dma = pltpu.VMEM, pltpu.SMEM, pltpu.SemaphoreType.DMA
        nodes = (512, LANES)
        return pl.pallas_call(
            functools.partial(kernel, slabs, pieces),
            out_shape=(
                pltpu.VMEM((HOLD7, FIELDS, 512), F32),
                pltpu.VMEM((ELEMS, 512), F32),
            ),
            in_specs=[pl.BlockSpec(memory_space=pltpu.HBM)] * len(operands),
            out_specs=[pl.BlockSpec(memory_space=pltpu.VMEM)] * 2,
            scratch_shapes=[
                vm((ELEMS, FIELDS, 512), F32),
                vm((3, ELEMS, 64), BF16),
                vm((6, ELEMS), jnp.int32),
                sm((ELEMS,), F32),
                sm((FIELDS,), F32),
                sm((ELEMS,), jnp.int32),
                sm((ELEMS,), jnp.int32),
            ]
            + [vm(table.shape, BF16) for table in tables]
            + [
                vm(nodes, F32),
                vm(nodes, F32),
                vm(nodes, F32),
                vm(nodes, F32),
                vm((3, 512, LANES), F32),
                vm((6, 64, LANES), F32),
                vm((192, LANES), F32),
                vm((384, LANES), F32),
                vm((4, LANES, LANES), BF16),
                vm((4, LANES, LANES), BF16),
                vm((4, 64, LANES), F32),
                vm((4, 4, 64, LANES), BF16),
                vm((4, 4, 64, LANES), BF16),
                vm((2, 8, LANES), jnp.int32),
                vm((2, 8, LANES), jnp.int32),
                vm((ELEMS, FIELDS, 512), F32),
                vm((2, 2, FIELDS, 512), F32),
                vm((2, 2, FIELDS, 512), F32),
                vm((2, 3 * LANES, LANES), BF16),
                vm((2, 3 * LANES, LANES), BF16),
                vm((2, 3, 64, LANES), BF16),
                vm((4, 64, LANES), F32),
                vm((LANES, LANES), F32),
                sm((HOLD7,), jnp.int32),
                dma((15,)),
                dma((4, 4)),
                dma((4, 4)),
                dma((2,)),
                dma((2,)),
                dma((2,)),
                dma((2,)),
                dma((2,)),
                dma((2,)),
                dma((2, 3)),
                dma((2, 3)),
            ],
            compiler_params=pltpu.CompilerParams(
                collective_id=0, has_side_effects=True, vmem_limit_bytes=62 * 2**20
            ),
        )(*operands)

    return jax.shard_map(
        per_device,
        mesh=mesh,
        in_specs=(
            P(("slab", "curve"), None, None),
            P(None, None, ("slab", "curve")),
            P(("slab", "curve")),
            P(),
            P(("slab", "curve"), None),
            P(("slab", "curve")),
            P(("slab", "curve")),
        ),
        out_specs=(P(("slab", "curve"), None, None), P(("slab", "curve"), None)),
        check_vma=False,
    )
```

```python
import functools

import jax
import jax.numpy as jnp
import ml_dtypes
import numpy as np
from jax import lax
from jax.experimental import pallas as pl
from jax.experimental.pallas import tpu as pltpu
from jax.sharding import PartitionSpec as P

P7 = 8
P3 = 4
ELEMS = 16
FIELDS = 8
LANES = ELEMS * FIELDS
HOLD7 = 12
STEP = 0.002
ACTIVATION = 1.5
MESH = pl.DeviceIdType.MESH
F32 = jnp.float32
BF16 = jnp.bfloat16


def lobatto_points(number):
    return -np.cos(np.pi * np.arange(number) / (number - 1))


def derivative_matrix(points):
    number = points.shape[0]
    weights = np.ones(number)
    for row in range(number):
        for col in range(number):
            if col != row:
                weights[row] = weights[row] / (points[row] - points[col])
    matrix = np.zeros((number, number))
    for row in range(number):
        for col in range(number):
            if col != row:
                matrix[row, col] = weights[col] / weights[row] / (points[row] - points[col])
        matrix[row, row] = -np.sum(matrix[row])
    return matrix


def interpolation_matrix(source, target):
    matrix = np.ones((target.shape[0], source.shape[0]))
    for col in range(source.shape[0]):
        for other in range(source.shape[0]):
            if other != col:
                matrix[:, col] = (
                    matrix[:, col] * (target - source[other]) / (source[col] - source[other])
                )
    return matrix


def kron3(a, b, c):
    return np.kron(a, np.kron(b, c))


def to_bf16(matrix):
    return np.asarray(matrix, np.float32).astype(ml_dtypes.bfloat16)


def split_columns(matrix):
    full = np.asarray(matrix, np.float32)
    high = full.astype(ml_dtypes.bfloat16)
    low = (full - high.astype(np.float32)).astype(ml_dtypes.bfloat16)
    return np.concatenate([high, low, high], axis=1)


def face_selectors(extent):
    ident = np.eye(extent)
    first, last = ident[:1], ident[-1:]
    picks = []
    for end in (first, last):
        picks.append(kron3(end, ident, ident))
    for end in (first, last):
        picks.append(kron3(ident, end, ident))
    for end in (first, last):
        picks.append(kron3(ident, ident, end))
    return np.stack(picks)


def make_tables():
    r7, r3 = lobatto_points(P7), lobatto_points(P3)
    d7, d3 = derivative_matrix(r7), derivative_matrix(r3)
    down = interpolation_matrix(r7, r3)
    up = interpolation_matrix(r3, r7)
    i7, i3 = np.eye(P7), np.eye(P3)
    div_i = np.kron(d7, np.eye(32))
    two = np.eye(2)
    div_jk = np.concatenate([np.kron(two, np.kron(d7, i7)), np.kron(two, np.kron(i7, d7))], axis=1)
    fine = to_bf16(np.concatenate([div_i, div_jk], axis=0))
    lift = to_bf16(kron3(up, up, up))
    project = split_columns(kron3(down, down, down))
    mortar_up = np.asarray(np.kron(up, up), np.float32).astype(np.float64)
    mortar_down = np.asarray(np.kron(down, down), np.float32).astype(np.float64)
    selectors = face_selectors(P3)
    raise_all = np.concatenate([mortar_up @ selectors[side] for side in range(6)], axis=0)
    lower_all = np.concatenate([selectors[side].T @ mortar_down for side in range(6)], axis=1)
    lower_all = STEP * (P3 * (P3 - 1) / 2.0) * lower_all
    raise_faces = split_columns(raise_all)
    lower_faces = split_columns(lower_all)
    project_all = np.asarray(kron3(down, down, down), np.float32).astype(np.float64)
    fine_selectors = face_selectors(P7)
    project_late = np.concatenate(
        [project_all @ fine_selectors[side].T for side in (0, 1, 4, 5)], axis=1
    )
    late_fine = split_columns(np.concatenate([raise_all @ project_late, project_late], axis=0))
    lower_x = lower_all[:, :128]
    late_coarse = split_columns(np.concatenate([raise_all @ lower_x, lower_x], axis=0))
    coarse = to_bf16(
        np.concatenate([kron3(d3, i3, i3), kron3(i3, d3, i3), kron3(i3, i3, d3)], axis=1)
    )
    return fine, lift, project, raise_faces, lower_faces, coarse, late_fine, late_coarse


def dot(a, b):
    return jnp.dot(a, b, preferred_element_type=F32)


def split_rows(value):
    high = value.astype(BF16)
    low = (value - high.astype(F32)).astype(BF16)
    return jnp.concatenate([high, high, low], axis=0)


def face_slices(side):
    dim, end = side // 2, side % 2
    if dim == 0:
        return [pl.ds(448 * end, 64)]
    if dim == 1:
        return [pl.ds(i * 64 + 56 * end, 8) for i in range(P7)]
    return [pl.ds(7 * end, 64, stride=8)]


def face_get(ref, side):
    parts = [ref[where, :] for where in face_slices(side)]
    return parts[0] if len(parts) == 1 else jnp.concatenate(parts, axis=0)


def face_add(ref, side, value):
    start = 0
    for where in face_slices(side):
        ref[where, :] += value[start : start + where.size]
        start += where.size


def edge_slice(x_end, z_end):
    return pl.ds(448 * x_end + 7 * z_end, P7, stride=8)


def kernel(
    slabs,
    pieces,
    state_h,
    vel_h,
    nbr_h,
    pre_h,
    stoich_h,
    switch_h,
    owner_h,
    fine_h,
    lift_h,
    project_h,
    raise_h,
    lower_h,
    coarse_h,
    late_fine_h,
    late_coarse_h,
    out7_v,
    out3_v,
    state_v,
    vel_v,
    nbr_v,
    pre_s,
    stoich_s,
    switch_s,
    owner_s,
    fine_v,
    lift_v,
    project_v,
    raise_v,
    lower_v,
    coarse_v,
    late_fine_v,
    late_coarse_v,
    u0,
    u1,
    u2,
    u3,
    speed,
    coef,
    vel_rep,
    vmin,
    perm_far,
    perm_near,
    local_nb,
    send,
    recv,
    count_send,
    count_recv,
    home,
    move_send,
    move_recv,
    early_send,
    early_recv,
    wide_send,
    wide_recv,
    far_trace,
    next_near,
    corner_send,
    corner_recv,
    extra_recv,
    move_coef,
    turned,
    home_list,
    load_sem,
    send_sem,
    recv_sem,
    count_ssem,
    count_rsem,
    move_ssem,
    move_rsem,
    early_ssem,
    early_rsem,
    extra_ssem,
    extra_rsem,
    wide_ssem,
    wide_rsem,
    corner_ssem,
    corner_rsem,
):
    slab, pos = lax.axis_index("slab"), lax.axis_index("curve")
    left, right = lax.rem(pos + pieces - 1, pieces), lax.rem(pos + 1, pieces)
    below, above = lax.rem(slab + slabs - 1, slabs), lax.rem(slab + 1, slabs)
    partner = {0: (slab, left), 1: (slab, right), 4: (below, pos), 5: (above, pos)}

    barrier = pltpu.get_barrier_semaphore()
    corners = [(below, left), (below, right), (above, left), (above, right)]
    for device in list(partner.values()) + corners:
        pl.semaphore_signal(barrier, inc=1, device_id=device, device_id_type=MESH)

    pairs = [
        (state_h, state_v),
        (vel_h, vel_v),
        (nbr_h, nbr_v),
        (lift_h, lift_v),
        (pre_h, pre_s),
        (stoich_h, stoich_s),
        (switch_h, switch_s),
        (owner_h, owner_s),
        (fine_h, fine_v),
        (raise_h, raise_v),
        (project_h, project_v),
        (lower_h, lower_v),
        (coarse_h, coarse_v),
        (late_fine_h, late_fine_v),
        (late_coarse_h, late_coarse_v),
    ]
    loads = [
        pltpu.make_async_copy(source, target, load_sem.at[number])
        for number, (source, target) in enumerate(pairs)
    ]
    for load in loads:
        load.start()

    lane_row = lax.broadcasted_iota(jnp.int32, (1, LANES), 1)
    lane_elem = lane_row // FIELDS
    lane_field = lane_row % FIELDS
    lanes = lax.broadcasted_iota(jnp.int32, (LANES, LANES), 1)
    rows = lax.broadcasted_iota(jnp.int32, (LANES, LANES), 0)
    spread = (
        lax.broadcasted_iota(jnp.int32, (ELEMS, LANES), 0)
        == lax.broadcasted_iota(jnp.int32, (ELEMS, LANES), 1) // FIELDS
    ).astype(F32)
    rep = ((rows % FIELDS == 0) & (rows // FIELDS == lanes // FIELDS)).astype(F32).astype(BF16)
    rep2 = jnp.concatenate([rep, rep], axis=0)

    loads[0].wait()
    u0[...] = jnp.transpose(state_v[...].reshape(LANES, 512))

    loads[2].wait()
    ids = nbr_v[...]
    me = slab * pieces + pos
    here = lax.shift_right_logical(ids, 4) == me
    code = jnp.where(here, ids & 15, (ids & 15) + 16).astype(F32)
    spread_t = (
        lax.broadcasted_iota(jnp.int32, (LANES, ELEMS), 1)
        == lax.broadcasted_iota(jnp.int32, (LANES, ELEMS), 0) // FIELDS
    ).astype(F32)
    target = lax.dot_general(
        spread_t.astype(BF16),
        code.astype(BF16),
        (((1,), (1,)), ((), ())),
        preferred_element_type=F32,
    )
    target = target.astype(jnp.int32) * FIELDS
    target = target + lax.broadcasted_iota(jnp.int32, (LANES, 6), 0) % FIELDS
    for side in range(6):
        column = target[:, side : side + 1]
        near = (column == lanes).astype(F32).astype(BF16)
        far = (column == lanes + LANES).astype(F32).astype(BF16)
        if side < 2:
            perm_far[side] = far
            perm_near[side] = near
        elif side < 4:
            perm_near[side] = near
        else:
            perm_far[side - 2] = far

    def launch(number, side, trace):
        slot = side if side < 2 else side - 2
        send[number, slot] = dot(trace, perm_far[slot]).astype(BF16)
        copy = pltpu.make_async_remote_copy(
            src_ref=send.at[number, slot],
            dst_ref=recv.at[number, slot ^ 1],
            send_sem=send_sem.at[number, slot],
            recv_sem=recv_sem.at[number, slot ^ 1],
            device_id=partner[side],
            device_id_type=MESH,
        )
        copy.start()
        started.append(copy)
        arrivals[number, side ^ 1] = copy

    def gather_local(traces):
        for side in range(4):
            local_nb[side ^ 1] = dot(traces[side], perm_near[side])

    started, arrivals = [], {}

    def fine_trace(ref, side):
        return face_get(ref, side).astype(BF16)

    traces = [fine_trace(u0, side) for side in range(6)]
    gather_local(traces)

    loads[1].wait()
    loads[3].wait()
    loads[9].wait()
    for dim in range(3):
        spread_vel = lax.dot_general(
            vel_v[dim],
            spread.astype(BF16),
            (((0,), (0,)), ((), ())),
            preferred_element_type=F32,
        ).astype(BF16)
        vel_rep[dim * 64 : dim * 64 + 64] = spread_vel.astype(F32)
        speed[dim] = dot(lift_v[...], spread_vel).astype(BF16).astype(F32)
        mortar = dot(raise_v[dim * 128 : dim * 128 + 128, :128], jnp.concatenate([spread_vel, spread_vel], axis=0))
        vmin[dim * 128 : dim * 128 + 64] = jnp.minimum(-mortar[:64], 0.0)
        vmin[dim * 128 + 64 : dim * 128 + 128] = jnp.minimum(mortar[64:], 0.0)
        for end in range(2):
            side = 2 * dim + end
            normal = face_get(speed.at[dim], side)
            lift_coef = STEP * (P7 * (P7 - 1) / 2.0)
            coef[side] = lift_coef * jnp.minimum(normal if end else -normal, 0.0)

    loads[4].wait()
    loads[5].wait()
    pre_row = jnp.zeros((1, LANES), F32)
    stoich_row = jnp.zeros((1, LANES), F32)
    for elem in range(ELEMS):
        pre_row = jnp.where(lane_elem == elem, pre_s[elem], pre_row)
    for field in range(FIELDS):
        stoich_row = jnp.where(lane_field == field, stoich_s[field], stoich_row)

    def source(u):
        rate = (
            pre_row
            * jnp.exp(-ACTIVATION * jnp.exp(-u))
            * pltpu.roll(u, LANES - 1, 1)
            * pltpu.roll(u, LANES - 2, 1)
        )
        high = rate.astype(BF16)
        low = (rate - high.astype(F32)).astype(BF16)
        return stoich_row * dot(jnp.concatenate([high, low], axis=1), rep2)

    for number in range(8, 15):
        if number != 9:
            loads[number].wait()

    def fine_start(ref, start, out, traces):
        scale = 1.0 if start is None else 0.5
        along_i = []
        for half in range(2):
            parts = []
            for i in range(P7):
                at = pl.ds(i * 64 + half * 32, 32)
                parts.append((speed[0, at, :] * ref[at, :]).astype(BF16))
            along_i.append(dot(fine_v[:256, :], jnp.concatenate(parts, axis=0)))
        for block in range(4):
            at = pl.ds(block * 128, 128)
            u = ref[at, :]
            flux = jnp.concatenate(
                [(speed[1, at, :] * u).astype(BF16), (speed[2, at, :] * u).astype(BF16)], axis=0
            )
            div = dot(fine_v[256:, :], flux) + jnp.concatenate(
                [
                    along_i[half][i * 32 : i * 32 + 32]
                    for i in (2 * block, 2 * block + 1)
                    for half in range(2)
                ],
                axis=0,
            )
            rate = STEP * (source(u) - div)
            out[at, :] = u + rate if start is None else 0.5 * (start[at, :] + u + rate)
        for side in range(6):
            jump = traces[side].astype(F32)
            if side < 4:
                jump = jump - local_nb[side]
            face_add(out, side, scale * (coef[side] * jump))

    def late_term(number, side, scale):
        slot = side if side < 2 else side - 2
        arrivals[number, side].wait_recv()
        return scale * (coef[side] * recv[number, slot].astype(F32))

    def fine_end_z(number, scale, out):
        for side in (4, 5):
            face_add(out, side, -late_term(number, side, scale))

    def fine_end_x(number, scale, out):
        terms = [late_term(number, side, scale) for side in (0, 1)]
        for side in (0, 1):
            face_add(out, side, -terms[side])
        return jnp.concatenate(terms, axis=0)

    def coarse_start(c, start):
        flux = jnp.concatenate(
            [(vel_rep[dim * 64 : dim * 64 + 64] * c).astype(BF16) for dim in range(3)], axis=0
        )
        rate = STEP * (source(c) - dot(coarse_v[...], flux))
        return c + rate if start is None else 0.5 * (start + c + rate)

    def coarse_end_z(number, own, scale, partial):
        jumps = []
        for side in range(6):
            near = local_nb[side] if side < 4 else recv[number, side - 2].astype(F32)
            mine = own[side * 64 : side * 64 + 64].astype(F32)
            jumps.append(vmin[side * 64 : side * 64 + 64] * (mine - near))
        return partial + scale * dot(lower_v[...], split_rows(jnp.concatenate(jumps, axis=0)))

    def coarse_jump_x(number):
        return split_rows(
            jnp.concatenate(
                [vmin[side * 64 : side * 64 + 64] * recv[number, side].astype(F32) for side in (0, 1)],
                axis=0,
            )
        )

    def launch_mixed(number, fine, raised_base, table, late):
        own, traces = [None] * 6, [None] * 6
        for sides in ((0, 1), (4, 5), (2, 3)):
            at = slice(sides[0] * 64, sides[0] * 64 + 128)
            raised = raised_base[at] - dot(table[at, :], late)
            for place, side in enumerate(sides):
                own[side] = raised[place * 64 : place * 64 + 64]
                traces[side] = fine_trace(fine, side)
                mixed = jnp.where(is_switched, own[side], traces[side].astype(F32)).astype(BF16)
                if side in (2, 3):
                    mixes[side] = mixed
                else:
                    launch(number, side, mixed)
                    mixes[side] = mixed
        return traces, jnp.concatenate(own, axis=0).astype(BF16)

    mixes = [None] * 6

    fine_start(u0, None, u1, traces)
    for side in (0, 1, 4, 5):
        slot, dim, end = side if side < 2 else side - 2, side // 2, side % 2
        edges = [(end, 0), (end, 1)] if dim == 0 else [(0, end), (1, end)]
        first = face_get(u1, side)
        high = first.astype(BF16)
        packed = [
            traces[side],
            face_get(speed.at[dim], side).astype(BF16),
            jnp.concatenate([speed[2 - dim, edge_slice(*edge), :] for edge in edges], axis=0).astype(BF16),
            high,
            (first - high.astype(F32)).astype(BF16),
        ]
        placed = dot(jnp.concatenate(packed, axis=0), perm_far[slot])
        wide_send[slot] = placed.astype(BF16)
        far_trace[slot] = placed[:64]
    for number, corner in enumerate(corners):
        z_end, x_end = number // 2, number % 2
        corner_send[number] = jnp.concatenate(
            [
                far_trace[x_end, pl.ds(7 * z_end, P7, stride=8), :],
                far_trace[2 + z_end, pl.ds(56 * x_end, P7), :],
            ],
            axis=0,
        ).astype(BF16)
    pl.semaphore_wait(barrier, 8)
    for number, corner in enumerate(corners):
        copy = pltpu.make_async_remote_copy(
            src_ref=corner_send.at[number],
            dst_ref=corner_recv.at[3 - number],
            send_sem=corner_ssem.at[number],
            recv_sem=corner_rsem.at[3 - number],
            device_id=corner,
            device_id_type=MESH,
        )
        copy.start()
        started.append(copy)
        arrivals["corner", 3 - number] = copy
    for part, (start_row, count) in enumerate(((0, 144), (144, 128))):
        for side in (0, 1, 4, 5):
            slot = side if side < 2 else side - 2
            at = pl.ds(start_row, count)
            copy = pltpu.make_async_remote_copy(
                src_ref=wide_send.at[slot, at],
                dst_ref=wide_recv.at[slot ^ 1, at],
                send_sem=wide_ssem.at[part, slot],
                recv_sem=wide_rsem.at[part, slot ^ 1],
                device_id=partner[side],
                device_id_type=MESH,
            )
            copy.start()
            started.append(copy)
            arrivals["wide", part, side ^ 1] = copy

    loads[6].wait()
    loads[7].wait()
    left_count = right_count = home_count = jnp.int32(0)
    left_pick = [jnp.int32(0)] * 2
    right_pick = [jnp.int32(0)] * 2
    home_pick = [jnp.int32(0)] * HOLD7
    switch_row = jnp.zeros((1, LANES), F32)
    for elem in range(ELEMS):
        switched = switch_s[elem]
        owner = owner_s[elem]
        switch_row = jnp.where(lane_elem == elem, switched.astype(F32), switch_row)
        fine_one = switched != 1
        goes_left = fine_one & (owner == left)
        goes_right = fine_one & (owner == right)
        stays = fine_one & jnp.logical_not(owner == left) & jnp.logical_not(owner == right)
        for slot in range(2):
            left_pick[slot] = jnp.where(goes_left & (left_count == slot), elem, left_pick[slot])
            right_pick[slot] = jnp.where(goes_right & (right_count == slot), elem, right_pick[slot])
        for slot in range(min(elem + 1, HOLD7)):
            home_pick[slot] = jnp.where(stays & (home_count == slot), elem, home_pick[slot])
        left_count = left_count + goes_left.astype(jnp.int32)
        right_count = right_count + goes_right.astype(jnp.int32)
        home_count = home_count + stays.astype(jnp.int32)
    for slot in range(HOLD7):
        home_list[slot] = home_pick[slot]
    count_arrivals = []
    count_send[0] = jnp.full((8, LANES), left_count, jnp.int32)
    count_send[1] = jnp.full((8, LANES), right_count, jnp.int32)
    for side in (0, 1):
        copy = pltpu.make_async_remote_copy(
            src_ref=count_send.at[side],
            dst_ref=count_recv.at[side ^ 1],
            send_sem=count_ssem.at[side],
            recv_sem=count_rsem.at[side ^ 1],
            device_id=partner[side],
            device_id_type=MESH,
        )
        copy.start()
        started.append(copy)
        count_arrivals.append(copy)
    is_switched = switch_row > 0.5

    for side, picks, count in ((0, left_pick, left_count), (1, right_pick, right_count)):
        chosen = jnp.zeros((LANES, LANES), F32)
        for slot in range(2):
            place = lanes // FIELDS == 2 * (1 - side) + slot
            source_row = rows - (lanes % FIELDS) == picks[slot] * FIELDS
            chosen = jnp.where(place & source_row & (count > slot), 1.0, chosen)
        chosen = chosen.astype(BF16)
        early_send[side, :LANES] = chosen
        normals = jnp.concatenate(
            [face_get(speed.at[other // 2], other).astype(BF16) for other in (0, 1, 4, 5)], axis=0
        )
        early_send[side, LANES:] = dot(normals, chosen).astype(BF16)
        copy = pltpu.make_async_remote_copy(
            src_ref=early_send.at[side],
            dst_ref=early_recv.at[side ^ 1],
            send_sem=early_ssem.at[side],
            recv_sem=early_rsem.at[side ^ 1],
            device_id=partner[side],
            device_id_type=MESH,
        )
        copy.start()
        started.append(copy)
        count_arrivals.append(copy)

    for side in (4, 5, 0, 1):
        slot = side if side < 2 else side - 2
        arrivals["wide", 0, side].wait_recv()
        face_add(u1, side, -(coef[side] * wide_recv[slot, pl.ds(0, 64), :].astype(F32)))
    next_traces = [fine_trace(u1, side) for side in range(6)]
    gather_local(next_traces)
    fine_start(u1, u0, u2, next_traces)
    c0 = dot(project_v[...], split_rows(u2[...]))
    raised = dot(raise_v[...], split_rows(c0))

    lift_coef = STEP * (P7 * (P7 - 1) / 2.0)
    for number in range(4):
        arrivals["corner", number].wait_recv()
    corner_values = [corner_recv[number].astype(F32) for number in range(4)]
    late = []
    for side in (0, 1, 4, 5):
        slot, dim, end = side if side < 2 else side - 2, side // 2, side % 2
        arrivals["wide", 1, side].wait_recv()
        got = wide_recv[slot].astype(F32)
        normal = -got[64:128] if end else got[64:128]
        first = got[144:208] + got[208:272]
        first = first - lift_coef * jnp.minimum(normal, 0.0) * traces[side].astype(F32)
        if dim == 0:
            around = [corner_values[end][8:16], corner_values[2 + end][8:16]]
        else:
            around = [corner_values[2 * end][0:8], corner_values[2 * end + 1][0:8]]
        around = lax.dot_general(
            jnp.concatenate(around, axis=0).astype(BF16),
            perm_far[slot],
            (((1,), (1,)), ((), ())),
            preferred_element_type=F32,
        )
        low_edge = lift_coef * jnp.minimum(-got[128:136], 0.0) * around[:8]
        high_edge = lift_coef * jnp.minimum(got[136:144], 0.0) * around[8:]
        next_near[slot] = first
        if dim == 0:
            next_near[slot, pl.ds(0, P7, stride=8), :] -= low_edge
            next_near[slot, pl.ds(7, P7, stride=8), :] -= high_edge
        else:
            next_near[slot, pl.ds(0, P7), :] -= low_edge
            next_near[slot, pl.ds(56, P7), :] -= high_edge
        late.append(0.5 * (coef[side] * next_near[slot].astype(BF16).astype(F32)))
    for place, side in enumerate((0, 1, 4, 5)):
        face_add(u2, side, -late[place])
    late = split_rows(jnp.concatenate(late, axis=0))

    traces, own = launch_mixed(2, u2, raised, late_fine_v, late)
    gather_local(mixes)
    c0 = c0 - dot(late_fine_v[384:, :], late)
    fine_start(u2, None, u3, traces)
    partial = coarse_start(c0, None)
    for copy in count_arrivals:
        copy.wait_recv()
    for place, side in enumerate((0, 1, 4, 5)):
        at = pl.ds(LANES + 64 * place, 64)
        normal = early_recv[0, at, :].astype(F32) + early_recv[1, at, :].astype(F32)
        lift_coef = 0.5 * STEP * (P7 * (P7 - 1) / 2.0)
        move_coef[place] = lift_coef * jnp.minimum(normal if side % 2 else -normal, 0.0)
    fine_end_z(2, 1.0, u3)
    c1 = coarse_end_z(2, own, 1.0, partial)
    raised = dot(raise_v[...], split_rows(c1))
    fine_end_x(2, 1.0, u3)
    late = coarse_jump_x(2)
    traces, own = launch_mixed(3, u3, raised, late_coarse_v, late)

    left2, right2 = lax.rem(pos + pieces - 2, pieces), lax.rem(pos + 2, pieces)
    extras = {
        (1, 1): (2, (below, right)),
        (1, 2): (3, (above, right)),
        (0, 1): (2, (below, left)),
        (0, 2): (3, (above, left)),
        (0, 0): (0, (slab, left2)),
        (1, 0): (1, (slab, right2)),
    }
    extra_copies = []
    for (toward, kind), (slot, device) in extras.items():
        place = 3 - kind if kind else 0
        copy = pltpu.make_async_remote_copy(
            src_ref=send.at[3, slot],
            dst_ref=extra_recv.at[1 - toward, place],
            send_sem=extra_ssem.at[toward, kind],
            recv_sem=extra_rsem.at[1 - toward, place],
            device_id=device,
            device_id_type=MESH,
        )
        copy.start()
        started.append(copy)
        extra_copies.append(copy)
    gather_local(mixes)
    c1 = c1 - dot(late_coarse_v[384:, :], late)
    fine_start(u3, u2, u1, traces)

    def turn_home():
        for number in range(4):
            home[:, :, number * 128 : number * 128 + 128] = jnp.transpose(
                u1[number * 128 : number * 128 + 128, :]
            ).reshape(ELEMS, FIELDS, 128)

    turn_home()
    for side in range(2):
        for slot in range(2):
            pick = (left_pick, right_pick)[side][slot]
            move_send[side, slot] = home[pick]
        copy = pltpu.make_async_remote_copy(
            src_ref=move_send.at[side],
            dst_ref=move_recv.at[side ^ 1],
            send_sem=move_ssem.at[side],
            recv_sem=move_rsem.at[side ^ 1],
            device_id=partner[side],
            device_id_type=MESH,
        )
        copy.start()
        started.append(copy)
        extra_copies.append(copy)
    partial = coarse_start(c1, c0)
    u3[...] = jnp.zeros_like(u3)
    fine_end_z(3, 0.5, u1)
    c2 = coarse_end_z(3, own, 0.5, partial)
    fine_end_x(3, 0.5, u1)
    c2 = c2 - 0.5 * dot(late_coarse_v[384:, :], coarse_jump_x(3))

    c2 = jnp.where(is_switched, c2, 0.0)
    turned[...] = jnp.transpose(jnp.concatenate([c2, pltpu.roll(c2, LANES - 1, 1)], axis=0))
    for pair in range(4):
        out3_v[:, pair * 128 : pair * 128 + 128] = turned[pl.ds(2 * pair, ELEMS, stride=FIELDS), :]
    turn_home()

    from_left = jnp.minimum(count_recv[0][0, 0], 2)
    from_right = jnp.minimum(count_recv[1][0, 0], 2)
    is_first, is_last = pos == 0, pos == pieces - 1
    at_left = jnp.where(is_first, home_count + from_right, jnp.where(is_last, from_right, 0))
    at_home = jnp.where(is_first, 0, jnp.where(is_last, from_right + from_left, from_left))
    at_right = jnp.where(is_first, home_count, jnp.where(is_last, 0, from_left + home_count))
    picks = []
    for slot in range(HOLD7):
        rank = slot - at_home
        stay = (rank >= 0) & (rank < home_count)
        value = home[home_list[jnp.clip(rank, 0, HOLD7 - 1)]]
        out7_v[slot] = jnp.where(stay, value, 0.0)
        rank_left, rank_right = slot - at_left, slot - at_right
        is_left = (rank_left >= 0) & (rank_left < from_left)
        is_right = (rank_right >= 0) & (rank_right < from_right)
        pick = jnp.where(is_left, rank_left, jnp.where(is_right, 2 + rank_right, 0))
        picks.append((is_left | is_right, pick))
    for copy in extra_copies:
        copy.wait_recv()
    chosen = jnp.concatenate([early_recv[0, :LANES, :], early_recv[1, :LANES, :]], axis=0)
    nears = {
        0: (extra_recv[0, 0], send[3, 1]),
        1: (send[3, 0], extra_recv[1, 0]),
        4: (extra_recv[0, 1], extra_recv[1, 1]),
        5: (extra_recv[0, 2], extra_recv[1, 2]),
    }
    for place, side in enumerate((0, 1, 4, 5)):
        near = dot(jnp.concatenate(nears[side], axis=1), chosen)
        face_add(u3, side, -(move_coef[place] * near))
    for number in range(4):
        moved = jnp.transpose(u3[number * 128 : number * 128 + 128, :])
        at = pl.ds(number * 128, 128)
        for pick in range(4):
            move_recv[pick // 2, pick % 2, :, at] += moved[pick * FIELDS : pick * FIELDS + FIELDS]
    for slot in range(HOLD7):
        arrived, pick = picks[slot]
        value = move_recv[pick // 2, pick % 2]
        out7_v[slot] = jnp.where(arrived, value, out7_v[slot])
    for copy in started:
        copy.wait_send()


def solution(mesh):
    slabs, pieces = mesh.shape["slab"], mesh.shape["curve"]
    tables = make_tables()

    def per_device(state, velocity, pre_exp, stoich, neighbours, switch, new_owner):
        velocity = jnp.transpose(velocity, (0, 2, 1))
        neighbours = jnp.transpose(neighbours)
        operands = (state, velocity, neighbours, pre_exp, stoich, switch, new_owner) + tuple(
            jnp.asarray(table) for table in tables
        )
        vm, sm, dma = pltpu.VMEM, pltpu.SMEM, pltpu.SemaphoreType.DMA
        nodes = (512, LANES)
        return pl.pallas_call(
            functools.partial(kernel, slabs, pieces),
            out_shape=(
                pltpu.VMEM((HOLD7, FIELDS, 512), F32),
                pltpu.VMEM((ELEMS, 512), F32),
            ),
            in_specs=[pl.BlockSpec(memory_space=pltpu.HBM)] * len(operands),
            out_specs=[pl.BlockSpec(memory_space=pltpu.VMEM)] * 2,
            scratch_shapes=[
                vm((ELEMS, FIELDS, 512), F32),
                vm((3, ELEMS, 64), BF16),
                vm((6, ELEMS), jnp.int32),
                sm((ELEMS,), F32),
                sm((FIELDS,), F32),
                sm((ELEMS,), jnp.int32),
                sm((ELEMS,), jnp.int32),
            ]
            + [vm(table.shape, BF16) for table in tables]
            + [
                vm(nodes, F32),
                vm(nodes, F32),
                vm(nodes, F32),
                vm(nodes, F32),
                vm((3, 512, LANES), F32),
                vm((6, 64, LANES), F32),
                vm((192, LANES), F32),
                vm((384, LANES), F32),
                vm((4, LANES, LANES), BF16),
                vm((4, LANES, LANES), BF16),
                vm((4, 64, LANES), F32),
                vm((4, 4, 64, LANES), BF16),
                vm((4, 4, 64, LANES), BF16),
                vm((2, 8, LANES), jnp.int32),
                vm((2, 8, LANES), jnp.int32),
                vm((ELEMS, FIELDS, 512), F32),
                vm((2, 2, FIELDS, 512), F32),
                vm((2, 2, FIELDS, 512), F32),
                vm((2, 3 * LANES, LANES), BF16),
                vm((2, 3 * LANES, LANES), BF16),
                vm((4, 272, LANES), BF16),
                vm((4, 272, LANES), BF16),
                vm((4, 64, LANES), F32),
                vm((4, 64, LANES), F32),
                vm((4, 16, LANES), BF16),
                vm((4, 16, LANES), BF16),
                vm((2, 3, 64, LANES), BF16),
                vm((4, 64, LANES), F32),
                vm((LANES, LANES), F32),
                sm((HOLD7,), jnp.int32),
                dma((15,)),
                dma((4, 4)),
                dma((4, 4)),
                dma((2,)),
                dma((2,)),
                dma((2,)),
                dma((2,)),
                dma((2,)),
                dma((2,)),
                dma((2, 3)),
                dma((2, 3)),
                dma((2, 4)),
                dma((2, 4)),
                dma((4,)),
                dma((4,)),
            ],
            compiler_params=pltpu.CompilerParams(
                collective_id=0, has_side_effects=True, vmem_limit_bytes=62 * 2**20
            ),
        )(*operands)

    return jax.shard_map(
        per_device,
        mesh=mesh,
        in_specs=(
            P(("slab", "curve"), None, None),
            P(None, None, ("slab", "curve")),
            P(("slab", "curve")),
            P(),
            P(("slab", "curve"), None),
            P(("slab", "curve")),
            P(("slab", "curve")),
        ),
        out_specs=(P(("slab", "curve"), None, None), P(("slab", "curve"), None)),
        check_vma=False,
    )
```

```python
import functools

import jax
import jax.numpy as jnp
import ml_dtypes
import numpy as np
from jax import lax
from jax.experimental import pallas as pl
from jax.experimental.pallas import tpu as pltpu
from jax.sharding import PartitionSpec as P

P7 = 8
P3 = 4
ELEMS = 16
FIELDS = 8
LANES = ELEMS * FIELDS
HOLD7 = 12
STEP = 0.002
ACTIVATION = 1.5
MESH = pl.DeviceIdType.MESH
F32 = jnp.float32
BF16 = jnp.bfloat16


def lobatto_points(number):
    return -np.cos(np.pi * np.arange(number) / (number - 1))


def derivative_matrix(points):
    number = points.shape[0]
    weights = np.ones(number)
    for row in range(number):
        for col in range(number):
            if col != row:
                weights[row] = weights[row] / (points[row] - points[col])
    matrix = np.zeros((number, number))
    for row in range(number):
        for col in range(number):
            if col != row:
                matrix[row, col] = weights[col] / weights[row] / (points[row] - points[col])
        matrix[row, row] = -np.sum(matrix[row])
    return matrix


def interpolation_matrix(source, target):
    matrix = np.ones((target.shape[0], source.shape[0]))
    for col in range(source.shape[0]):
        for other in range(source.shape[0]):
            if other != col:
                matrix[:, col] = (
                    matrix[:, col] * (target - source[other]) / (source[col] - source[other])
                )
    return matrix


def kron3(a, b, c):
    return np.kron(a, np.kron(b, c))


def to_bf16(matrix):
    return np.asarray(matrix, np.float32).astype(ml_dtypes.bfloat16)


def split_columns(matrix):
    full = np.asarray(matrix, np.float32)
    high = full.astype(ml_dtypes.bfloat16)
    low = (full - high.astype(np.float32)).astype(ml_dtypes.bfloat16)
    return np.concatenate([high, low, high], axis=1)


def face_selectors(extent):
    ident = np.eye(extent)
    first, last = ident[:1], ident[-1:]
    picks = []
    for end in (first, last):
        picks.append(kron3(end, ident, ident))
    for end in (first, last):
        picks.append(kron3(ident, end, ident))
    for end in (first, last):
        picks.append(kron3(ident, ident, end))
    return np.stack(picks)


def make_tables():
    r7, r3 = lobatto_points(P7), lobatto_points(P3)
    d7, d3 = derivative_matrix(r7), derivative_matrix(r3)
    down = interpolation_matrix(r7, r3)
    up = interpolation_matrix(r3, r7)
    i7, i3 = np.eye(P7), np.eye(P3)
    div_i = np.kron(d7, np.eye(32))
    two = np.eye(2)
    div_jk = np.concatenate([np.kron(two, np.kron(d7, i7)), np.kron(two, np.kron(i7, d7))], axis=1)
    fine = to_bf16(np.concatenate([div_i, div_jk], axis=0))
    lift = to_bf16(kron3(up, up, up))
    project = split_columns(kron3(down, down, down))
    mortar_up = np.asarray(np.kron(up, up), np.float32).astype(np.float64)
    mortar_down = np.asarray(np.kron(down, down), np.float32).astype(np.float64)
    selectors = face_selectors(P3)
    raise_all = np.concatenate([mortar_up @ selectors[side] for side in range(6)], axis=0)
    lower_all = np.concatenate([selectors[side].T @ mortar_down for side in range(6)], axis=1)
    lower_all = STEP * (P3 * (P3 - 1) / 2.0) * lower_all
    raise_faces = split_columns(raise_all)
    lower_faces = split_columns(lower_all)
    project_all = np.asarray(kron3(down, down, down), np.float32).astype(np.float64)
    fine_selectors = face_selectors(P7)
    project_late = np.concatenate(
        [project_all @ fine_selectors[side].T for side in (0, 1, 4, 5)], axis=1
    )
    late_fine = split_columns(np.concatenate([raise_all @ project_late, project_late], axis=0))
    lower_x = lower_all[:, :128]
    late_coarse = split_columns(np.concatenate([raise_all @ lower_x, lower_x], axis=0))
    coarse = to_bf16(
        np.concatenate([kron3(d3, i3, i3), kron3(i3, d3, i3), kron3(i3, i3, d3)], axis=1)
    )
    return fine, lift, project, raise_faces, lower_faces, coarse, late_fine, late_coarse


def dot(a, b):
    return jnp.dot(a, b, preferred_element_type=F32)


def split_rows(value):
    high = value.astype(BF16)
    low = (value - high.astype(F32)).astype(BF16)
    return jnp.concatenate([high, high, low], axis=0)


def face_slices(side):
    dim, end = side // 2, side % 2
    if dim == 0:
        return [pl.ds(448 * end, 64)]
    if dim == 1:
        return [pl.ds(i * 64 + 56 * end, 8) for i in range(P7)]
    return [pl.ds(7 * end, 64, stride=8)]


def face_get(ref, side):
    parts = [ref[where, :] for where in face_slices(side)]
    return parts[0] if len(parts) == 1 else jnp.concatenate(parts, axis=0)


def face_add(ref, side, value):
    start = 0
    for where in face_slices(side):
        ref[where, :] += value[start : start + where.size]
        start += where.size


def edge_slice(x_end, z_end):
    return pl.ds(448 * x_end + 7 * z_end, P7, stride=8)


def kernel(
    slabs,
    pieces,
    state_h,
    vel_h,
    nbr_h,
    pre_h,
    stoich_h,
    switch_h,
    owner_h,
    fine_h,
    lift_h,
    project_h,
    raise_h,
    lower_h,
    coarse_h,
    late_fine_h,
    late_coarse_h,
    out7_v,
    out3_v,
    state_v,
    vel_v,
    nbr_v,
    pre_s,
    stoich_s,
    switch_s,
    owner_s,
    fine_v,
    lift_v,
    project_v,
    raise_v,
    lower_v,
    coarse_v,
    late_fine_v,
    late_coarse_v,
    u0,
    u1,
    u2,
    u3,
    speed,
    coef,
    vel_rep,
    vmin,
    perm_far,
    perm_near,
    local_nb,
    send,
    recv,
    count_send,
    count_recv,
    home,
    move_send,
    move_recv,
    early_send,
    early_recv,
    wide_send,
    wide_recv,
    far_trace,
    next_near,
    corner_send,
    corner_recv,
    extra_recv,
    move_coef,
    turned,
    home_list,
    load_sem,
    send_sem,
    recv_sem,
    count_ssem,
    count_rsem,
    move_ssem,
    move_rsem,
    early_ssem,
    early_rsem,
    extra_ssem,
    extra_rsem,
    wide_ssem,
    wide_rsem,
    corner_ssem,
    corner_rsem,
):
    slab, pos = lax.axis_index("slab"), lax.axis_index("curve")
    left, right = lax.rem(pos + pieces - 1, pieces), lax.rem(pos + 1, pieces)
    below, above = lax.rem(slab + slabs - 1, slabs), lax.rem(slab + 1, slabs)
    partner = {0: (slab, left), 1: (slab, right), 4: (below, pos), 5: (above, pos)}

    barrier = pltpu.get_barrier_semaphore()
    corners = [(below, left), (below, right), (above, left), (above, right)]
    for device in list(partner.values()) + corners:
        pl.semaphore_signal(barrier, inc=1, device_id=device, device_id_type=MESH)

    pairs = [
        (state_h, state_v),
        (vel_h, vel_v),
        (nbr_h, nbr_v),
        (lift_h, lift_v),
        (pre_h, pre_s),
        (stoich_h, stoich_s),
        (switch_h, switch_s),
        (owner_h, owner_s),
        (fine_h, fine_v),
        (raise_h, raise_v),
        (project_h, project_v),
        (lower_h, lower_v),
        (coarse_h, coarse_v),
        (late_fine_h, late_fine_v),
        (late_coarse_h, late_coarse_v),
    ]
    loads = [
        pltpu.make_async_copy(source, target, load_sem.at[number])
        for number, (source, target) in enumerate(pairs)
    ]
    for number in (0, 2, 1, 3, 8, 4, 5, 6, 7):
        loads[number].start()

    lane_row = lax.broadcasted_iota(jnp.int32, (1, LANES), 1)
    lane_elem = lane_row // FIELDS
    lane_field = lane_row % FIELDS
    lanes = lax.broadcasted_iota(jnp.int32, (LANES, LANES), 1)
    rows = lax.broadcasted_iota(jnp.int32, (LANES, LANES), 0)
    spread = (
        lax.broadcasted_iota(jnp.int32, (ELEMS, LANES), 0)
        == lax.broadcasted_iota(jnp.int32, (ELEMS, LANES), 1) // FIELDS
    ).astype(F32)
    rep = ((rows % FIELDS == 0) & (rows // FIELDS == lanes // FIELDS)).astype(F32).astype(BF16)
    rep2 = jnp.concatenate([rep, rep], axis=0)

    loads[0].wait()
    for load in loads[9:]:
        load.start()
    u0[...] = jnp.transpose(state_v[...].reshape(LANES, 512))

    loads[2].wait()
    ids = nbr_v[...]
    me = slab * pieces + pos
    here = lax.shift_right_logical(ids, 4) == me
    code = jnp.where(here, ids & 15, (ids & 15) + 16).astype(F32)
    spread_t = (
        lax.broadcasted_iota(jnp.int32, (LANES, ELEMS), 1)
        == lax.broadcasted_iota(jnp.int32, (LANES, ELEMS), 0) // FIELDS
    ).astype(F32)
    target = lax.dot_general(
        spread_t.astype(BF16),
        code.astype(BF16),
        (((1,), (1,)), ((), ())),
        preferred_element_type=F32,
    )
    target = target.astype(jnp.int32) * FIELDS
    target = target + lax.broadcasted_iota(jnp.int32, (LANES, 6), 0) % FIELDS
    for side in range(6):
        column = target[:, side : side + 1]
        near = (column == lanes).astype(F32).astype(BF16)
        far = (column == lanes + LANES).astype(F32).astype(BF16)
        if side < 2:
            perm_far[side] = far
            perm_near[side] = near
        elif side < 4:
            perm_near[side] = near
        else:
            perm_far[side - 2] = far

    def launch(number, side, trace):
        slot = side if side < 2 else side - 2
        send[number, slot] = dot(trace, perm_far[slot]).astype(BF16)
        copy = pltpu.make_async_remote_copy(
            src_ref=send.at[number, slot],
            dst_ref=recv.at[number, slot ^ 1],
            send_sem=send_sem.at[number, slot],
            recv_sem=recv_sem.at[number, slot ^ 1],
            device_id=partner[side],
            device_id_type=MESH,
        )
        copy.start()
        started.append(copy)
        arrivals[number, side ^ 1] = copy

    def gather_local(traces):
        for side in range(4):
            local_nb[side ^ 1] = dot(traces[side], perm_near[side])

    started, arrivals = [], {}

    def fine_trace(ref, side):
        return face_get(ref, side).astype(BF16)

    traces = [fine_trace(u0, side) for side in range(6)]
    gather_local(traces)

    loads[1].wait()
    loads[3].wait()
    for dim in range(3):
        spread_vel = lax.dot_general(
            vel_v[dim],
            spread.astype(BF16),
            (((0,), (0,)), ((), ())),
            preferred_element_type=F32,
        ).astype(BF16)
        vel_rep[dim * 64 : dim * 64 + 64] = spread_vel.astype(F32)
        speed[dim] = dot(lift_v[...], spread_vel).astype(BF16).astype(F32)
        for end in range(2):
            side = 2 * dim + end
            normal = face_get(speed.at[dim], side)
            lift_coef = STEP * (P7 * (P7 - 1) / 2.0)
            coef[side] = lift_coef * jnp.minimum(normal if end else -normal, 0.0)

    loads[4].wait()
    loads[5].wait()
    pre_row = jnp.zeros((1, LANES), F32)
    stoich_row = jnp.zeros((1, LANES), F32)
    for elem in range(ELEMS):
        pre_row = jnp.where(lane_elem == elem, pre_s[elem], pre_row)
    for field in range(FIELDS):
        stoich_row = jnp.where(lane_field == field, stoich_s[field], stoich_row)

    def source(u):
        rate = (
            pre_row
            * jnp.exp(-ACTIVATION * jnp.exp(-u))
            * pltpu.roll(u, LANES - 1, 1)
            * pltpu.roll(u, LANES - 2, 1)
        )
        high = rate.astype(BF16)
        low = (rate - high.astype(F32)).astype(BF16)
        return stoich_row * dot(jnp.concatenate([high, low], axis=1), rep2)

    loads[8].wait()

    def fine_start(ref, start, out, traces):
        scale = 1.0 if start is None else 0.5
        along_i = []
        for half in range(2):
            parts = []
            for i in range(P7):
                at = pl.ds(i * 64 + half * 32, 32)
                parts.append((speed[0, at, :] * ref[at, :]).astype(BF16))
            along_i.append(dot(fine_v[:256, :], jnp.concatenate(parts, axis=0)))
        for block in range(4):
            at = pl.ds(block * 128, 128)
            u = ref[at, :]
            flux = jnp.concatenate(
                [(speed[1, at, :] * u).astype(BF16), (speed[2, at, :] * u).astype(BF16)], axis=0
            )
            div = dot(fine_v[256:, :], flux) + jnp.concatenate(
                [
                    along_i[half][i * 32 : i * 32 + 32]
                    for i in (2 * block, 2 * block + 1)
                    for half in range(2)
                ],
                axis=0,
            )
            rate = STEP * (source(u) - div)
            out[at, :] = u + rate if start is None else 0.5 * (start[at, :] + u + rate)
        for side in range(6):
            jump = traces[side].astype(F32)
            if side < 4:
                jump = jump - local_nb[side]
            face_add(out, side, scale * (coef[side] * jump))

    def late_term(number, side, scale):
        slot = side if side < 2 else side - 2
        arrivals[number, side].wait_recv()
        return scale * (coef[side] * recv[number, slot].astype(F32))

    def fine_end_z(number, scale, out):
        for side in (4, 5):
            face_add(out, side, -late_term(number, side, scale))

    def fine_end_x(number, scale, out):
        terms = [late_term(number, side, scale) for side in (0, 1)]
        for side in (0, 1):
            face_add(out, side, -terms[side])
        return jnp.concatenate(terms, axis=0)

    def coarse_start(c, start):
        flux = jnp.concatenate(
            [(vel_rep[dim * 64 : dim * 64 + 64] * c).astype(BF16) for dim in range(3)], axis=0
        )
        rate = STEP * (source(c) - dot(coarse_v[...], flux))
        return c + rate if start is None else 0.5 * (start + c + rate)

    def coarse_end_z(number, own, scale, partial):
        jumps = []
        for side in range(6):
            near = local_nb[side] if side < 4 else recv[number, side - 2].astype(F32)
            mine = own[side * 64 : side * 64 + 64].astype(F32)
            jumps.append(vmin[side * 64 : side * 64 + 64] * (mine - near))
        return partial + scale * dot(lower_v[...], split_rows(jnp.concatenate(jumps, axis=0)))

    def coarse_jump_x(number):
        return split_rows(
            jnp.concatenate(
                [vmin[side * 64 : side * 64 + 64] * recv[number, side].astype(F32) for side in (0, 1)],
                axis=0,
            )
        )

    def launch_mixed(number, fine, raised_base, table, late):
        own, traces = [None] * 6, [None] * 6
        for sides in ((0, 1), (4, 5), (2, 3)):
            at = slice(sides[0] * 64, sides[0] * 64 + 128)
            raised = raised_base[at] - dot(table[at, :], late)
            for place, side in enumerate(sides):
                own[side] = raised[place * 64 : place * 64 + 64]
                traces[side] = fine_trace(fine, side)
                mixed = jnp.where(is_switched, own[side], traces[side].astype(F32)).astype(BF16)
                if side in (2, 3):
                    mixes[side] = mixed
                else:
                    launch(number, side, mixed)
                    mixes[side] = mixed
        return traces, jnp.concatenate(own, axis=0).astype(BF16)

    mixes = [None] * 6

    fine_start(u0, None, u1, traces)
    for side in (0, 1, 4, 5):
        slot, dim, end = side if side < 2 else side - 2, side // 2, side % 2
        edges = [(end, 0), (end, 1)] if dim == 0 else [(0, end), (1, end)]
        first = face_get(u1, side)
        high = first.astype(BF16)
        packed = [
            traces[side],
            face_get(speed.at[dim], side).astype(BF16),
            jnp.concatenate([speed[2 - dim, edge_slice(*edge), :] for edge in edges], axis=0).astype(BF16),
            high,
            (first - high.astype(F32)).astype(BF16),
        ]
        placed = dot(jnp.concatenate(packed, axis=0), perm_far[slot])
        wide_send[slot] = placed.astype(BF16)
        far_trace[slot] = placed[:64]
    for number, corner in enumerate(corners):
        z_end, x_end = number // 2, number % 2
        corner_send[number] = jnp.concatenate(
            [
                far_trace[x_end, pl.ds(7 * z_end, P7, stride=8), :],
                far_trace[2 + z_end, pl.ds(56 * x_end, P7), :],
            ],
            axis=0,
        ).astype(BF16)
    pl.semaphore_wait(barrier, 8)
    for number, corner in enumerate(corners):
        copy = pltpu.make_async_remote_copy(
            src_ref=corner_send.at[number],
            dst_ref=corner_recv.at[3 - number],
            send_sem=corner_ssem.at[number],
            recv_sem=corner_rsem.at[3 - number],
            device_id=corner,
            device_id_type=MESH,
        )
        copy.start()
        started.append(copy)
        arrivals["corner", 3 - number] = copy
    for part, (start_row, count) in enumerate(((0, 144), (144, 128))):
        for side in (0, 1, 4, 5):
            slot = side if side < 2 else side - 2
            at = pl.ds(start_row, count)
            copy = pltpu.make_async_remote_copy(
                src_ref=wide_send.at[slot, at],
                dst_ref=wide_recv.at[slot ^ 1, at],
                send_sem=wide_ssem.at[part, slot],
                recv_sem=wide_rsem.at[part, slot ^ 1],
                device_id=partner[side],
                device_id_type=MESH,
            )
            copy.start()
            started.append(copy)
            arrivals["wide", part, side ^ 1] = copy

    loads[6].wait()
    loads[7].wait()
    left_count = right_count = home_count = jnp.int32(0)
    left_pick = [jnp.int32(0)] * 2
    right_pick = [jnp.int32(0)] * 2
    home_pick = [jnp.int32(0)] * HOLD7
    switch_row = jnp.zeros((1, LANES), F32)
    for elem in range(ELEMS):
        switched = switch_s[elem]
        owner = owner_s[elem]
        switch_row = jnp.where(lane_elem == elem, switched.astype(F32), switch_row)
        fine_one = switched != 1
        goes_left = fine_one & (owner == left)
        goes_right = fine_one & (owner == right)
        stays = fine_one & jnp.logical_not(owner == left) & jnp.logical_not(owner == right)
        for slot in range(2):
            left_pick[slot] = jnp.where(goes_left & (left_count == slot), elem, left_pick[slot])
            right_pick[slot] = jnp.where(goes_right & (right_count == slot), elem, right_pick[slot])
        for slot in range(min(elem + 1, HOLD7)):
            home_pick[slot] = jnp.where(stays & (home_count == slot), elem, home_pick[slot])
        left_count = left_count + goes_left.astype(jnp.int32)
        right_count = right_count + goes_right.astype(jnp.int32)
        home_count = home_count + stays.astype(jnp.int32)
    for slot in range(HOLD7):
        home_list[slot] = home_pick[slot]
    count_arrivals = []
    count_send[0] = jnp.full((8, LANES), left_count, jnp.int32)
    count_send[1] = jnp.full((8, LANES), right_count, jnp.int32)
    for side in (0, 1):
        copy = pltpu.make_async_remote_copy(
            src_ref=count_send.at[side],
            dst_ref=count_recv.at[side ^ 1],
            send_sem=count_ssem.at[side],
            recv_sem=count_rsem.at[side ^ 1],
            device_id=partner[side],
            device_id_type=MESH,
        )
        copy.start()
        started.append(copy)
        count_arrivals.append(copy)
    is_switched = switch_row > 0.5

    for side, picks, count in ((0, left_pick, left_count), (1, right_pick, right_count)):
        chosen = jnp.zeros((LANES, LANES), F32)
        for slot in range(2):
            place = lanes // FIELDS == 2 * (1 - side) + slot
            source_row = rows - (lanes % FIELDS) == picks[slot] * FIELDS
            chosen = jnp.where(place & source_row & (count > slot), 1.0, chosen)
        chosen = chosen.astype(BF16)
        early_send[side, :LANES] = chosen
        normals = jnp.concatenate(
            [face_get(speed.at[other // 2], other).astype(BF16) for other in (0, 1, 4, 5)], axis=0
        )
        early_send[side, LANES:] = dot(normals, chosen).astype(BF16)
        copy = pltpu.make_async_remote_copy(
            src_ref=early_send.at[side],
            dst_ref=early_recv.at[side ^ 1],
            send_sem=early_ssem.at[side],
            recv_sem=early_rsem.at[side ^ 1],
            device_id=partner[side],
            device_id_type=MESH,
        )
        copy.start()
        started.append(copy)
        count_arrivals.append(copy)

    for load in loads[9:]:
        load.wait()
    for dim in range(3):
        spread_vel = vel_rep[dim * 64 : dim * 64 + 64].astype(BF16)
        mortar = dot(
            raise_v[dim * 128 : dim * 128 + 128, :128],
            jnp.concatenate([spread_vel, spread_vel], axis=0),
        )
        vmin[dim * 128 : dim * 128 + 64] = jnp.minimum(-mortar[:64], 0.0)
        vmin[dim * 128 + 64 : dim * 128 + 128] = jnp.minimum(mortar[64:], 0.0)

    for side in (4, 5, 0, 1):
        slot = side if side < 2 else side - 2
        arrivals["wide", 0, side].wait_recv()
        face_add(u1, side, -(coef[side] * wide_recv[slot, pl.ds(0, 64), :].astype(F32)))
    next_traces = [fine_trace(u1, side) for side in range(6)]
    gather_local(next_traces)
    fine_start(u1, u0, u2, next_traces)
    c0 = dot(project_v[...], split_rows(u2[...]))
    raised = dot(raise_v[...], split_rows(c0))

    lift_coef = STEP * (P7 * (P7 - 1) / 2.0)
    edge_coef = {}
    for side in (0, 1, 4, 5):
        slot, end = side if side < 2 else side - 2, side % 2
        normal = wide_recv[slot, pl.ds(64, 64), :].astype(F32)
        normal = -normal if end else normal
        next_near[slot] = lift_coef * jnp.minimum(normal, 0.0) * traces[side].astype(F32)
        edge = wide_recv[slot, pl.ds(128, 16), :].astype(F32)
        edge_coef[side] = [
            lift_coef * jnp.minimum(-edge[:8], 0.0),
            lift_coef * jnp.minimum(edge[8:], 0.0),
        ]
    for side in (4, 5, 0, 1):
        slot = side if side < 2 else side - 2
        arrivals["wide", 1, side].wait_recv()
        got = wide_recv[slot, pl.ds(144, 128), :].astype(F32)
        next_near[slot] = got[:64] + got[64:] - next_near[slot]
    for number in range(4):
        arrivals["corner", number].wait_recv()
    corner_values = [corner_recv[number].astype(F32) for number in range(4)]
    late = []
    for side in (0, 1, 4, 5):
        slot, dim, end = side if side < 2 else side - 2, side // 2, side % 2
        if dim == 0:
            around = [corner_values[end][8:16], corner_values[2 + end][8:16]]
        else:
            around = [corner_values[2 * end][0:8], corner_values[2 * end + 1][0:8]]
        around = lax.dot_general(
            jnp.concatenate(around, axis=0).astype(BF16),
            perm_far[slot],
            (((1,), (1,)), ((), ())),
            preferred_element_type=F32,
        )
        for which in range(2):
            term = edge_coef[side][which] * around[8 * which : 8 * which + 8]
            at = pl.ds(7 * which, P7, stride=8) if dim == 0 else pl.ds(56 * which, P7)
            next_near[slot, at, :] -= term
        late.append(0.5 * (coef[side] * next_near[slot].astype(BF16).astype(F32)))
    for place, side in enumerate((0, 1, 4, 5)):
        face_add(u2, side, -late[place])
    late = split_rows(jnp.concatenate(late, axis=0))

    traces, own = launch_mixed(2, u2, raised, late_fine_v, late)
    gather_local(mixes)
    c0 = c0 - dot(late_fine_v[384:, :], late)
    fine_start(u2, None, u3, traces)
    partial = coarse_start(c0, None)
    for copy in count_arrivals:
        copy.wait_recv()
    for place, side in enumerate((0, 1, 4, 5)):
        at = pl.ds(LANES + 64 * place, 64)
        normal = early_recv[0, at, :].astype(F32) + early_recv[1, at, :].astype(F32)
        lift_coef = 0.5 * STEP * (P7 * (P7 - 1) / 2.0)
        move_coef[place] = lift_coef * jnp.minimum(normal if side % 2 else -normal, 0.0)
    fine_end_z(2, 1.0, u3)
    c1 = coarse_end_z(2, own, 1.0, partial)
    raised = dot(raise_v[...], split_rows(c1))
    fine_end_x(2, 1.0, u3)
    late = coarse_jump_x(2)
    traces, own = launch_mixed(3, u3, raised, late_coarse_v, late)

    left2, right2 = lax.rem(pos + pieces - 2, pieces), lax.rem(pos + 2, pieces)
    extras = {
        (1, 1): (2, (below, right)),
        (1, 2): (3, (above, right)),
        (0, 1): (2, (below, left)),
        (0, 2): (3, (above, left)),
        (0, 0): (0, (slab, left2)),
        (1, 0): (1, (slab, right2)),
    }
    extra_copies = []
    for (toward, kind), (slot, device) in extras.items():
        place = 3 - kind if kind else 0
        copy = pltpu.make_async_remote_copy(
            src_ref=send.at[3, slot],
            dst_ref=extra_recv.at[1 - toward, place],
            send_sem=extra_ssem.at[toward, kind],
            recv_sem=extra_rsem.at[1 - toward, place],
            device_id=device,
            device_id_type=MESH,
        )
        copy.start()
        started.append(copy)
        extra_copies.append(copy)
    gather_local(mixes)
    c1 = c1 - dot(late_coarse_v[384:, :], late)
    fine_start(u3, u2, u1, traces)

    def turn_home():
        for number in range(4):
            home[:, :, number * 128 : number * 128 + 128] = jnp.transpose(
                u1[number * 128 : number * 128 + 128, :]
            ).reshape(ELEMS, FIELDS, 128)

    turn_home()
    for side in range(2):
        for slot in range(2):
            pick = (left_pick, right_pick)[side][slot]
            move_send[side, slot] = home[pick]
        copy = pltpu.make_async_remote_copy(
            src_ref=move_send.at[side],
            dst_ref=move_recv.at[side ^ 1],
            send_sem=move_ssem.at[side],
            recv_sem=move_rsem.at[side ^ 1],
            device_id=partner[side],
            device_id_type=MESH,
        )
        copy.start()
        started.append(copy)
        extra_copies.append(copy)
    partial = coarse_start(c1, c0)
    u3[...] = jnp.zeros_like(u3)
    fine_end_z(3, 0.5, u1)
    c2 = coarse_end_z(3, own, 0.5, partial)
    fine_end_x(3, 0.5, u1)
    c2 = c2 - 0.5 * dot(late_coarse_v[384:, :], coarse_jump_x(3))

    c2 = jnp.where(is_switched, c2, 0.0)
    turned[...] = jnp.transpose(jnp.concatenate([c2, pltpu.roll(c2, LANES - 1, 1)], axis=0))
    for pair in range(4):
        out3_v[:, pair * 128 : pair * 128 + 128] = turned[pl.ds(2 * pair, ELEMS, stride=FIELDS), :]
    turn_home()

    from_left = jnp.minimum(count_recv[0][0, 0], 2)
    from_right = jnp.minimum(count_recv[1][0, 0], 2)
    is_first, is_last = pos == 0, pos == pieces - 1
    at_left = jnp.where(is_first, home_count + from_right, jnp.where(is_last, from_right, 0))
    at_home = jnp.where(is_first, 0, jnp.where(is_last, from_right + from_left, from_left))
    at_right = jnp.where(is_first, home_count, jnp.where(is_last, 0, from_left + home_count))
    picks = []
    for slot in range(HOLD7):
        rank = slot - at_home
        stay = (rank >= 0) & (rank < home_count)
        value = home[home_list[jnp.clip(rank, 0, HOLD7 - 1)]]
        out7_v[slot] = jnp.where(stay, value, 0.0)
        rank_left, rank_right = slot - at_left, slot - at_right
        is_left = (rank_left >= 0) & (rank_left < from_left)
        is_right = (rank_right >= 0) & (rank_right < from_right)
        pick = jnp.where(is_left, rank_left, jnp.where(is_right, 2 + rank_right, 0))
        picks.append((is_left | is_right, pick))
    for copy in extra_copies:
        copy.wait_recv()
    chosen = jnp.concatenate([early_recv[0, :LANES, :], early_recv[1, :LANES, :]], axis=0)
    nears = {
        0: (extra_recv[0, 0], send[3, 1]),
        1: (send[3, 0], extra_recv[1, 0]),
        4: (extra_recv[0, 1], extra_recv[1, 1]),
        5: (extra_recv[0, 2], extra_recv[1, 2]),
    }
    for place, side in enumerate((0, 1, 4, 5)):
        near = dot(jnp.concatenate(nears[side], axis=1), chosen)
        face_add(u3, side, -(move_coef[place] * near))
    for number in range(4):
        moved = jnp.transpose(u3[number * 128 : number * 128 + 128, :])
        at = pl.ds(number * 128, 128)
        for pick in range(4):
            move_recv[pick // 2, pick % 2, :, at] += moved[pick * FIELDS : pick * FIELDS + FIELDS]
    for slot in range(HOLD7):
        arrived, pick = picks[slot]
        value = move_recv[pick // 2, pick % 2]
        out7_v[slot] = jnp.where(arrived, value, out7_v[slot])
    for copy in started:
        copy.wait_send()


def store_kernel(held7, held3, out7, out3, sem):
    copies = [
        pltpu.make_async_copy(held7, out7, sem.at[0]),
        pltpu.make_async_copy(held3, out3, sem.at[1]),
    ]
    for copy in copies:
        copy.start()
    for copy in copies:
        copy.wait()


def solution(mesh):
    slabs, pieces = mesh.shape["slab"], mesh.shape["curve"]
    tables = make_tables()

    def per_device(state, velocity, pre_exp, stoich, neighbours, switch, new_owner):
        velocity = jnp.transpose(velocity, (0, 2, 1))
        neighbours = jnp.transpose(neighbours)
        operands = (state, velocity, neighbours, pre_exp, stoich, switch, new_owner) + tuple(
            jnp.asarray(table) for table in tables
        )
        vm, sm, dma = pltpu.VMEM, pltpu.SMEM, pltpu.SemaphoreType.DMA
        nodes = (512, LANES)
        held = pl.pallas_call(
            functools.partial(kernel, slabs, pieces),
            out_shape=(
                pltpu.VMEM((HOLD7, FIELDS, 512), F32),
                pltpu.VMEM((ELEMS, 512), F32),
            ),
            in_specs=[pl.BlockSpec(memory_space=pltpu.HBM)] * len(operands),
            out_specs=[pl.BlockSpec(memory_space=pltpu.VMEM)] * 2,
            scratch_shapes=[
                vm((ELEMS, FIELDS, 512), F32),
                vm((3, ELEMS, 64), BF16),
                vm((6, ELEMS), jnp.int32),
                sm((ELEMS,), F32),
                sm((FIELDS,), F32),
                sm((ELEMS,), jnp.int32),
                sm((ELEMS,), jnp.int32),
            ]
            + [vm(table.shape, BF16) for table in tables]
            + [
                vm(nodes, F32),
                vm(nodes, F32),
                vm(nodes, F32),
                vm(nodes, F32),
                vm((3, 512, LANES), F32),
                vm((6, 64, LANES), F32),
                vm((192, LANES), F32),
                vm((384, LANES), F32),
                vm((4, LANES, LANES), BF16),
                vm((4, LANES, LANES), BF16),
                vm((4, 64, LANES), F32),
                vm((4, 4, 64, LANES), BF16),
                vm((4, 4, 64, LANES), BF16),
                vm((2, 8, LANES), jnp.int32),
                vm((2, 8, LANES), jnp.int32),
                vm((ELEMS, FIELDS, 512), F32),
                vm((2, 2, FIELDS, 512), F32),
                vm((2, 2, FIELDS, 512), F32),
                vm((2, 3 * LANES, LANES), BF16),
                vm((2, 3 * LANES, LANES), BF16),
                vm((4, 272, LANES), BF16),
                vm((4, 272, LANES), BF16),
                vm((4, 64, LANES), F32),
                vm((4, 64, LANES), F32),
                vm((4, 16, LANES), BF16),
                vm((4, 16, LANES), BF16),
                vm((2, 3, 64, LANES), BF16),
                vm((4, 64, LANES), F32),
                vm((LANES, LANES), F32),
                sm((HOLD7,), jnp.int32),
                dma((15,)),
                dma((4, 4)),
                dma((4, 4)),
                dma((2,)),
                dma((2,)),
                dma((2,)),
                dma((2,)),
                dma((2,)),
                dma((2,)),
                dma((2, 3)),
                dma((2, 3)),
                dma((2, 4)),
                dma((2, 4)),
                dma((4,)),
                dma((4,)),
            ],
            compiler_params=pltpu.CompilerParams(
                collective_id=0, has_side_effects=True, vmem_limit_bytes=62 * 2**20
            ),
        )(*operands)
        return pl.pallas_call(
            store_kernel,
            out_shape=(
                jax.ShapeDtypeStruct((HOLD7, FIELDS, 512), F32),
                jax.ShapeDtypeStruct((ELEMS, 512), F32),
            ),
            in_specs=[pl.BlockSpec(memory_space=pl.ANY)] * 2,
            out_specs=[pl.BlockSpec(memory_space=pltpu.HBM)] * 2,
            scratch_shapes=[dma((2,))],
            compiler_params=pltpu.CompilerParams(vmem_limit_bytes=2**20),
        )(*held)

    return jax.shard_map(
        per_device,
        mesh=mesh,
        in_specs=(
            P(("slab", "curve"), None, None),
            P(None, None, ("slab", "curve")),
            P(("slab", "curve")),
            P(),
            P(("slab", "curve"), None),
            P(("slab", "curve")),
            P(("slab", "curve")),
        ),
        out_specs=(P(("slab", "curve"), None, None), P(("slab", "curve"), None)),
        check_vma=False,
    )
```

```python
import functools

import jax
import jax.numpy as jnp
import ml_dtypes
import numpy as np
from jax import lax
from jax.experimental import pallas as pl
from jax.experimental.pallas import tpu as pltpu
from jax.sharding import PartitionSpec as P

P7 = 8
P3 = 4
ELEMS = 16
FIELDS = 8
LANES = ELEMS * FIELDS
HOLD7 = 12
STEP = 0.002
ACTIVATION = 1.5
MESH = pl.DeviceIdType.MESH
F32 = jnp.float32
BF16 = jnp.bfloat16


def lobatto_points(number):
    return -np.cos(np.pi * np.arange(number) / (number - 1))


def derivative_matrix(points):
    number = points.shape[0]
    weights = np.ones(number)
    for row in range(number):
        for col in range(number):
            if col != row:
                weights[row] = weights[row] / (points[row] - points[col])
    matrix = np.zeros((number, number))
    for row in range(number):
        for col in range(number):
            if col != row:
                matrix[row, col] = weights[col] / weights[row] / (points[row] - points[col])
        matrix[row, row] = -np.sum(matrix[row])
    return matrix


def interpolation_matrix(source, target):
    matrix = np.ones((target.shape[0], source.shape[0]))
    for col in range(source.shape[0]):
        for other in range(source.shape[0]):
            if other != col:
                matrix[:, col] = (
                    matrix[:, col] * (target - source[other]) / (source[col] - source[other])
                )
    return matrix


def kron3(a, b, c):
    return np.kron(a, np.kron(b, c))


def to_bf16(matrix):
    return np.asarray(matrix, np.float32).astype(ml_dtypes.bfloat16)


def split_columns(matrix):
    full = np.asarray(matrix, np.float32)
    high = full.astype(ml_dtypes.bfloat16)
    low = (full - high.astype(np.float32)).astype(ml_dtypes.bfloat16)
    return np.concatenate([high, low, high], axis=1)


def face_selectors(extent):
    ident = np.eye(extent)
    first, last = ident[:1], ident[-1:]
    picks = []
    for end in (first, last):
        picks.append(kron3(end, ident, ident))
    for end in (first, last):
        picks.append(kron3(ident, end, ident))
    for end in (first, last):
        picks.append(kron3(ident, ident, end))
    return np.stack(picks)


def make_tables():
    r7, r3 = lobatto_points(P7), lobatto_points(P3)
    d7, d3 = derivative_matrix(r7), derivative_matrix(r3)
    down = interpolation_matrix(r7, r3)
    up = interpolation_matrix(r3, r7)
    i7, i3 = np.eye(P7), np.eye(P3)
    div_i = np.kron(d7, np.eye(32))
    two = np.eye(2)
    div_jk = np.concatenate([np.kron(two, np.kron(d7, i7)), np.kron(two, np.kron(i7, d7))], axis=1)
    fine = to_bf16(np.concatenate([div_i, div_jk], axis=0))
    lift = to_bf16(kron3(up, up, up))
    project = split_columns(kron3(down, down, down))
    mortar_up = np.asarray(np.kron(up, up), np.float32).astype(np.float64)
    mortar_down = np.asarray(np.kron(down, down), np.float32).astype(np.float64)
    selectors = face_selectors(P3)
    raise_all = np.concatenate([mortar_up @ selectors[side] for side in range(6)], axis=0)
    lower_all = np.concatenate([selectors[side].T @ mortar_down for side in range(6)], axis=1)
    lower_all = STEP * (P3 * (P3 - 1) / 2.0) * lower_all
    raise_faces = split_columns(raise_all)
    lower_faces = split_columns(lower_all)
    project_all = np.asarray(kron3(down, down, down), np.float32).astype(np.float64)
    fine_selectors = face_selectors(P7)
    project_late = np.concatenate(
        [project_all @ fine_selectors[side].T for side in (0, 1, 4, 5)], axis=1
    )
    lower_late = np.concatenate([lower_all[:, :128], lower_all[:, 256:]], axis=1)
    late_raise = to_bf16(np.concatenate([raise_all @ project_late, raise_all @ lower_late], axis=0))
    late_nodes = split_columns(np.concatenate([project_late, lower_late], axis=0))
    coarse = to_bf16(
        np.concatenate([kron3(d3, i3, i3), kron3(i3, d3, i3), kron3(i3, i3, d3)], axis=1)
    )
    return fine, lift, project, raise_faces, lower_faces, coarse, late_raise, late_nodes


def dot(a, b):
    return jnp.dot(a, b, preferred_element_type=F32)


def split_rows(value):
    high = value.astype(BF16)
    low = (value - high.astype(F32)).astype(BF16)
    return jnp.concatenate([high, high, low], axis=0)


def face_slices(side):
    dim, end = side // 2, side % 2
    if dim == 0:
        return [pl.ds(448 * end, 64)]
    if dim == 1:
        return [pl.ds(i * 64 + 56 * end, 8) for i in range(P7)]
    return [pl.ds(7 * end, 64, stride=8)]


def face_get(ref, side):
    parts = [ref[where, :] for where in face_slices(side)]
    return parts[0] if len(parts) == 1 else jnp.concatenate(parts, axis=0)


def face_add(ref, side, value):
    start = 0
    for where in face_slices(side):
        ref[where, :] += value[start : start + where.size]
        start += where.size


def edge_slice(x_end, z_end):
    return pl.ds(448 * x_end + 7 * z_end, P7, stride=8)


def kernel(
    slabs,
    pieces,
    state_h,
    vel_h,
    nbr_h,
    pre_h,
    stoich_h,
    switch_h,
    owner_h,
    fine_h,
    lift_h,
    project_h,
    raise_h,
    lower_h,
    coarse_h,
    late_raise_h,
    late_nodes_h,
    out7_v,
    out3_v,
    state_v,
    vel_v,
    nbr_v,
    pre_s,
    stoich_s,
    switch_s,
    owner_s,
    fine_v,
    lift_v,
    project_v,
    raise_v,
    lower_v,
    coarse_v,
    late_raise_v,
    late_nodes_v,
    u0,
    u1,
    u2,
    u3,
    speed,
    coef,
    vel_rep,
    vmin,
    perm_far,
    perm_near,
    local_nb,
    send,
    recv,
    count_send,
    count_recv,
    home,
    move_send,
    move_recv,
    early_send,
    early_recv,
    wide_send,
    wide_recv,
    far_trace,
    next_near,
    corner_send,
    corner_recv,
    extra_recv,
    move_coef,
    turned,
    home_list,
    load_sem,
    send_sem,
    recv_sem,
    count_ssem,
    count_rsem,
    move_ssem,
    move_rsem,
    early_ssem,
    early_rsem,
    extra_ssem,
    extra_rsem,
    wide_ssem,
    wide_rsem,
    corner_ssem,
    corner_rsem,
):
    slab, pos = lax.axis_index("slab"), lax.axis_index("curve")
    left, right = lax.rem(pos + pieces - 1, pieces), lax.rem(pos + 1, pieces)
    below, above = lax.rem(slab + slabs - 1, slabs), lax.rem(slab + 1, slabs)
    partner = {0: (slab, left), 1: (slab, right), 4: (below, pos), 5: (above, pos)}

    barrier = pltpu.get_barrier_semaphore()
    corners = [(below, left), (below, right), (above, left), (above, right)]
    for device in corners + list(partner.values()):
        pl.semaphore_signal(barrier, inc=1, device_id=device, device_id_type=MESH)

    pairs = [
        (state_h, state_v),
        (vel_h, vel_v),
        (nbr_h, nbr_v),
        (lift_h, lift_v),
        (pre_h, pre_s),
        (stoich_h, stoich_s),
        (switch_h, switch_s),
        (owner_h, owner_s),
        (fine_h, fine_v),
        (raise_h, raise_v),
        (project_h, project_v),
        (lower_h, lower_v),
        (coarse_h, coarse_v),
        (late_raise_h, late_raise_v),
        (late_nodes_h, late_nodes_v),
    ]
    loads = [
        pltpu.make_async_copy(source, target, load_sem.at[number])
        for number, (source, target) in enumerate(pairs)
    ]
    for number in (0, 2, 1, 3, 8, 4, 5, 6, 7):
        loads[number].start()

    lane_row = lax.broadcasted_iota(jnp.int32, (1, LANES), 1)
    lane_elem = lane_row // FIELDS
    lane_field = lane_row % FIELDS
    lanes = lax.broadcasted_iota(jnp.int32, (LANES, LANES), 1)
    rows = lax.broadcasted_iota(jnp.int32, (LANES, LANES), 0)
    spread = (
        lax.broadcasted_iota(jnp.int32, (ELEMS, LANES), 0)
        == lax.broadcasted_iota(jnp.int32, (ELEMS, LANES), 1) // FIELDS
    ).astype(F32)
    rep = ((rows % FIELDS == 0) & (rows // FIELDS == lanes // FIELDS)).astype(F32).astype(BF16)
    rep2 = jnp.concatenate([rep, rep], axis=0)

    loads[0].wait()
    for load in loads[9:]:
        load.start()
    u0[...] = jnp.transpose(state_v[...].reshape(LANES, 512))

    loads[2].wait()
    ids = nbr_v[...]
    me = slab * pieces + pos
    here = lax.shift_right_logical(ids, 4) == me
    code = jnp.where(here, ids & 15, (ids & 15) + 16).astype(F32)
    spread_t = (
        lax.broadcasted_iota(jnp.int32, (LANES, ELEMS), 1)
        == lax.broadcasted_iota(jnp.int32, (LANES, ELEMS), 0) // FIELDS
    ).astype(F32)
    target = lax.dot_general(
        spread_t.astype(BF16),
        code.astype(BF16),
        (((1,), (1,)), ((), ())),
        preferred_element_type=F32,
    )
    target = target.astype(jnp.int32) * FIELDS
    target = target + lax.broadcasted_iota(jnp.int32, (LANES, 6), 0) % FIELDS
    for side in range(6):
        column = target[:, side : side + 1]
        near = (column == lanes).astype(F32).astype(BF16)
        far = (column == lanes + LANES).astype(F32).astype(BF16)
        if side < 2:
            perm_far[side] = far
            perm_near[side] = near
        elif side < 4:
            perm_near[side] = near
        else:
            perm_far[side - 2] = far

    def launch(number, side, trace):
        slot = side if side < 2 else side - 2
        send[number, slot] = dot(trace, perm_far[slot]).astype(BF16)
        copy = pltpu.make_async_remote_copy(
            src_ref=send.at[number, slot],
            dst_ref=recv.at[number, slot ^ 1],
            send_sem=send_sem.at[number, slot],
            recv_sem=recv_sem.at[number, slot ^ 1],
            device_id=partner[side],
            device_id_type=MESH,
        )
        copy.start()
        started.append(copy)
        arrivals[number, side ^ 1] = copy

    def gather_local(traces):
        for side in range(4):
            local_nb[side ^ 1] = dot(traces[side], perm_near[side])

    started, arrivals = [], {}

    def fine_trace(ref, side):
        return face_get(ref, side).astype(BF16)

    traces = [fine_trace(u0, side) for side in range(6)]
    gather_local(traces)

    loads[1].wait()
    loads[3].wait()
    for dim in range(3):
        spread_vel = lax.dot_general(
            vel_v[dim],
            spread.astype(BF16),
            (((0,), (0,)), ((), ())),
            preferred_element_type=F32,
        ).astype(BF16)
        vel_rep[dim * 64 : dim * 64 + 64] = spread_vel.astype(F32)
        speed[dim] = dot(lift_v[...], spread_vel).astype(BF16).astype(F32)
        for end in range(2):
            side = 2 * dim + end
            normal = face_get(speed.at[dim], side)
            lift_coef = STEP * (P7 * (P7 - 1) / 2.0)
            coef[side] = lift_coef * jnp.minimum(normal if end else -normal, 0.0)

    loads[4].wait()
    loads[5].wait()
    pre_row = jnp.zeros((1, LANES), F32)
    stoich_row = jnp.zeros((1, LANES), F32)
    for elem in range(ELEMS):
        pre_row = jnp.where(lane_elem == elem, pre_s[elem], pre_row)
    for field in range(FIELDS):
        stoich_row = jnp.where(lane_field == field, stoich_s[field], stoich_row)

    def source(u):
        rate = (
            pre_row
            * jnp.exp(-ACTIVATION * jnp.exp(-u))
            * pltpu.roll(u, LANES - 1, 1)
            * pltpu.roll(u, LANES - 2, 1)
        )
        high = rate.astype(BF16)
        low = (rate - high.astype(F32)).astype(BF16)
        return stoich_row * dot(jnp.concatenate([high, low], axis=1), rep2)

    loads[8].wait()

    def fine_start(ref, start, out, traces):
        scale = 1.0 if start is None else 0.5
        along_i = []
        for half in range(2):
            parts = []
            for i in range(P7):
                at = pl.ds(i * 64 + half * 32, 32)
                parts.append((speed[0, at, :] * ref[at, :]).astype(BF16))
            along_i.append(dot(fine_v[:256, :], jnp.concatenate(parts, axis=0)))
        for block in range(4):
            at = pl.ds(block * 128, 128)
            u = ref[at, :]
            flux = jnp.concatenate(
                [(speed[1, at, :] * u).astype(BF16), (speed[2, at, :] * u).astype(BF16)], axis=0
            )
            div = dot(fine_v[256:, :], flux) + jnp.concatenate(
                [
                    along_i[half][i * 32 : i * 32 + 32]
                    for i in (2 * block, 2 * block + 1)
                    for half in range(2)
                ],
                axis=0,
            )
            rate = STEP * (source(u) - div)
            out[at, :] = u + rate if start is None else 0.5 * (start[at, :] + u + rate)
        for side in range(6):
            jump = traces[side].astype(F32)
            if side < 4:
                jump = jump - local_nb[side]
            face_add(out, side, scale * (coef[side] * jump))

    def late_term(number, side, scale):
        slot = side if side < 2 else side - 2
        arrivals[number, side].wait_recv()
        return scale * (coef[side] * recv[number, slot].astype(F32))

    def fine_end_z(number, scale, out):
        for side in (4, 5):
            face_add(out, side, -late_term(number, side, scale))

    def fine_end_x(number, scale, out):
        for side in (0, 1):
            face_add(out, side, -late_term(number, side, scale))

    def coarse_start(c, start):
        flux = jnp.concatenate(
            [(vel_rep[dim * 64 : dim * 64 + 64] * c).astype(BF16) for dim in range(3)], axis=0
        )
        rate = STEP * (source(c) - dot(coarse_v[...], flux))
        return c + rate if start is None else 0.5 * (start + c + rate)

    def coarse_local(own, scale, partial):
        jumps = []
        for side in range(6):
            jump = own[side * 64 : side * 64 + 64].astype(F32)
            if side < 4:
                jump = jump - local_nb[side]
            jumps.append(vmin[side * 64 : side * 64 + 64] * jump)
        return partial + scale * dot(lower_v[...], split_rows(jnp.concatenate(jumps, axis=0)))

    def coarse_late(number):
        terms = []
        for slot, side in enumerate((0, 1, 4, 5)):
            terms.append(vmin[side * 64 : side * 64 + 64] * recv[number, slot].astype(F32))
        return jnp.concatenate(terms, axis=0)

    def launch_mixed(number, fine, raised_base, first_row, late, order, after=None):
        late = late.astype(BF16)
        own, traces = [None] * 6, [None] * 6
        for sides in order:
            at = slice(sides[0] * 64, sides[0] * 64 + 128)
            raised = raised_base[at] - dot(
                late_raise_v[pl.ds(first_row + sides[0] * 64, 128), :], late
            )
            for place, side in enumerate(sides):
                own[side] = raised[place * 64 : place * 64 + 64]
                traces[side] = fine_trace(fine, side)
                mixed = jnp.where(is_switched, own[side], traces[side].astype(F32)).astype(BF16)
                if side in (2, 3):
                    mixes[side] = mixed
                else:
                    launch(number, side, mixed)
                    mixes[side] = mixed
            if after is not None:
                after(sides)
        return traces, jnp.concatenate(own, axis=0).astype(BF16)

    mixes = [None] * 6

    fine_start(u0, None, u1, traces)
    for side in (0, 1, 4, 5):
        slot, dim, end = side if side < 2 else side - 2, side // 2, side % 2
        edges = [(end, 0), (end, 1)] if dim == 0 else [(0, end), (1, end)]
        first = face_get(u1, side)
        high = first.astype(BF16)
        packed = [
            traces[side],
            face_get(speed.at[dim], side).astype(BF16),
            jnp.concatenate([speed[2 - dim, edge_slice(*edge), :] for edge in edges], axis=0).astype(BF16),
            high,
            (first - high.astype(F32)).astype(BF16),
        ]
        placed = dot(jnp.concatenate(packed, axis=0), perm_far[slot])
        wide_send[slot] = placed.astype(BF16)
        far_trace[slot] = placed[:64]
    for number, corner in enumerate(corners):
        z_end, x_end = number // 2, number % 2
        corner_send[number] = jnp.concatenate(
            [
                far_trace[x_end, pl.ds(7 * z_end, P7, stride=8), :],
                far_trace[2 + z_end, pl.ds(56 * x_end, P7), :],
            ],
            axis=0,
        ).astype(BF16)
    pl.semaphore_wait(barrier, 8)
    for number, corner in enumerate(corners):
        copy = pltpu.make_async_remote_copy(
            src_ref=corner_send.at[number],
            dst_ref=corner_recv.at[3 - number],
            send_sem=corner_ssem.at[number],
            recv_sem=corner_rsem.at[3 - number],
            device_id=corner,
            device_id_type=MESH,
        )
        copy.start()
        started.append(copy)
        arrivals["corner", 3 - number] = copy
    for part, (start_row, count) in enumerate(((0, 144), (144, 128))):
        for side in (0, 1, 4, 5):
            slot = side if side < 2 else side - 2
            at = pl.ds(start_row, count)
            copy = pltpu.make_async_remote_copy(
                src_ref=wide_send.at[slot, at],
                dst_ref=wide_recv.at[slot ^ 1, at],
                send_sem=wide_ssem.at[part, slot],
                recv_sem=wide_rsem.at[part, slot ^ 1],
                device_id=partner[side],
                device_id_type=MESH,
            )
            copy.start()
            started.append(copy)
            arrivals["wide", part, side ^ 1] = copy

    loads[6].wait()
    loads[7].wait()
    left_count = right_count = home_count = jnp.int32(0)
    left_pick = [jnp.int32(0)] * 2
    right_pick = [jnp.int32(0)] * 2
    home_pick = [jnp.int32(0)] * HOLD7
    switch_row = jnp.zeros((1, LANES), F32)
    for elem in range(ELEMS):
        switched = switch_s[elem]
        owner = owner_s[elem]
        switch_row = jnp.where(lane_elem == elem, switched.astype(F32), switch_row)
        fine_one = switched != 1
        goes_left = fine_one & (owner == left)
        goes_right = fine_one & (owner == right)
        stays = fine_one & jnp.logical_not(owner == left) & jnp.logical_not(owner == right)
        for slot in range(2):
            left_pick[slot] = jnp.where(goes_left & (left_count == slot), elem, left_pick[slot])
            right_pick[slot] = jnp.where(goes_right & (right_count == slot), elem, right_pick[slot])
        for slot in range(min(elem + 1, HOLD7)):
            home_pick[slot] = jnp.where(stays & (home_count == slot), elem, home_pick[slot])
        left_count = left_count + goes_left.astype(jnp.int32)
        right_count = right_count + goes_right.astype(jnp.int32)
        home_count = home_count + stays.astype(jnp.int32)
    for slot in range(HOLD7):
        home_list[slot] = home_pick[slot]
    count_arrivals = []
    count_send[0] = jnp.full((8, LANES), left_count, jnp.int32)
    count_send[1] = jnp.full((8, LANES), right_count, jnp.int32)
    for side in (0, 1):
        copy = pltpu.make_async_remote_copy(
            src_ref=count_send.at[side],
            dst_ref=count_recv.at[side ^ 1],
            send_sem=count_ssem.at[side],
            recv_sem=count_rsem.at[side ^ 1],
            device_id=partner[side],
            device_id_type=MESH,
        )
        copy.start()
        started.append(copy)
        count_arrivals.append(copy)
    is_switched = switch_row > 0.5

    for side, picks, count in ((0, left_pick, left_count), (1, right_pick, right_count)):
        chosen = jnp.zeros((LANES, LANES), F32)
        for slot in range(2):
            place = lanes // FIELDS == 2 * (1 - side) + slot
            source_row = rows - (lanes % FIELDS) == picks[slot] * FIELDS
            chosen = jnp.where(place & source_row & (count > slot), 1.0, chosen)
        chosen = chosen.astype(BF16)
        early_send[side, :LANES] = chosen
        normals = jnp.concatenate(
            [face_get(speed.at[other // 2], other).astype(BF16) for other in (0, 1, 4, 5)], axis=0
        )
        early_send[side, LANES:] = dot(normals, chosen).astype(BF16)
        copy = pltpu.make_async_remote_copy(
            src_ref=early_send.at[side],
            dst_ref=early_recv.at[side ^ 1],
            send_sem=early_ssem.at[side],
            recv_sem=early_rsem.at[side ^ 1],
            device_id=partner[side],
            device_id_type=MESH,
        )
        copy.start()
        started.append(copy)
        count_arrivals.append(copy)

    for load in loads[9:]:
        load.wait()
    for dim in range(3):
        spread_vel = vel_rep[dim * 64 : dim * 64 + 64].astype(BF16)
        mortar = dot(
            raise_v[dim * 128 : dim * 128 + 128, :128],
            jnp.concatenate([spread_vel, spread_vel], axis=0),
        )
        vmin[dim * 128 : dim * 128 + 64] = jnp.minimum(-mortar[:64], 0.0)
        vmin[dim * 128 + 64 : dim * 128 + 128] = jnp.minimum(mortar[64:], 0.0)

    for side in (4, 5, 0, 1):
        slot = side if side < 2 else side - 2
        arrivals["wide", 0, side].wait_recv()
        face_add(u1, side, -(coef[side] * wide_recv[slot, pl.ds(0, 64), :].astype(F32)))
    next_traces = [fine_trace(u1, side) for side in range(6)]
    gather_local(next_traces)
    fine_start(u1, u0, u2, next_traces)
    c0 = dot(project_v[...], split_rows(u2[...]))
    raised = dot(raise_v[...], split_rows(c0))

    lift_coef = STEP * (P7 * (P7 - 1) / 2.0)
    edge_coef = {}
    for side in (0, 1, 4, 5):
        slot, end = side if side < 2 else side - 2, side % 2
        normal = wide_recv[slot, pl.ds(64, 64), :].astype(F32)
        normal = -normal if end else normal
        next_near[slot] = lift_coef * jnp.minimum(normal, 0.0) * traces[side].astype(F32)
        edge = wide_recv[slot, pl.ds(128, 16), :].astype(F32)
        edge_coef[side] = [
            lift_coef * jnp.minimum(-edge[:8], 0.0),
            lift_coef * jnp.minimum(edge[8:], 0.0),
        ]
    for side in (4, 5, 0, 1):
        slot = side if side < 2 else side - 2
        arrivals["wide", 1, side].wait_recv()
        got = wide_recv[slot, pl.ds(144, 128), :].astype(F32)
        next_near[slot] = got[:64] + got[64:] - next_near[slot]
    for number in range(4):
        arrivals["corner", number].wait_recv()
    corner_values = [corner_recv[number].astype(F32) for number in range(4)]
    late = []
    for side in (0, 1, 4, 5):
        slot, dim, end = side if side < 2 else side - 2, side // 2, side % 2
        if dim == 0:
            around = [corner_values[end][8:16], corner_values[2 + end][8:16]]
        else:
            around = [corner_values[2 * end][0:8], corner_values[2 * end + 1][0:8]]
        around = lax.dot_general(
            jnp.concatenate(around, axis=0).astype(BF16),
            perm_far[slot],
            (((1,), (1,)), ((), ())),
            preferred_element_type=F32,
        )
        for which in range(2):
            term = edge_coef[side][which] * around[8 * which : 8 * which + 8]
            at = pl.ds(7 * which, P7, stride=8) if dim == 0 else pl.ds(56 * which, P7)
            next_near[slot, at, :] -= term
        late.append(0.5 * (coef[side] * next_near[slot].astype(BF16).astype(F32)))
    for place, side in enumerate((0, 1, 4, 5)):
        face_add(u2, side, -late[place])
    late = jnp.concatenate(late, axis=0)

    traces, own = launch_mixed(
        2, u2, raised, 0, late, ((0, 1), (4, 5), (2, 3))
    )
    gather_local(mixes)
    c0 = c0 - dot(late_nodes_v[:64, :], split_rows(late))
    fine_start(u2, None, u3, traces)
    partial = coarse_start(c0, None)
    for copy in count_arrivals:
        copy.wait_recv()
    for place, side in enumerate((0, 1, 4, 5)):
        at = pl.ds(LANES + 64 * place, 64)
        normal = early_recv[0, at, :].astype(F32) + early_recv[1, at, :].astype(F32)
        lift_coef = 0.5 * STEP * (P7 * (P7 - 1) / 2.0)
        move_coef[place] = lift_coef * jnp.minimum(normal if side % 2 else -normal, 0.0)
    c1 = coarse_local(own, 1.0, partial)
    raised = dot(raise_v[...], split_rows(c1))
    fine_end_z(2, 1.0, u3)
    fine_end_x(2, 1.0, u3)
    late = coarse_late(2)

    left2, right2 = lax.rem(pos + pieces - 2, pieces), lax.rem(pos + 2, pieces)
    extras = {
        (1, 1): (2, (below, right)),
        (1, 2): (3, (above, right)),
        (0, 1): (2, (below, left)),
        (0, 2): (3, (above, left)),
        (0, 0): (0, (slab, left2)),
        (1, 0): (1, (slab, right2)),
    }
    extra_copies = []

    def launch_extras(sides):
        for (toward, kind), (slot, device) in extras.items():
            if (kind == 0) != (0 in sides) or 2 in sides:
                continue
            place = 3 - kind if kind else 0
            copy = pltpu.make_async_remote_copy(
                src_ref=send.at[3, slot],
                dst_ref=extra_recv.at[1 - toward, place],
                send_sem=extra_ssem.at[toward, kind],
                recv_sem=extra_rsem.at[1 - toward, place],
                device_id=device,
                device_id_type=MESH,
            )
            copy.start()
            started.append(copy)
            extra_copies.append(copy)

    earlier = list(started)
    started.clear()
    traces, own = launch_mixed(
        3, u3, raised, 384, late, ((4, 5), (0, 1), (2, 3)), launch_extras
    )
    gather_local(mixes)
    fine_start(u3, u2, u1, traces)

    def turn_home():
        for number in range(4):
            home[:, :, number * 128 : number * 128 + 128] = jnp.transpose(
                u1[number * 128 : number * 128 + 128, :]
            ).reshape(ELEMS, FIELDS, 128)

    turn_home()
    for side in range(2):
        for slot in range(2):
            pick = (left_pick, right_pick)[side][slot]
            move_send[side, slot] = home[pick]
        copy = pltpu.make_async_remote_copy(
            src_ref=move_send.at[side],
            dst_ref=move_recv.at[side ^ 1],
            send_sem=move_ssem.at[side],
            recv_sem=move_rsem.at[side ^ 1],
            device_id=partner[side],
            device_id_type=MESH,
        )
        copy.start()
        started.append(copy)
        extra_copies.append(copy)
    c1 = c1 - dot(late_nodes_v[64:, :], split_rows(late))
    partial = coarse_start(c1, c0)
    u3[...] = jnp.zeros_like(u3)
    for copy in earlier:
        copy.wait_send()
    c2 = coarse_local(own, 0.5, partial)
    fine_end_z(3, 0.5, u1)
    fine_end_x(3, 0.5, u1)
    c2 = c2 - 0.5 * dot(late_nodes_v[64:, :], split_rows(coarse_late(3)))

    c2 = jnp.where(is_switched, c2, 0.0)
    turned[...] = jnp.transpose(jnp.concatenate([c2, pltpu.roll(c2, LANES - 1, 1)], axis=0))
    for pair in range(4):
        out3_v[:, pair * 128 : pair * 128 + 128] = turned[pl.ds(2 * pair, ELEMS, stride=FIELDS), :]
    turn_home()

    from_left = jnp.minimum(count_recv[0][0, 0], 2)
    from_right = jnp.minimum(count_recv[1][0, 0], 2)
    is_first, is_last = pos == 0, pos == pieces - 1
    at_left = jnp.where(is_first, home_count + from_right, jnp.where(is_last, from_right, 0))
    at_home = jnp.where(is_first, 0, jnp.where(is_last, from_right + from_left, from_left))
    at_right = jnp.where(is_first, home_count, jnp.where(is_last, 0, from_left + home_count))
    picks = []
    for slot in range(HOLD7):
        rank = slot - at_home
        stay = (rank >= 0) & (rank < home_count)
        value = home[home_list[jnp.clip(rank, 0, HOLD7 - 1)]]
        out7_v[slot] = jnp.where(stay, value, 0.0)
        rank_left, rank_right = slot - at_left, slot - at_right
        is_left = (rank_left >= 0) & (rank_left < from_left)
        is_right = (rank_right >= 0) & (rank_right < from_right)
        pick = jnp.where(is_left, rank_left, jnp.where(is_right, 2 + rank_right, 0))
        picks.append((is_left | is_right, pick))
    for copy in extra_copies:
        copy.wait_recv()
    chosen = jnp.concatenate([early_recv[0, :LANES, :], early_recv[1, :LANES, :]], axis=0)
    nears = {
        0: (extra_recv[0, 0], send[3, 1]),
        1: (send[3, 0], extra_recv[1, 0]),
        4: (extra_recv[0, 1], extra_recv[1, 1]),
        5: (extra_recv[0, 2], extra_recv[1, 2]),
    }
    for place, side in enumerate((0, 1, 4, 5)):
        near = dot(jnp.concatenate(nears[side], axis=1), chosen)
        face_add(u3, side, -(move_coef[place] * near))
    for number in range(4):
        moved = jnp.transpose(u3[number * 128 : number * 128 + 128, :])
        at = pl.ds(number * 128, 128)
        for pick in range(4):
            move_recv[pick // 2, pick % 2, :, at] += moved[pick * FIELDS : pick * FIELDS + FIELDS]
    for slot in range(HOLD7):
        arrived, pick = picks[slot]
        value = move_recv[pick // 2, pick % 2]
        out7_v[slot] = jnp.where(arrived, value, out7_v[slot])
    for copy in started:
        copy.wait_send()


def store_kernel(held7, held3, out7, out3, sem):
    copies = [
        pltpu.make_async_copy(held7, out7, sem.at[0]),
        pltpu.make_async_copy(held3, out3, sem.at[1]),
    ]
    for copy in copies:
        copy.start()
    for copy in copies:
        copy.wait()


def solution(mesh):
    slabs, pieces = mesh.shape["slab"], mesh.shape["curve"]
    tables = make_tables()

    def per_device(state, velocity, pre_exp, stoich, neighbours, switch, new_owner):
        velocity = jnp.transpose(velocity, (0, 2, 1))
        neighbours = jnp.transpose(neighbours)
        operands = (state, velocity, neighbours, pre_exp, stoich, switch, new_owner) + tuple(
            jnp.asarray(table) for table in tables
        )
        vm, sm, dma = pltpu.VMEM, pltpu.SMEM, pltpu.SemaphoreType.DMA
        nodes = (512, LANES)
        held = pl.pallas_call(
            functools.partial(kernel, slabs, pieces),
            out_shape=(
                pltpu.VMEM((HOLD7, FIELDS, 512), F32),
                pltpu.VMEM((ELEMS, 512), F32),
            ),
            in_specs=[pl.BlockSpec(memory_space=pltpu.HBM)] * len(operands),
            out_specs=[pl.BlockSpec(memory_space=pltpu.VMEM)] * 2,
            scratch_shapes=[
                vm((ELEMS, FIELDS, 512), F32),
                vm((3, ELEMS, 64), BF16),
                vm((6, ELEMS), jnp.int32),
                sm((ELEMS,), F32),
                sm((FIELDS,), F32),
                sm((ELEMS,), jnp.int32),
                sm((ELEMS,), jnp.int32),
            ]
            + [vm(table.shape, BF16) for table in tables]
            + [
                vm(nodes, F32),
                vm(nodes, F32),
                vm(nodes, F32),
                vm(nodes, F32),
                vm((3, 512, LANES), F32),
                vm((6, 64, LANES), F32),
                vm((192, LANES), F32),
                vm((384, LANES), F32),
                vm((4, LANES, LANES), BF16),
                vm((4, LANES, LANES), BF16),
                vm((4, 64, LANES), F32),
                vm((4, 4, 64, LANES), BF16),
                vm((4, 4, 64, LANES), BF16),
                vm((2, 8, LANES), jnp.int32),
                vm((2, 8, LANES), jnp.int32),
                vm((ELEMS, FIELDS, 512), F32),
                vm((2, 2, FIELDS, 512), F32),
                vm((2, 2, FIELDS, 512), F32),
                vm((2, 3 * LANES, LANES), BF16),
                vm((2, 3 * LANES, LANES), BF16),
                vm((4, 272, LANES), BF16),
                vm((4, 272, LANES), BF16),
                vm((4, 64, LANES), F32),
                vm((4, 64, LANES), F32),
                vm((4, 16, LANES), BF16),
                vm((4, 16, LANES), BF16),
                vm((2, 3, 64, LANES), BF16),
                vm((4, 64, LANES), F32),
                vm((LANES, LANES), F32),
                sm((HOLD7,), jnp.int32),
                dma((15,)),
                dma((4, 4)),
                dma((4, 4)),
                dma((2,)),
                dma((2,)),
                dma((2,)),
                dma((2,)),
                dma((2,)),
                dma((2,)),
                dma((2, 3)),
                dma((2, 3)),
                dma((2, 4)),
                dma((2, 4)),
                dma((4,)),
                dma((4,)),
            ],
            compiler_params=pltpu.CompilerParams(
                collective_id=0, has_side_effects=True, vmem_limit_bytes=62 * 2**20
            ),
        )(*operands)
        return pl.pallas_call(
            store_kernel,
            out_shape=(
                jax.ShapeDtypeStruct((HOLD7, FIELDS, 512), F32),
                jax.ShapeDtypeStruct((ELEMS, 512), F32),
            ),
            in_specs=[pl.BlockSpec(memory_space=pl.ANY)] * 2,
            out_specs=[pl.BlockSpec(memory_space=pltpu.HBM)] * 2,
            scratch_shapes=[dma((2,))],
            compiler_params=pltpu.CompilerParams(vmem_limit_bytes=2**20),
        )(*held)

    return jax.shard_map(
        per_device,
        mesh=mesh,
        in_specs=(
            P(("slab", "curve"), None, None),
            P(None, None, ("slab", "curve")),
            P(("slab", "curve")),
            P(),
            P(("slab", "curve"), None),
            P(("slab", "curve")),
            P(("slab", "curve")),
        ),
        out_specs=(P(("slab", "curve"), None, None), P(("slab", "curve"), None)),
        check_vma=False,
    )
```

```python
import functools

import jax
import jax.numpy as jnp
import ml_dtypes
import numpy as np
from jax import lax
from jax.experimental import pallas as pl
from jax.experimental.pallas import tpu as pltpu
from jax.sharding import PartitionSpec as P

P7 = 8
P3 = 4
ELEMS = 16
FIELDS = 8
LANES = ELEMS * FIELDS
HOLD7 = 12
STEP = 0.002
ACTIVATION = 1.5
MESH = pl.DeviceIdType.MESH
F32 = jnp.float32
BF16 = jnp.bfloat16


def lobatto_points(number):
    return -np.cos(np.pi * np.arange(number) / (number - 1))


def derivative_matrix(points):
    number = points.shape[0]
    weights = np.ones(number)
    for row in range(number):
        for col in range(number):
            if col != row:
                weights[row] = weights[row] / (points[row] - points[col])
    matrix = np.zeros((number, number))
    for row in range(number):
        for col in range(number):
            if col != row:
                matrix[row, col] = weights[col] / weights[row] / (points[row] - points[col])
        matrix[row, row] = -np.sum(matrix[row])
    return matrix


def interpolation_matrix(source, target):
    matrix = np.ones((target.shape[0], source.shape[0]))
    for col in range(source.shape[0]):
        for other in range(source.shape[0]):
            if other != col:
                matrix[:, col] = (
                    matrix[:, col] * (target - source[other]) / (source[col] - source[other])
                )
    return matrix


def kron3(a, b, c):
    return np.kron(a, np.kron(b, c))


def to_bf16(matrix):
    return np.asarray(matrix, np.float32).astype(ml_dtypes.bfloat16)


def split_columns(matrix):
    full = np.asarray(matrix, np.float32)
    high = full.astype(ml_dtypes.bfloat16)
    low = (full - high.astype(np.float32)).astype(ml_dtypes.bfloat16)
    return np.concatenate([high, low, high], axis=1)


def face_selectors(extent):
    ident = np.eye(extent)
    first, last = ident[:1], ident[-1:]
    picks = []
    for end in (first, last):
        picks.append(kron3(end, ident, ident))
    for end in (first, last):
        picks.append(kron3(ident, end, ident))
    for end in (first, last):
        picks.append(kron3(ident, ident, end))
    return np.stack(picks)


def make_tables():
    r7, r3 = lobatto_points(P7), lobatto_points(P3)
    d7, d3 = derivative_matrix(r7), derivative_matrix(r3)
    down = interpolation_matrix(r7, r3)
    up = interpolation_matrix(r3, r7)
    i7, i3 = np.eye(P7), np.eye(P3)
    div_i = np.kron(d7, np.eye(32))
    two = np.eye(2)
    div_jk = np.concatenate([np.kron(two, np.kron(d7, i7)), np.kron(two, np.kron(i7, d7))], axis=1)
    fine = to_bf16(np.concatenate([div_i, div_jk], axis=0))
    lift = to_bf16(kron3(up, up, up))
    project = split_columns(kron3(down, down, down))
    mortar_up = np.asarray(np.kron(up, up), np.float32).astype(np.float64)
    mortar_down = np.asarray(np.kron(down, down), np.float32).astype(np.float64)
    selectors = face_selectors(P3)
    raise_all = np.concatenate([mortar_up @ selectors[side] for side in range(6)], axis=0)
    lower_all = np.concatenate([selectors[side].T @ mortar_down for side in range(6)], axis=1)
    lower_all = STEP * (P3 * (P3 - 1) / 2.0) * lower_all
    raise_faces = split_columns(raise_all)
    lower_faces = split_columns(lower_all)
    project_all = np.asarray(kron3(down, down, down), np.float32).astype(np.float64)
    fine_selectors = face_selectors(P7)
    project_late = np.concatenate(
        [project_all @ fine_selectors[side].T for side in (0, 1, 4, 5)], axis=1
    )
    lower_late = np.concatenate([lower_all[:, :128], lower_all[:, 256:]], axis=1)
    late_raise = to_bf16(np.concatenate([raise_all @ project_late, raise_all @ lower_late], axis=0))
    late_nodes = split_columns(np.concatenate([project_late, lower_late], axis=0))
    coarse = to_bf16(
        np.concatenate([kron3(d3, i3, i3), kron3(i3, d3, i3), kron3(i3, i3, d3)], axis=1)
    )
    return fine, lift, project, raise_faces, lower_faces, coarse, late_raise, late_nodes


def dot(a, b):
    return jnp.dot(a, b, preferred_element_type=F32)


def split_rows(value):
    high = value.astype(BF16)
    low = (value - high.astype(F32)).astype(BF16)
    return jnp.concatenate([high, high, low], axis=0)


def face_slices(side):
    dim, end = side // 2, side % 2
    if dim == 0:
        return [pl.ds(448 * end, 64)]
    if dim == 1:
        return [pl.ds(i * 64 + 56 * end, 8) for i in range(P7)]
    return [pl.ds(7 * end, 64, stride=8)]


def face_get(ref, side):
    parts = [ref[where, :] for where in face_slices(side)]
    return parts[0] if len(parts) == 1 else jnp.concatenate(parts, axis=0)


def face_add(ref, side, value):
    start = 0
    for where in face_slices(side):
        ref[where, :] += value[start : start + where.size]
        start += where.size


def edge_slice(x_end, z_end):
    return pl.ds(448 * x_end + 7 * z_end, P7, stride=8)


def kernel(
    slabs,
    pieces,
    state_h,
    vel_h,
    nbr_h,
    pre_h,
    stoich_h,
    switch_h,
    owner_h,
    fine_h,
    lift_h,
    project_h,
    raise_h,
    lower_h,
    coarse_h,
    late_raise_h,
    late_nodes_h,
    out7_v,
    out3_v,
    state_v,
    vel_v,
    nbr_v,
    pre_s,
    stoich_s,
    switch_s,
    owner_s,
    fine_v,
    lift_v,
    project_v,
    raise_v,
    lower_v,
    coarse_v,
    late_raise_v,
    late_nodes_v,
    u0,
    u1,
    u2,
    u3,
    speed,
    coef,
    vel_rep,
    vmin,
    perm_far,
    perm_near,
    origin,
    has_origin,
    local_nb,
    send,
    recv,
    count_send,
    count_recv,
    home,
    move_send,
    move_recv,
    early_send,
    early_recv,
    wide_send,
    wide_recv,
    far_trace,
    next_near,
    corner_send,
    corner_recv,
    extra_recv,
    move_coef,
    turned,
    home_list,
    load_sem,
    send_sem,
    recv_sem,
    count_ssem,
    count_rsem,
    move_ssem,
    move_rsem,
    early_ssem,
    early_rsem,
    extra_ssem,
    extra_rsem,
    wide_ssem,
    wide_rsem,
    corner_ssem,
    corner_rsem,
):
    slab, pos = lax.axis_index("slab"), lax.axis_index("curve")
    left, right = lax.rem(pos + pieces - 1, pieces), lax.rem(pos + 1, pieces)
    below, above = lax.rem(slab + slabs - 1, slabs), lax.rem(slab + 1, slabs)
    partner = {0: (slab, left), 1: (slab, right), 4: (below, pos), 5: (above, pos)}

    barrier = pltpu.get_barrier_semaphore()
    corners = [(below, left), (below, right), (above, left), (above, right)]
    for device in corners + list(partner.values()):
        pl.semaphore_signal(barrier, inc=1, device_id=device, device_id_type=MESH)

    pairs = [
        (state_h, state_v),
        (vel_h, vel_v),
        (nbr_h, nbr_v),
        (lift_h, lift_v),
        (pre_h, pre_s),
        (stoich_h, stoich_s),
        (switch_h, switch_s),
        (owner_h, owner_s),
        (fine_h, fine_v),
        (raise_h, raise_v),
        (project_h, project_v),
        (lower_h, lower_v),
        (coarse_h, coarse_v),
        (late_raise_h, late_raise_v),
        (late_nodes_h, late_nodes_v),
    ]
    loads = [
        pltpu.make_async_copy(source, target, load_sem.at[number])
        for number, (source, target) in enumerate(pairs)
    ]
    for number in (0, 2, 1, 3, 8, 4, 5, 6, 7):
        loads[number].start()

    lane_row = lax.broadcasted_iota(jnp.int32, (1, LANES), 1)
    lane_elem = lane_row // FIELDS
    lane_field = lane_row % FIELDS
    lanes = lax.broadcasted_iota(jnp.int32, (LANES, LANES), 1)
    rows = lax.broadcasted_iota(jnp.int32, (LANES, LANES), 0)
    spread = (
        lax.broadcasted_iota(jnp.int32, (ELEMS, LANES), 0)
        == lax.broadcasted_iota(jnp.int32, (ELEMS, LANES), 1) // FIELDS
    ).astype(F32)
    rep = ((rows % FIELDS == 0) & (rows // FIELDS == lanes // FIELDS)).astype(F32).astype(BF16)
    rep2 = jnp.concatenate([rep, rep], axis=0)

    loads[0].wait()
    for load in loads[9:]:
        load.start()
    u0[...] = jnp.transpose(state_v[...].reshape(LANES, 512))

    loads[2].wait()
    ids = nbr_v[...]
    me = slab * pieces + pos
    here = lax.shift_right_logical(ids, 4) == me
    code = jnp.where(here, ids & 15, (ids & 15) + 16).astype(F32)
    spread_t = (
        lax.broadcasted_iota(jnp.int32, (LANES, ELEMS), 1)
        == lax.broadcasted_iota(jnp.int32, (LANES, ELEMS), 0) // FIELDS
    ).astype(F32)
    target = lax.dot_general(
        spread_t.astype(BF16),
        code.astype(BF16),
        (((1,), (1,)), ((), ())),
        preferred_element_type=F32,
    )
    target = target.astype(jnp.int32) * FIELDS
    target = target + lax.broadcasted_iota(jnp.int32, (LANES, 6), 0) % FIELDS
    for side in range(6):
        column = target[:, side : side + 1]
        near = (column == lanes).astype(F32).astype(BF16)
        far = (column == lanes + LANES).astype(F32).astype(BF16)
        if side < 2:
            perm_far[side] = far
            perm_near[side] = near
        elif side < 4:
            perm_near[side] = near
        else:
            perm_far[side - 2] = far

    lane_numbers = lax.broadcasted_iota(jnp.int32, (64, LANES), 1).astype(F32).astype(BF16)
    for slot in range(4):
        origin[slot] = dot(lane_numbers, perm_far[slot]).astype(jnp.int32)
        has_origin[slot] = dot(jnp.ones((64, LANES), BF16), perm_far[slot])

    def launch(number, side, trace):
        slot = side if side < 2 else side - 2
        moved = jnp.take_along_axis(
            trace.astype(F32), origin[slot], axis=1, mode="promise_in_bounds"
        )
        send[number, slot] = jnp.where(has_origin[slot] > 0.5, moved, 0.0).astype(BF16)
        copy = pltpu.make_async_remote_copy(
            src_ref=send.at[number, slot],
            dst_ref=recv.at[number, slot ^ 1],
            send_sem=send_sem.at[number, slot],
            recv_sem=recv_sem.at[number, slot ^ 1],
            device_id=partner[side],
            device_id_type=MESH,
        )
        copy.start()
        started.append(copy)
        arrivals[number, side ^ 1] = copy

    def gather_local(traces):
        for side in range(4):
            local_nb[side ^ 1] = dot(traces[side], perm_near[side])

    started, arrivals = [], {}

    def fine_trace(ref, side):
        return face_get(ref, side).astype(BF16)

    traces = [fine_trace(u0, side) for side in range(6)]
    gather_local(traces)

    loads[1].wait()
    loads[3].wait()
    for dim in range(3):
        spread_vel = lax.dot_general(
            vel_v[dim],
            spread.astype(BF16),
            (((0,), (0,)), ((), ())),
            preferred_element_type=F32,
        ).astype(BF16)
        vel_rep[dim * 64 : dim * 64 + 64] = spread_vel.astype(F32)
        speed[dim] = dot(lift_v[...], spread_vel).astype(BF16).astype(F32)
        for end in range(2):
            side = 2 * dim + end
            normal = face_get(speed.at[dim], side)
            lift_coef = STEP * (P7 * (P7 - 1) / 2.0)
            coef[side] = lift_coef * jnp.minimum(normal if end else -normal, 0.0)

    loads[4].wait()
    loads[5].wait()
    pre_row = jnp.zeros((1, LANES), F32)
    stoich_row = jnp.zeros((1, LANES), F32)
    for elem in range(ELEMS):
        pre_row = jnp.where(lane_elem == elem, pre_s[elem], pre_row)
    for field in range(FIELDS):
        stoich_row = jnp.where(lane_field == field, stoich_s[field], stoich_row)

    def source(u):
        rate = (
            pre_row
            * jnp.exp(-ACTIVATION * jnp.exp(-u))
            * pltpu.roll(u, LANES - 1, 1)
            * pltpu.roll(u, LANES - 2, 1)
        )
        high = rate.astype(BF16)
        low = (rate - high.astype(F32)).astype(BF16)
        return stoich_row * dot(jnp.concatenate([high, low], axis=1), rep2)

    loads[8].wait()

    def fine_start(ref, start, out, traces):
        scale = 1.0 if start is None else 0.5
        along_i = []
        for half in range(2):
            parts = []
            for i in range(P7):
                at = pl.ds(i * 64 + half * 32, 32)
                parts.append((speed[0, at, :] * ref[at, :]).astype(BF16))
            along_i.append(dot(fine_v[:256, :], jnp.concatenate(parts, axis=0)))
        for block in range(4):
            at = pl.ds(block * 128, 128)
            u = ref[at, :]
            flux = jnp.concatenate(
                [(speed[1, at, :] * u).astype(BF16), (speed[2, at, :] * u).astype(BF16)], axis=0
            )
            div = dot(fine_v[256:, :], flux) + jnp.concatenate(
                [
                    along_i[half][i * 32 : i * 32 + 32]
                    for i in (2 * block, 2 * block + 1)
                    for half in range(2)
                ],
                axis=0,
            )
            rate = STEP * (source(u) - div)
            out[at, :] = u + rate if start is None else 0.5 * (start[at, :] + u + rate)
        for side in range(6):
            jump = traces[side].astype(F32)
            if side < 4:
                jump = jump - local_nb[side]
            face_add(out, side, scale * (coef[side] * jump))

    def late_term(number, side, scale):
        slot = side if side < 2 else side - 2
        arrivals[number, side].wait_recv()
        return scale * (coef[side] * recv[number, slot].astype(F32))

    def fine_end_z(number, scale, out):
        for side in (4, 5):
            face_add(out, side, -late_term(number, side, scale))

    def fine_end_x(number, scale, out):
        for side in (0, 1):
            face_add(out, side, -late_term(number, side, scale))

    def coarse_start(c, start):
        flux = jnp.concatenate(
            [(vel_rep[dim * 64 : dim * 64 + 64] * c).astype(BF16) for dim in range(3)], axis=0
        )
        rate = STEP * (source(c) - dot(coarse_v[...], flux))
        return c + rate if start is None else 0.5 * (start + c + rate)

    def coarse_local(own, scale, partial):
        jumps = []
        for side in range(6):
            jump = own[side * 64 : side * 64 + 64].astype(F32)
            if side < 4:
                jump = jump - local_nb[side]
            jumps.append(vmin[side * 64 : side * 64 + 64] * jump)
        return partial + scale * dot(lower_v[...], split_rows(jnp.concatenate(jumps, axis=0)))

    def coarse_late(number):
        terms = []
        for slot, side in enumerate((0, 1, 4, 5)):
            terms.append(vmin[side * 64 : side * 64 + 64] * recv[number, slot].astype(F32))
        return jnp.concatenate(terms, axis=0)

    def launch_mixed(number, fine, raised_base, first_row, late, order, after=None):
        late = late.astype(BF16)
        own, traces = [None] * 6, [None] * 6
        for sides in order:
            at = slice(sides[0] * 64, sides[0] * 64 + 128)
            raised = raised_base[at] - dot(
                late_raise_v[pl.ds(first_row + sides[0] * 64, 128), :], late
            )
            for place, side in enumerate(sides):
                own[side] = raised[place * 64 : place * 64 + 64]
                traces[side] = fine_trace(fine, side)
                mixed = jnp.where(is_switched, own[side], traces[side].astype(F32)).astype(BF16)
                if side in (2, 3):
                    mixes[side] = mixed
                else:
                    launch(number, side, mixed)
                    mixes[side] = mixed
            if after is not None:
                after(sides)
        return traces, jnp.concatenate(own, axis=0).astype(BF16)

    mixes = [None] * 6

    fine_start(u0, None, u1, traces)
    for side in (0, 1, 4, 5):
        slot, dim, end = side if side < 2 else side - 2, side // 2, side % 2
        edges = [(end, 0), (end, 1)] if dim == 0 else [(0, end), (1, end)]
        first = face_get(u1, side)
        high = first.astype(BF16)
        packed = [
            traces[side],
            face_get(speed.at[dim], side).astype(BF16),
            jnp.concatenate([speed[2 - dim, edge_slice(*edge), :] for edge in edges], axis=0).astype(BF16),
            high,
            (first - high.astype(F32)).astype(BF16),
        ]
        placed = dot(jnp.concatenate(packed, axis=0), perm_far[slot])
        wide_send[slot] = placed.astype(BF16)
        far_trace[slot] = placed[:64]
    for number, corner in enumerate(corners):
        z_end, x_end = number // 2, number % 2
        corner_send[number] = jnp.concatenate(
            [
                far_trace[x_end, pl.ds(7 * z_end, P7, stride=8), :],
                far_trace[2 + z_end, pl.ds(56 * x_end, P7), :],
            ],
            axis=0,
        ).astype(BF16)
    pl.semaphore_wait(barrier, 8)
    for number, corner in enumerate(corners):
        copy = pltpu.make_async_remote_copy(
            src_ref=corner_send.at[number],
            dst_ref=corner_recv.at[3 - number],
            send_sem=corner_ssem.at[number],
            recv_sem=corner_rsem.at[3 - number],
            device_id=corner,
            device_id_type=MESH,
        )
        copy.start()
        started.append(copy)
        arrivals["corner", 3 - number] = copy
    for part, (start_row, count) in enumerate(((0, 144), (144, 128))):
        for side in (0, 1, 4, 5):
            slot = side if side < 2 else side - 2
            at = pl.ds(start_row, count)
            copy = pltpu.make_async_remote_copy(
                src_ref=wide_send.at[slot, at],
                dst_ref=wide_recv.at[slot ^ 1, at],
                send_sem=wide_ssem.at[part, slot],
                recv_sem=wide_rsem.at[part, slot ^ 1],
                device_id=partner[side],
                device_id_type=MESH,
            )
            copy.start()
            started.append(copy)
            arrivals["wide", part, side ^ 1] = copy

    loads[6].wait()
    loads[7].wait()
    left_count = right_count = home_count = jnp.int32(0)
    left_pick = [jnp.int32(0)] * 2
    right_pick = [jnp.int32(0)] * 2
    home_pick = [jnp.int32(0)] * HOLD7
    switch_row = jnp.zeros((1, LANES), F32)
    for elem in range(ELEMS):
        switched = switch_s[elem]
        owner = owner_s[elem]
        switch_row = jnp.where(lane_elem == elem, switched.astype(F32), switch_row)
        fine_one = switched != 1
        goes_left = fine_one & (owner == left)
        goes_right = fine_one & (owner == right)
        stays = fine_one & jnp.logical_not(owner == left) & jnp.logical_not(owner == right)
        for slot in range(2):
            left_pick[slot] = jnp.where(goes_left & (left_count == slot), elem, left_pick[slot])
            right_pick[slot] = jnp.where(goes_right & (right_count == slot), elem, right_pick[slot])
        for slot in range(min(elem + 1, HOLD7)):
            home_pick[slot] = jnp.where(stays & (home_count == slot), elem, home_pick[slot])
        left_count = left_count + goes_left.astype(jnp.int32)
        right_count = right_count + goes_right.astype(jnp.int32)
        home_count = home_count + stays.astype(jnp.int32)
    for slot in range(HOLD7):
        home_list[slot] = home_pick[slot]
    count_arrivals = []
    count_send[0] = jnp.full((8, LANES), left_count, jnp.int32)
    count_send[1] = jnp.full((8, LANES), right_count, jnp.int32)
    for side in (0, 1):
        copy = pltpu.make_async_remote_copy(
            src_ref=count_send.at[side],
            dst_ref=count_recv.at[side ^ 1],
            send_sem=count_ssem.at[side],
            recv_sem=count_rsem.at[side ^ 1],
            device_id=partner[side],
            device_id_type=MESH,
        )
        copy.start()
        started.append(copy)
        count_arrivals.append(copy)
    is_switched = switch_row > 0.5

    for side, picks, count in ((0, left_pick, left_count), (1, right_pick, right_count)):
        chosen = jnp.zeros((LANES, LANES), F32)
        for slot in range(2):
            place = lanes // FIELDS == 2 * (1 - side) + slot
            source_row = rows - (lanes % FIELDS) == picks[slot] * FIELDS
            chosen = jnp.where(place & source_row & (count > slot), 1.0, chosen)
        chosen = chosen.astype(BF16)
        early_send[side, :LANES] = chosen
        normals = jnp.concatenate(
            [face_get(speed.at[other // 2], other).astype(BF16) for other in (0, 1, 4, 5)], axis=0
        )
        early_send[side, LANES:] = dot(normals, chosen).astype(BF16)
        copy = pltpu.make_async_remote_copy(
            src_ref=early_send.at[side],
            dst_ref=early_recv.at[side ^ 1],
            send_sem=early_ssem.at[side],
            recv_sem=early_rsem.at[side ^ 1],
            device_id=partner[side],
            device_id_type=MESH,
        )
        copy.start()
        started.append(copy)
        count_arrivals.append(copy)

    for load in loads[9:]:
        load.wait()
    for dim in range(3):
        spread_vel = vel_rep[dim * 64 : dim * 64 + 64].astype(BF16)
        mortar = dot(
            raise_v[dim * 128 : dim * 128 + 128, :128],
            jnp.concatenate([spread_vel, spread_vel], axis=0),
        )
        vmin[dim * 128 : dim * 128 + 64] = jnp.minimum(-mortar[:64], 0.0)
        vmin[dim * 128 + 64 : dim * 128 + 128] = jnp.minimum(mortar[64:], 0.0)

    for side in (4, 5, 0, 1):
        slot = side if side < 2 else side - 2
        arrivals["wide", 0, side].wait_recv()
        face_add(u1, side, -(coef[side] * wide_recv[slot, pl.ds(0, 64), :].astype(F32)))
    next_traces = [fine_trace(u1, side) for side in range(6)]
    gather_local(next_traces)
    fine_start(u1, u0, u2, next_traces)
    c0 = dot(project_v[...], split_rows(u2[...]))
    raised = dot(raise_v[...], split_rows(c0))

    lift_coef = STEP * (P7 * (P7 - 1) / 2.0)
    edge_coef = {}
    for side in (0, 1, 4, 5):
        slot, end = side if side < 2 else side - 2, side % 2
        normal = wide_recv[slot, pl.ds(64, 64), :].astype(F32)
        normal = -normal if end else normal
        next_near[slot] = lift_coef * jnp.minimum(normal, 0.0) * traces[side].astype(F32)
        edge = wide_recv[slot, pl.ds(128, 16), :].astype(F32)
        edge_coef[side] = [
            lift_coef * jnp.minimum(-edge[:8], 0.0),
            lift_coef * jnp.minimum(edge[8:], 0.0),
        ]
    for side in (4, 5, 0, 1):
        slot = side if side < 2 else side - 2
        arrivals["wide", 1, side].wait_recv()
        got = wide_recv[slot, pl.ds(144, 128), :].astype(F32)
        next_near[slot] = got[:64] + got[64:] - next_near[slot]
    for number in range(4):
        arrivals["corner", number].wait_recv()
    corner_values = [corner_recv[number].astype(F32) for number in range(4)]
    late = []
    for side in (0, 1, 4, 5):
        slot, dim, end = side if side < 2 else side - 2, side // 2, side % 2
        if dim == 0:
            around = [corner_values[end][8:16], corner_values[2 + end][8:16]]
        else:
            around = [corner_values[2 * end][0:8], corner_values[2 * end + 1][0:8]]
        around = lax.dot_general(
            jnp.concatenate(around, axis=0).astype(BF16),
            perm_far[slot],
            (((1,), (1,)), ((), ())),
            preferred_element_type=F32,
        )
        for which in range(2):
            term = edge_coef[side][which] * around[8 * which : 8 * which + 8]
            at = pl.ds(7 * which, P7, stride=8) if dim == 0 else pl.ds(56 * which, P7)
            next_near[slot, at, :] -= term
        late.append(0.5 * (coef[side] * next_near[slot].astype(BF16).astype(F32)))
    for place, side in enumerate((0, 1, 4, 5)):
        face_add(u2, side, -late[place])
    late = jnp.concatenate(late, axis=0)

    traces, own = launch_mixed(
        2, u2, raised, 0, late, ((0, 1), (4, 5), (2, 3))
    )
    gather_local(mixes)
    c0 = c0 - dot(late_nodes_v[:64, :], split_rows(late))
    fine_start(u2, None, u3, traces)
    partial = coarse_start(c0, None)
    for copy in count_arrivals:
        copy.wait_recv()
    for place, side in enumerate((0, 1, 4, 5)):
        at = pl.ds(LANES + 64 * place, 64)
        normal = early_recv[0, at, :].astype(F32) + early_recv[1, at, :].astype(F32)
        lift_coef = 0.5 * STEP * (P7 * (P7 - 1) / 2.0)
        move_coef[place] = lift_coef * jnp.minimum(normal if side % 2 else -normal, 0.0)
    c1 = coarse_local(own, 1.0, partial)
    raised = dot(raise_v[...], split_rows(c1))
    fine_end_z(2, 1.0, u3)
    fine_end_x(2, 1.0, u3)
    late = coarse_late(2)

    left2, right2 = lax.rem(pos + pieces - 2, pieces), lax.rem(pos + 2, pieces)
    extras = {
        (1, 1): (2, (below, right)),
        (1, 2): (3, (above, right)),
        (0, 1): (2, (below, left)),
        (0, 2): (3, (above, left)),
        (0, 0): (0, (slab, left2)),
        (1, 0): (1, (slab, right2)),
    }
    extra_copies = []

    def launch_extras(sides):
        for (toward, kind), (slot, device) in extras.items():
            if (kind == 0) != (0 in sides) or 2 in sides:
                continue
            place = 3 - kind if kind else 0
            copy = pltpu.make_async_remote_copy(
                src_ref=send.at[3, slot],
                dst_ref=extra_recv.at[1 - toward, place],
                send_sem=extra_ssem.at[toward, kind],
                recv_sem=extra_rsem.at[1 - toward, place],
                device_id=device,
                device_id_type=MESH,
            )
            copy.start()
            started.append(copy)
            extra_copies.append(copy)

    earlier = list(started)
    started.clear()
    traces, own = launch_mixed(
        3, u3, raised, 384, late, ((4, 5), (0, 1), (2, 3)), launch_extras
    )
    gather_local(mixes)
    fine_start(u3, u2, u1, traces)

    def turn_home():
        for number in range(4):
            home[:, :, number * 128 : number * 128 + 128] = jnp.transpose(
                u1[number * 128 : number * 128 + 128, :]
            ).reshape(ELEMS, FIELDS, 128)

    turn_home()
    for side in range(2):
        for slot in range(2):
            pick = (left_pick, right_pick)[side][slot]
            move_send[side, slot] = home[pick]
        copy = pltpu.make_async_remote_copy(
            src_ref=move_send.at[side],
            dst_ref=move_recv.at[side ^ 1],
            send_sem=move_ssem.at[side],
            recv_sem=move_rsem.at[side ^ 1],
            device_id=partner[side],
            device_id_type=MESH,
        )
        copy.start()
        started.append(copy)
        extra_copies.append(copy)
    c1 = c1 - dot(late_nodes_v[64:, :], split_rows(late))
    partial = coarse_start(c1, c0)
    u3[...] = jnp.zeros_like(u3)
    for copy in earlier:
        copy.wait_send()
    c2 = coarse_local(own, 0.5, partial)
    fine_end_z(3, 0.5, u1)
    fine_end_x(3, 0.5, u1)
    c2 = c2 - 0.5 * dot(late_nodes_v[64:, :], split_rows(coarse_late(3)))

    c2 = jnp.where(is_switched, c2, 0.0)
    turned[...] = jnp.transpose(jnp.concatenate([c2, pltpu.roll(c2, LANES - 1, 1)], axis=0))
    for pair in range(4):
        out3_v[:, pair * 128 : pair * 128 + 128] = turned[pl.ds(2 * pair, ELEMS, stride=FIELDS), :]
    turn_home()

    from_left = jnp.minimum(count_recv[0][0, 0], 2)
    from_right = jnp.minimum(count_recv[1][0, 0], 2)
    is_first, is_last = pos == 0, pos == pieces - 1
    at_left = jnp.where(is_first, home_count + from_right, jnp.where(is_last, from_right, 0))
    at_home = jnp.where(is_first, 0, jnp.where(is_last, from_right + from_left, from_left))
    at_right = jnp.where(is_first, home_count, jnp.where(is_last, 0, from_left + home_count))
    picks = []
    for slot in range(HOLD7):
        rank = slot - at_home
        stay = (rank >= 0) & (rank < home_count)
        value = home[home_list[jnp.clip(rank, 0, HOLD7 - 1)]]
        out7_v[slot] = jnp.where(stay, value, 0.0)
        rank_left, rank_right = slot - at_left, slot - at_right
        is_left = (rank_left >= 0) & (rank_left < from_left)
        is_right = (rank_right >= 0) & (rank_right < from_right)
        pick = jnp.where(is_left, rank_left, jnp.where(is_right, 2 + rank_right, 0))
        picks.append((is_left | is_right, pick))
    for copy in extra_copies:
        copy.wait_recv()
    chosen = jnp.concatenate([early_recv[0, :LANES, :], early_recv[1, :LANES, :]], axis=0)
    nears = {
        0: (extra_recv[0, 0], send[3, 1]),
        1: (send[3, 0], extra_recv[1, 0]),
        4: (extra_recv[0, 1], extra_recv[1, 1]),
        5: (extra_recv[0, 2], extra_recv[1, 2]),
    }
    for place, side in enumerate((0, 1, 4, 5)):
        near = dot(jnp.concatenate(nears[side], axis=1), chosen)
        face_add(u3, side, -(move_coef[place] * near))
    for number in range(4):
        moved = jnp.transpose(u3[number * 128 : number * 128 + 128, :])
        at = pl.ds(number * 128, 128)
        for pick in range(4):
            move_recv[pick // 2, pick % 2, :, at] += moved[pick * FIELDS : pick * FIELDS + FIELDS]
    for slot in range(HOLD7):
        arrived, pick = picks[slot]
        value = move_recv[pick // 2, pick % 2]
        out7_v[slot] = jnp.where(arrived, value, out7_v[slot])
    for copy in started:
        copy.wait_send()


def store_kernel(held7, held3, out7, out3, sem):
    copies = [
        pltpu.make_async_copy(held7, out7, sem.at[0]),
        pltpu.make_async_copy(held3, out3, sem.at[1]),
    ]
    for copy in copies:
        copy.start()
    for copy in copies:
        copy.wait()


def solution(mesh):
    slabs, pieces = mesh.shape["slab"], mesh.shape["curve"]
    tables = make_tables()

    def per_device(state, velocity, pre_exp, stoich, neighbours, switch, new_owner):
        velocity = jnp.transpose(velocity, (0, 2, 1))
        neighbours = jnp.transpose(neighbours)
        operands = (state, velocity, neighbours, pre_exp, stoich, switch, new_owner) + tuple(
            jnp.asarray(table) for table in tables
        )
        vm, sm, dma = pltpu.VMEM, pltpu.SMEM, pltpu.SemaphoreType.DMA
        nodes = (512, LANES)
        held = pl.pallas_call(
            functools.partial(kernel, slabs, pieces),
            out_shape=(
                pltpu.VMEM((HOLD7, FIELDS, 512), F32),
                pltpu.VMEM((ELEMS, 512), F32),
            ),
            in_specs=[pl.BlockSpec(memory_space=pltpu.HBM)] * len(operands),
            out_specs=[pl.BlockSpec(memory_space=pltpu.VMEM)] * 2,
            scratch_shapes=[
                vm((ELEMS, FIELDS, 512), F32),
                vm((3, ELEMS, 64), BF16),
                vm((6, ELEMS), jnp.int32),
                sm((ELEMS,), F32),
                sm((FIELDS,), F32),
                sm((ELEMS,), jnp.int32),
                sm((ELEMS,), jnp.int32),
            ]
            + [vm(table.shape, BF16) for table in tables]
            + [
                vm(nodes, F32),
                vm(nodes, F32),
                vm(nodes, F32),
                vm(nodes, F32),
                vm((3, 512, LANES), F32),
                vm((6, 64, LANES), F32),
                vm((192, LANES), F32),
                vm((384, LANES), F32),
                vm((4, LANES, LANES), BF16),
                vm((4, LANES, LANES), BF16),
                vm((4, 64, LANES), jnp.int32),
                vm((4, 64, LANES), F32),
                vm((4, 64, LANES), F32),
                vm((4, 4, 64, LANES), BF16),
                vm((4, 4, 64, LANES), BF16),
                vm((2, 8, LANES), jnp.int32),
                vm((2, 8, LANES), jnp.int32),
                vm((ELEMS, FIELDS, 512), F32),
                vm((2, 2, FIELDS, 512), F32),
                vm((2, 2, FIELDS, 512), F32),
                vm((2, 3 * LANES, LANES), BF16),
                vm((2, 3 * LANES, LANES), BF16),
                vm((4, 272, LANES), BF16),
                vm((4, 272, LANES), BF16),
                vm((4, 64, LANES), F32),
                vm((4, 64, LANES), F32),
                vm((4, 16, LANES), BF16),
                vm((4, 16, LANES), BF16),
                vm((2, 3, 64, LANES), BF16),
                vm((4, 64, LANES), F32),
                vm((LANES, LANES), F32),
                sm((HOLD7,), jnp.int32),
                dma((15,)),
                dma((4, 4)),
                dma((4, 4)),
                dma((2,)),
                dma((2,)),
                dma((2,)),
                dma((2,)),
                dma((2,)),
                dma((2,)),
                dma((2, 3)),
                dma((2, 3)),
                dma((2, 4)),
                dma((2, 4)),
                dma((4,)),
                dma((4,)),
            ],
            compiler_params=pltpu.CompilerParams(
                collective_id=0, has_side_effects=True, vmem_limit_bytes=62 * 2**20
            ),
        )(*operands)
        return pl.pallas_call(
            store_kernel,
            out_shape=(
                jax.ShapeDtypeStruct((HOLD7, FIELDS, 512), F32),
                jax.ShapeDtypeStruct((ELEMS, 512), F32),
            ),
            in_specs=[pl.BlockSpec(memory_space=pl.ANY)] * 2,
            out_specs=[pl.BlockSpec(memory_space=pltpu.HBM)] * 2,
            scratch_shapes=[dma((2,))],
            compiler_params=pltpu.CompilerParams(vmem_limit_bytes=2**20),
        )(*held)

    return jax.shard_map(
        per_device,
        mesh=mesh,
        in_specs=(
            P(("slab", "curve"), None, None),
            P(None, None, ("slab", "curve")),
            P(("slab", "curve")),
            P(),
            P(("slab", "curve"), None),
            P(("slab", "curve")),
            P(("slab", "curve")),
        ),
        out_specs=(P(("slab", "curve"), None, None), P(("slab", "curve"), None)),
        check_vma=False,
    )
```
